32 devices in a mesh: groups: 2 (over y), lon: 4 (over z), lat: 2 (over x), dp: 2 (over core).
Axes of the slice: x: 2, y: 2, z: 4, core: 2. Of those that a mesh axis runs over, the one named last changes fastest.
Arguments:
- fine_field: bfloat16 [8, 128, 128, 128], P(('groups', 'dp'), 'lat', 'lon'), parts along dimension 0, may hold values from -6 to 6
- grad_out: bfloat16 [8, 64, 64, 256], P(('groups', 'dp'), 'lat', 'lon'), parts along dimension 0, may hold values from -6 to 6
- conv_kernel: float32 [49, 256], replicated, may hold values from -0.875 to 0.875
- norm_gain: float32 [256], replicated, may hold values from 0.1 to 1.9
- w_expand: bfloat16 [256, 1024], replicated, may hold values from -0.375 to 0.375
- w_contract: bfloat16 [1024, 256], replicated, may hold values from -0.1875 to 0.1875
- w_merge: bfloat16 [512, 256], replicated, may hold values from -0.25 to 0.25
Outputs:
- section_out: bfloat16 [8, 64, 64, 256], P(('groups', 'dp'), 'lat', 'lon'), parts along dimension 0
- grad_fine: bfloat16 [8, 128, 128, 128], P(('groups', 'dp'), 'lat', 'lon'), parts along dimension 0
- grad_kernel: float32 [98, 256], P('groups', 'dp'), parts along dimension 0
- grad_gain: float32 [512], P(('groups', 'dp')), parts along dimension 0
- grad_expand: float32 [512, 1024], P(('groups', 'dp')), parts along dimension 0
- grad_contract: float32 [2048, 256], P(('groups', 'dp')), parts along dimension 0
- grad_merge: float32 [1024, 256], P(('groups', 'dp')), parts along dimension 0
The draws below stay inside these ranges and needn't reach their ends.
There are 2 independent parts, one for each index of `groups`. The reference program is written for one: setup_inputs(seed, part) draws one part's arguments, and reference() takes and returns one part's arrays. A program takes and returns all parts, laid end to end along the dimension named above; an argument that names none is the same for every part. Nothing has to cross between parts.
All inputs are finite; a program needn't handle non-finite values.
Results may differ from the reference program's by a relative error of at most 0.012.
Values may be sent and summed in bfloat16 or wider, within the bound.
No kernel may reach another device: no remote copies, remote signals or barrier semaphores. Data moves between devices by JAX's collectives and lax.ppermute only.
A program may use at most 64 MiB of HBM per device.

```python
import math
import jax
import jax.numpy as jnp
from jax import lax

CI = 128
C = 256
FF = 1024
KS = 7
B = 4
H = 64
W = 64
CELLS = 16384


def levels(own_key, shape, cuts, smallest, high):
    factor_of = 1.0
    for position, parts in cuts:
        heights = jax.random.uniform(jax.random.fold_in(jax.random.fold_in(own_key, 6), position), (parts,), jnp.float32, smallest / len(cuts), high / len(cuts))
        factor_of = factor_of * jnp.repeat(jnp.exp(heights), shape[position] // parts).reshape((-1,) + (1,) * (len(shape) - 1 - position))
    return factor_of


def normal_values(key, shape, width, bound, shards=(), kind=jnp.bfloat16):
    drawn = jax.random.normal(key, shape, jnp.float32) * width
    if len(shards) > 0:
        drawn = levels(key, shape, shards, -0.22, 0.18) * drawn
    return jnp.clip(drawn, min=-bound, max=bound).astype(kind)


def setup_inputs(seed: int = 0, part: int = 0) -> dict:
    key_list = jax.random.split(jax.random.key(seed), 8)
    own_keys = jax.random.split(jax.random.fold_in(key_list[7], part), 8)
    fine_field = normal_values(own_keys[0], (B, 2 * H, 2 * W, CI), 1.0, 6.0, ((0, 2), (1, 2), (2, 4)))
    grad_out = normal_values(own_keys[1], (B, H, W, C), 1.0, 6.0, ((0, 2), (1, 2), (2, 4)))
    conv_kernel = normal_values(key_list[2], (KS * KS, C), (KS * KS) ** -0.5, 0.875, (), jnp.float32)
    norm_gain = jnp.clip(1.0 + 0.18 * jax.random.normal(key_list[3], (C,), jnp.float32), 0.1, 1.9)
    w_expand = normal_values(key_list[4], (C, FF), C ** -0.5, 0.375)
    w_contract = normal_values(key_list[5], (FF, C), FF ** -0.5, 0.1875)
    w_merge = normal_values(key_list[6], (4 * CI, C), (4 * CI) ** -0.5, 0.25)
    return dict(fine_field=fine_field, grad_out=grad_out, conv_kernel=conv_kernel, norm_gain=norm_gain, w_expand=w_expand, w_contract=w_contract, w_merge=w_merge)


def normalize(values):
    centered = values - lax.optimization_barrier(jnp.mean(values, axis=-1, keepdims=True))
    inverse = lax.rsqrt(lax.optimization_barrier(jnp.mean(centered * centered, axis=-1, keepdims=True)) + 1e-06)
    return (centered * inverse, inverse)

def norm_back(upstream, normed, inverse):
    return inverse * (upstream - lax.optimization_barrier(jnp.mean(upstream, axis=-1, keepdims=True)) - normed * lax.optimization_barrier(jnp.mean(upstream * normed, axis=-1, keepdims=True)))

def gelu_slope(pre_act):
    return 0.5 * (1.0 + lax.erf(pre_act * 0.7071067811865476)) + pre_act * jnp.exp(-0.5 * pre_act * pre_act) * 0.3989422804014327

def pad_grid(field):
    margin = KS // 2
    looped = jnp.concatenate([field[:, :, -margin:], field, field[:, :, :margin]], axis=2)
    return jnp.pad(looped, ((0, 0), (margin, margin), (0, 0), (0, 0)))

def depthwise(padded, kernel, lat_rows, lon_cols, flipped):
    total = jnp.zeros(padded.shape[:1] + (lat_rows, lon_cols, padded.shape[3]), jnp.float32)
    for kernel_row in range(KS):
        for kernel_col in range(KS):
            start_row = KS - 1 - kernel_row if flipped else kernel_row
            start_col = KS - 1 - kernel_col if flipped else kernel_col
            window = padded[:, start_row:start_row + lat_rows, start_col:start_col + lon_cols, :].astype(jnp.float32)
            total = total + window * kernel[kernel_row * KS + kernel_col]
    return total

def kernel_terms(padded, upstream, lat_rows, lon_cols):
    terms = []
    for kernel_row in range(KS):
        for kernel_col in range(KS):
            window = padded[:, kernel_row:kernel_row + lat_rows, kernel_col:kernel_col + lon_cols, :].astype(jnp.float32)
            terms.append(lax.optimization_barrier(jnp.sum(window * upstream, axis=(0, 1, 2))))
    return jnp.stack(terms)

def reference(fine_field, grad_out, conv_kernel, norm_gain, w_expand, w_contract, w_merge):
    samples, fine_rows, fine_cols, narrow = fine_field.shape
    lat_rows = fine_rows // 2
    lon_cols = fine_cols // 2
    channels = w_merge.shape[1]
    fine_unit, fine_inv = normalize(fine_field.astype(jnp.float32))
    fine_normed = fine_unit.astype(jnp.bfloat16)
    patches = fine_normed.reshape(samples, lat_rows, 2, lon_cols, 2, narrow).transpose(0, 1, 3, 2, 4, 5).reshape(-1, 4 * narrow)
    coarse = jnp.dot(patches, w_merge, preferred_element_type=jnp.float32).astype(jnp.bfloat16).reshape(samples, lat_rows, lon_cols, channels)
    padded = pad_grid(coarse)
    mixed = depthwise(padded, conv_kernel, lat_rows, lon_cols, False)
    unit, inverse = normalize(mixed)
    normed = (unit * norm_gain).astype(jnp.bfloat16).reshape(-1, channels)
    pre_act = jnp.dot(normed, w_expand, preferred_element_type=jnp.float32)
    hidden = jax.nn.gelu(pre_act, approximate=False).astype(jnp.bfloat16)
    branch = jnp.dot(hidden, w_contract, preferred_element_type=jnp.float32)
    section_out = (coarse.reshape(-1, channels).astype(jnp.float32) + branch).astype(jnp.bfloat16).reshape(samples, lat_rows, lon_cols, channels)
    latitude = math.pi * ((jnp.arange(lat_rows, dtype=jnp.float32) + 0.5) / lat_rows - 0.5)
    weighted = (grad_out.astype(jnp.float32) * jnp.cos(latitude)[None, :, None, None]).astype(jnp.bfloat16).reshape(-1, channels)
    term_contract = jnp.dot(hidden.T, weighted, preferred_element_type=jnp.float32)
    back_hidden = jnp.dot(weighted, w_contract.T, preferred_element_type=jnp.float32)
    slope = (back_hidden * gelu_slope(pre_act)).astype(jnp.bfloat16)
    term_expand = jnp.dot(normed.T, slope, preferred_element_type=jnp.float32)
    back_normed = jnp.dot(slope, w_expand.T, preferred_element_type=jnp.float32).reshape(samples, lat_rows, lon_cols, channels)
    term_gain = lax.optimization_barrier(jnp.sum(back_normed * unit, axis=(0, 1, 2)))
    back_mixed = norm_back(back_normed * norm_gain, unit, inverse)
    term_kernel = kernel_terms(padded, back_mixed, lat_rows, lon_cols)
    back_low = back_mixed.astype(jnp.bfloat16)
    spread_back = depthwise(pad_grid(back_low), conv_kernel, lat_rows, lon_cols, True)
    back_coarse = (weighted.astype(jnp.float32).reshape(samples, lat_rows, lon_cols, channels) + spread_back).astype(jnp.bfloat16).reshape(-1, channels)
    term_merge = jnp.dot(patches.T, back_coarse, preferred_element_type=jnp.float32)
    back_patch = jnp.dot(back_coarse, w_merge.T, preferred_element_type=jnp.float32)
    back_fine = back_patch.reshape(samples, lat_rows, lon_cols, 2, 2, narrow).transpose(0, 1, 3, 2, 4, 5).reshape(samples, fine_rows, fine_cols, narrow)
    grad_fine = norm_back(back_fine, fine_unit, fine_inv).astype(jnp.bfloat16)
    factor = 1.0 / math.sqrt(CELLS)
    return (section_out, grad_fine, term_kernel * factor, term_gain * factor, term_expand * factor, term_contract * factor, term_merge * factor)
```

```python
import functools
import math

import jax
import jax.numpy as jnp
from jax import lax
from jax.experimental import pallas as pl
from jax.experimental.pallas import tpu as pltpu
from jax.sharding import PartitionSpec as P

KS = 7
M = KS // 2
SUB = 8
LANE = 128
F32 = jnp.float32
BF16 = jnp.bfloat16


def kernel_call(fn, outs, args, scratch=(), flops=0):
    whole = pl.BlockSpec(memory_space=pltpu.VMEM)
    return pl.pallas_call(
        fn,
        out_shape=[jax.ShapeDtypeStruct(s, d) for s, d in outs],
        in_specs=[whole] * len(args),
        out_specs=[whole] * len(outs),
        scratch_shapes=[pltpu.VMEM(s, d) for s, d in scratch],
        compiler_params=pltpu.CompilerParams(vmem_limit_bytes=40 * 2**20),
        cost_estimate=pl.CostEstimate(
            flops=flops, bytes_accessed=sum(a.size * a.dtype.itemsize for a in args), transcendentals=0
        ),
    )(*args)


def rows(start, size):
    return pl.ds(start if isinstance(start, int) else pl.multiple_of(start, size & -size), size)


def dot(a, b):
    return jnp.dot(a, b, preferred_element_type=F32)


def dot_nt(a, b):
    return lax.dot_general(a, b, (((1,), (1,)), ((), ())), preferred_element_type=F32)


def dot_tn(a, b):
    return lax.dot_general(a, b, (((0,), (0,)), ((), ())), preferred_element_type=F32)


class Sizes:
    def __init__(self, fine_field, w_merge, w_expand):
        self.samples, fine_rows, fine_cols, self.narrow = fine_field.shape
        self.lat_rows, self.cols = fine_rows // 2, fine_cols // 2
        self.channels, self.wide = w_merge.shape[1], w_expand.shape[1]
        self.blocks = SUB // self.samples
        self.block_rows = self.lat_rows // self.blocks
        self.col = self.block_rows * SUB
        self.pad_rows = self.block_rows + 2 * M
        self.pad_col = self.pad_rows * SUB
        self.cells = self.cols * self.col
        self.fine = 4 * self.cells
        self.fine_stride = 2 * self.block_rows * fine_cols
        self.fine_cols = fine_cols
        self.halves = self.channels // LANE


def fine_stats(z, x):
    ones = jnp.full((z.narrow, z.narrow), 1.0 / z.narrow, BF16)
    centered = x.astype(F32) - dot(x, ones)
    inverse = lax.rsqrt(dot((centered * centered).astype(BF16), ones) + 1e-06)
    return centered * inverse, inverse


def fine_rows_of(z, j, i, p, q):
    return pl.ds((2 * i + p) * z.fine_cols + 2 * j + q, SUB, stride=z.fine_stride)


def edge_rows(z, scratch, before_ref, after_ref):
    for ref, first_row, block in ((after_ref, 0, 0), (before_ref, z.block_rows - M, z.blocks - 1)):
        parts = []
        for r in range(M):
            for s in range(z.samples):
                start = (first_row + r) * SUB + s * z.blocks + block
                parts.append(
                    jnp.concatenate(
                        [scratch[h, pl.ds(start, z.cols, stride=z.col), :] for h in range(z.halves)], axis=1
                    )
                )
        ref[...] = jnp.concatenate(parts, axis=0).astype(BF16)


def merge_kernel(z, fine_ref, w_ref, patches_ref, coarse_ref, last_ref, first_ref, unit_s, split_s):
    def norm_step(t, _):
        at = rows(t * 512, 512)
        unit_s[at, :] = fine_stats(z, fine_ref[at, :])[0]
        return 0

    lax.fori_loop(0, z.fine // 512, norm_step, 0)
    group = 4

    def step(g, _):
        for jj in range(group):
            j = g * group + jj
            quarters = []
            for p in range(2):
                for q in range(2):
                    quarters.append(
                        jnp.concatenate(
                            [unit_s[fine_rows_of(z, j, i, p, q), :] for i in range(z.block_rows)], axis=0
                        ).astype(BF16)
                    )
            patches_ref[rows(j * z.col, z.col), :] = jnp.concatenate(quarters, axis=1)
        at = rows(g * group * z.col, group * z.col)
        low = dot(patches_ref[at, :], w_ref[...]).astype(BF16)
        coarse_ref[at, :] = low
        for h in range(z.halves):
            split_s[h, at, :] = low[:, h * LANE : (h + 1) * LANE].astype(F32)
        return 0

    lax.fori_loop(0, z.cols // group, step, 0)
    edge_rows(z, split_s, last_ref, first_ref)


def weighted_kernel(z, grad_ref, cos_ref, out_ref, split_s):
    for h in range(z.halves):
        split_s[h, :, :] = grad_ref[:, h * LANE : (h + 1) * LANE].astype(F32)

    def step(j, _):
        for h in range(z.halves):
            col = jnp.concatenate(
                [
                    split_s[h, pl.ds(i * z.cols + j, SUB, stride=z.block_rows * z.cols), :]
                    for i in range(z.block_rows)
                ],
                axis=0,
            )
            out_ref[rows(j * z.col, z.col), h * LANE : (h + 1) * LANE] = (col * cos_ref[...]).astype(BF16)
        return 0

    lax.fori_loop(0, z.cols, step, 0)


def pad_kernel(z, lats, own_ref, before_ref, after_ref, pad_ref, left_ref, right_ref, halo_s):
    lat = lax.axis_index("lat")
    near = z.samples * M * z.cols
    halo_s[0:near, :] = jnp.where(lat > 0, before_ref[...].astype(F32), 0.0)
    halo_s[near : 2 * near, :] = jnp.where(lat < lats - 1, after_ref[...].astype(F32), 0.0)
    place = lax.broadcasted_iota(jnp.int32, (SUB, z.channels), 0)

    def halo(base, r, j, block, inner):
        for s in range(z.samples):
            line = halo_s[pl.ds(base + (r * z.samples + s) * z.cols + j, 1), :]
            inner = jnp.where(place == s * z.blocks + block, line, inner)
        return inner

    def step(j, _):
        own = own_ref[rows(j * z.col, z.col), :].astype(F32)
        pad_ref[rows(j * z.pad_col + M * SUB, SUB * z.block_rows), :] = own
        for r in range(M):
            i = z.block_rows - M + r
            up = pltpu.roll(own[i * SUB : (i + 1) * SUB], 1, 0)
            down = pltpu.roll(own[r * SUB : (r + 1) * SUB], SUB - 1, 0)
            pad_ref[rows(j * z.pad_col + r * SUB, SUB), :] = halo(0, r, j, 0, up)
            pad_ref[rows(j * z.pad_col + (M + z.block_rows + r) * SUB, SUB), :] = halo(
                near, r, j, z.blocks - 1, down
            )
        return 0

    lax.fori_loop(0, z.cols, step, 0)
    edge = M * z.pad_col
    left_ref[...] = pad_ref[0:edge, :].astype(BF16)
    right_ref[...] = pad_ref[z.cols * z.pad_col - edge :, :].astype(BF16)


def taps(z, pad, taps_s, start, h, flipped):
    lanes = slice(h * LANE, (h + 1) * LANE)
    total = jnp.zeros((z.block_rows, SUB, LANE), F32)
    for e in range(KS):
        column = pad[rows((start + e) * z.pad_col, z.pad_col), lanes].reshape(z.pad_rows, SUB, LANE)
        for a in range(KS):
            t = a * KS + e
            t = KS * KS - 1 - t if flipped else t
            total = total + column[a : a + z.block_rows] * taps_s[t * SUB : (t + 1) * SUB, lanes]
    return total.reshape(z.col, LANE)


def spread_taps(z, kern_ref, taps_s):
    for t in range(KS * KS):
        taps_s[t * SUB : (t + 1) * SUB, :] = jnp.broadcast_to(kern_ref[t : t + 1, :], (SUB, z.channels))


def gelu_parts(x):
    t = 1.0 / (1.0 + jnp.abs(x) * (0.3275911 * 0.7071067811865476))
    bell = jnp.exp(-0.5 * x * x)
    poly = 0.5 * 1.061405429
    for c in (-1.453152027, 1.421413741, -0.284496736, 0.254829592):
        poly = poly * t + 0.5 * c
    tail = poly * t * bell
    return jnp.where(x >= 0, 1.0 - tail, tail), x * bell * 0.3989422804014327


def row_mean(z, x):
    return jnp.sum(x, axis=-1, keepdims=True) * (1.0 / z.channels)


def section(z, pad, sources, groups, refs, scratch, chunk, section_ref, mixed_ref, taps_s):
    gain_ref, we_ref, wc_ref, coarse_ref, weighted_ref = refs
    unit_s, inv_s, normed_s, hidden_s, slope_s, weighted_s = scratch
    count = sum(g[2] for g in groups)

    def step(j, _):
        parts = [taps(z, pad, taps_s, sources(j), h, False) for h in range(z.halves)]
        at = rows(j * z.col, z.col)
        mean = sum(jnp.sum(p, axis=-1, keepdims=True) for p in parts) * (1.0 / z.channels)
        parts = [p - mean for p in parts]
        var = sum(jnp.sum(p * p, axis=-1, keepdims=True) for p in parts) * (1.0 / z.channels)
        inverse = lax.rsqrt(var + 1e-06)
        inv_s[at, :] = jnp.broadcast_to(inverse, (z.col, LANE))
        for h, p in enumerate(parts):
            lanes = slice(h * LANE, (h + 1) * LANE)
            unit = p * inverse
            unit_s[at, lanes] = unit
            normed_s[at, lanes] = (unit * gain_ref[:, lanes]).astype(BF16)
        return 0

    lax.fori_loop(0, count // z.col, step, 0)
    for low, full, size in groups:
        weighted_s[low : low + size, :] = weighted_ref[full : full + size, :]
    gain_sum = jnp.zeros((SUB, z.channels), F32)
    for low, full, size in groups:
        for c in range(size // chunk):
            at = slice(low + c * chunk, low + (c + 1) * chunk)
            place = slice(full + c * chunk, full + (c + 1) * chunk)
            part = 256
            for f in range(z.wide // part):
                cut = slice(f * part, (f + 1) * part)
                pre = dot(normed_s[at, :], we_ref[:, cut])
                back = dot_nt(weighted_s[at, :], wc_ref[cut, :])
                phi, density = gelu_parts(pre)
                hidden_s[at, cut] = (pre * phi).astype(BF16)
                slope_s[at, cut] = (back * (phi + density)).astype(BF16)
            branch = dot(hidden_s[at, :], wc_ref[...])
            section_ref[at, :] = (coarse_ref[place, :].astype(F32) + branch).astype(BF16)
            back = dot_nt(slope_s[at, :], we_ref[...])
            unit = unit_s[at, :]
            gain_sum = gain_sum + jnp.sum((back * unit).reshape(-1, SUB, z.channels), axis=0)
            back = back * gain_ref[...]
            inverse = jnp.concatenate([inv_s[at, :]] * z.halves, axis=1)
            mixed_ref[at, :] = inverse * (back - row_mean(z, back) - unit * row_mean(z, back * unit))
    return gain_sum


def inner_kernel(
    z, pad_ref, kern_ref, gain_ref, we_ref, wc_ref, coarse_ref, weighted_ref,
    section_ref, mixed_ref, expand_ref, contract_ref, gain_sum_ref, taps_s, *scratch,
):
    spread_taps(z, kern_ref, taps_s)
    size = (z.cols - 2 * M) * z.col
    refs = (gain_ref, we_ref, wc_ref, coarse_ref, weighted_ref)
    gain_sum_ref[...] = section(
        z, pad_ref, lambda j: j, [(0, M * z.col, size)], refs, scratch, size // 2, section_ref, mixed_ref, taps_s
    )
    unit_s, inv_s, normed_s, hidden_s, slope_s, weighted_s = scratch
    expand_ref[...] = dot_tn(normed_s[...], slope_s[...])
    contract_ref[...] = dot_tn(weighted_s[...], hidden_s[...])


def outer_kernel(
    z, pad_ref, left_ref, right_ref, kern_ref, gain_ref, we_ref, wc_ref, coarse_ref, weighted_ref,
    expand_ref, contract_ref, gain_sum_ref, inner_mixed_ref,
    section_ref, mixed_ref, mine_ref, other_ref, low_ref, last_ref, first_ref, gain_out_ref,
    taps_s, edge_s, sum_s, split_s, *scratch,
):
    spread_taps(z, kern_ref, taps_s)
    edge, near = M * z.pad_col, 2 * M * z.pad_col
    edge_s[0:edge, :] = left_ref[...].astype(F32)
    edge_s[edge : edge + near, :] = pad_ref[0:near, :]
    edge_s[edge + near : edge + 2 * near, :] = pad_ref[z.cols * z.pad_col - near :, :]
    edge_s[edge + 2 * near :, :] = right_ref[...].astype(F32)
    size = M * z.col
    refs = (gain_ref, we_ref, wc_ref, coarse_ref, weighted_ref)
    groups = [(0, 0, size), (size, z.cells - size, size)]
    gain_sum = section(
        z, edge_s, lambda j: jnp.where(j < M, j, j + 2 * M), groups, refs, scratch, size, section_ref, mixed_ref, taps_s
    )
    unit_s, inv_s, normed_s, hidden_s, slope_s, weighted_s = scratch
    gain_out_ref[...] = gain_sum + gain_sum_ref[...]
    sum_s[0, :, :] = expand_ref[...] + dot_tn(normed_s[...], slope_s[...])
    sum_s[1, :, :] = contract_ref[...] + dot_tn(weighted_s[...], hidden_s[...])
    own = lax.axis_index("dp")
    half, cut = z.channels // 2, z.wide // 2
    for ref, owner in ((mine_ref, own), (other_ref, 1 - own)):
        ref[0:half, :] = sum_s[0, rows(owner * half, half), :].astype(BF16)
        for t in range(2):
            ref[half:, t * cut : (t + 1) * cut] = sum_s[1, t * half : (t + 1) * half, rows(owner * cut, cut)].astype(
                BF16
            )
    low_ref[0:size, :] = mixed_ref[0:size, :].astype(BF16)
    low_ref[size : z.cells - size, :] = inner_mixed_ref[...].astype(BF16)
    low_ref[z.cells - size :, :] = mixed_ref[size:, :].astype(BF16)
    for h in range(z.halves):
        split_s[h, :, :] = low_ref[:, h * LANE : (h + 1) * LANE].astype(F32)
    edge_rows(z, split_s, last_ref, first_ref)


def terms_kernel(z, pad_ref, left_ref, right_ref, inner_ref, outer_ref, gain_ref, out_ref, full_s, mixed_s):
    edge = M * z.pad_col
    full_s[0:edge, :] = left_ref[...].astype(F32)
    full_s[edge : edge + z.cols * z.pad_col, :] = pad_ref[...]
    full_s[edge + z.cols * z.pad_col :, :] = right_ref[...].astype(F32)
    size = M * z.col
    mixed_s[0:size, :] = outer_ref[0:size, :]
    mixed_s[size : z.cells - size, :] = inner_ref[...]
    mixed_s[z.cells - size :, :] = outer_ref[size:, :]
    out_ref[...] = jnp.zeros_like(out_ref)
    for h in range(z.halves):
        lanes = slice(h * LANE, (h + 1) * LANE)
        for e in range(KS):

            def step(j, sums):
                column = full_s[rows((j + e) * z.pad_col, z.pad_col), lanes].reshape(z.pad_rows, SUB, LANE)
                back = mixed_s[rows(j * z.col, z.col), lanes].reshape(z.block_rows, SUB, LANE)
                return tuple(
                    sums[a] + jnp.sum(column[a : a + z.block_rows] * back, axis=0) for a in range(KS)
                )

            sums = lax.fori_loop(0, z.cols, step, tuple(jnp.zeros((SUB, LANE), F32) for _ in range(KS)))
            for a in range(KS):
                t = a * KS + e
                out_ref[t : t + 1, lanes] = jnp.sum(sums[a], axis=0, keepdims=True)
    out_ref[KS * KS : KS * KS + 1, :] = jnp.sum(gain_ref[...], axis=0, keepdims=True)


def back_kernel(
    z, pad_ref, left_ref, right_ref, kern_ref, weighted_ref, patches_ref, aux_ref,
    coarse_ref, mine_ref, other_ref, taps_s, full_s, sum_s,
):
    spread_taps(z, kern_ref, taps_s)
    edge = M * z.pad_col
    full_s[0:edge, :] = left_ref[...].astype(F32)
    full_s[edge : edge + z.cols * z.pad_col, :] = pad_ref[...]
    full_s[edge + z.cols * z.pad_col :, :] = right_ref[...].astype(F32)

    def step(j, _):
        at = rows(j * z.col, z.col)
        for h in range(z.halves):
            lanes = slice(h * LANE, (h + 1) * LANE)
            spread = taps(z, full_s, taps_s, j, h, True)
            coarse_ref[at, lanes] = (weighted_ref[at, lanes].astype(F32) + spread).astype(BF16)
        return 0

    lax.fori_loop(0, z.cols, step, 0)
    sum_s[...] = dot_tn(coarse_ref[...], patches_ref[...])
    own = lax.axis_index("dp")
    cut, depth = 2 * z.narrow, aux_ref.shape[0] // 2
    half = z.channels // 2
    for ref, owner in ((mine_ref, own), (other_ref, 1 - own)):
        ref[0 : z.channels, :] = sum_s[:, rows(owner * cut, cut)].astype(BF16)
        for t in range(2):
            ref[z.channels :, t * half : (t + 1) * half] = aux_ref[
                t * depth : (t + 1) * depth, rows(owner * half, half)
            ].astype(BF16)


def fine_kernel(z, coarse_ref, w_ref, fine_ref, out_ref, back_s):
    group = 4

    def step(g, _):
        back = dot_nt(coarse_ref[rows(g * group * z.col, group * z.col), :], w_ref[...])
        for jj in range(group):
            j = g * group + jj
            for p in range(2):
                for q in range(2):
                    lanes = slice((p * 2 + q) * z.narrow, (p * 2 + q + 1) * z.narrow)
                    for i in range(z.block_rows):
                        first = jj * z.col + i * SUB
                        back_s[fine_rows_of(z, j, i, p, q), :] = back[first : first + SUB, lanes]
        return 0

    lax.fori_loop(0, z.cols // group, step, 0)
    ones = jnp.full((z.narrow, z.narrow), 1.0 / z.narrow, BF16)

    def mean(x):
        high = x.astype(BF16)
        return dot(high, ones) + dot((x - high.astype(F32)).astype(BF16), ones)

    def norm_step(t, _):
        at = rows(t * 512, 512)
        unit, inverse = fine_stats(z, fine_ref[at, :])
        back = back_s[at, :]
        out_ref[at, :] = (inverse * (back - mean(back) - unit * mean(back * unit))).astype(BF16)
        return 0

    lax.fori_loop(0, z.fine // 512, norm_step, 0)


def section_kernel(z, inner_ref, outer_ref, out_ref, all_s, split_s):
    size = M * z.col
    all_s[0:size, :] = outer_ref[0:size, :].astype(F32)
    all_s[size : z.cells - size, :] = inner_ref[...].astype(F32)
    all_s[z.cells - size :, :] = outer_ref[size:, :].astype(F32)

    def step(j, _):
        for h in range(z.halves):
            for i in range(z.block_rows):
                split_s[h, pl.ds(i * z.cols + j, SUB, stride=z.block_rows * z.cols), :] = all_s[
                    rows(j * z.col + i * SUB, SUB), h * LANE : (h + 1) * LANE
                ]
        return 0

    lax.fori_loop(0, z.cols, step, 0)
    for h in range(z.halves):
        out_ref[:, h * LANE : (h + 1) * LANE] = split_s[h, :, :].astype(BF16)


def final_wide_kernel(z, factor, sum_ref, expand_ref, contract_ref):
    half, cut = z.channels // 2, z.wide // 2
    expand_ref[...] = sum_ref[0:half, :].astype(F32) * factor
    for t in range(2):
        part = sum_ref[half:, t * cut : (t + 1) * cut].astype(F32) * factor
        contract_ref[:, t * half : (t + 1) * half] = part.T


def final_small_kernel(z, factor, sum_ref, merge_ref, kernel_ref, gain_ref):
    merge_ref[...] = (sum_ref[0 : z.channels, :].astype(F32) * factor).T
    half = z.channels // 2
    tail = sum_ref[z.channels :, :].astype(F32) * factor
    depth = tail.shape[0]
    kernel_ref[0:depth, :] = tail[:, :half]
    kernel_ref[depth:, :] = tail[: KS * KS - depth, half:]
    gain_ref[...] = tail[KS * KS - depth : KS * KS - depth + 1, half:]


def swap(x, axis, distance):
    size = lax.axis_size(axis)
    return lax.ppermute(x, axis, [(i, i ^ distance) for i in range(size)])


def reduce_rows(x, halving):
    steps = []
    for axis in ("lat", "lon"):
        distance = 1
        while distance < lax.axis_size(axis):
            steps.append((axis, distance))
            distance *= 2
    done = []
    for n, (axis, distance) in enumerate(steps):
        if halving and n < len(steps) - 1:
            low = ((lax.axis_index(axis) // distance) % 2) == 0
            half = x.shape[0] // 2
            mine = jnp.where(low, x[:half], x[half:])
            send = jnp.where(low, x[half:], x[:half])
            got = swap(send, axis, distance)
            done.append((axis, distance, low))
        else:
            mine, got = x, swap(x, axis, distance)
        x = (mine.astype(F32) + got.astype(F32)).astype(BF16)
    for axis, distance, low in reversed(done):
        got = swap(x, axis, distance)
        x = jnp.concatenate([jnp.where(low, x, got), jnp.where(low, got, x)], axis=0)
    return x


def lat_margins(last, first):
    lats = lax.axis_size("lat")
    if lats == 2:
        got = swap(jnp.where(lax.axis_index("lat") == 0, last, first), "lat", 1)
        return got, got
    up = [(i, i + 1) for i in range(lats - 1)]
    return lax.ppermute(last, "lat", up), lax.ppermute(first, "lat", [(j, i) for i, j in up])


def lon_margins(left, right):
    size = lax.axis_size("lon")
    up = [(i, (i + 1) % size) for i in range(size)]
    return lax.ppermute(right, "lon", up), lax.ppermute(left, "lon", [(j, i) for i, j in up])


def body(fine_field, grad_out, conv_kernel, norm_gain, w_expand, w_contract, w_merge):
    z = Sizes(fine_field, w_merge, w_expand)
    ch, wide, lats = z.channels, z.wide, lax.axis_size("lat")
    fine = fine_field.reshape(z.fine, z.narrow)
    gain = norm_gain.reshape(1, ch)
    total_rows = z.lat_rows * lats
    place = jnp.arange(z.col, dtype=jnp.int32)
    row = lax.axis_index("lat") * z.lat_rows + (place % SUB) % z.blocks * z.block_rows + place // SUB
    latitude = math.pi * ((row.astype(F32) + 0.5) / total_rows - 0.5)
    cosine = jnp.broadcast_to(jnp.cos(latitude)[:, None], (z.col, LANE))

    part = functools.partial
    split = ((z.halves, z.cells, LANE), F32)
    edge = ((z.samples * M * z.cols, ch), BF16)
    patches, coarse, last, first = kernel_call(
        part(merge_kernel, z),
        [((z.cells, 4 * z.narrow), BF16), ((z.cells, ch), BF16), edge, edge],
        (fine, w_merge),
        [((z.fine, z.narrow), F32), split],
    )
    before, after = lat_margins(last, first)
    (weighted,) = kernel_call(
        part(weighted_kernel, z),
        [((z.cells, ch), BF16)],
        (grad_out.reshape(z.cells, ch), cosine),
        [split],
        flops=2_000_000_000,
    )
    slab = ((M * z.pad_col, ch), BF16)
    padded = ((z.cols * z.pad_col, ch), F32)
    pad_scratch = [((2 * z.samples * M * z.cols, ch), F32)]
    pad, left, right = kernel_call(part(pad_kernel, z, lats), [padded, slab, slab], (coarse, before, after), pad_scratch)
    left, right = lon_margins(left, right)

    taps_s = ((KS * KS * SUB, ch), F32)

    def section_scratch(count):
        return [
            ((count, ch), F32),
            ((count, LANE), F32),
            ((count, ch), BF16),
            ((count, wide), BF16),
            ((count, wide), BF16),
            ((count, ch), BF16),
        ]

    outer = 2 * M * z.col
    inner = z.cells - outer
    section_in, mixed_in, expand, contract, gain_sum = kernel_call(
        part(inner_kernel, z),
        [((inner, ch), BF16), ((inner, ch), F32), ((ch, wide), F32), ((ch, wide), F32), ((SUB, ch), F32)],
        (pad, conv_kernel, gain, w_expand, w_contract, coarse, weighted),
        [taps_s] + section_scratch(inner),
        flops=8_000_000_000,
    )
    section_out, mixed_out, mine, other, low, last, first, gain_sum = kernel_call(
        part(outer_kernel, z),
        [
            ((outer, ch), BF16),
            ((outer, ch), F32),
            ((ch, wide), BF16),
            ((ch, wide), BF16),
            ((z.cells, ch), BF16),
            edge,
            edge,
            ((SUB, ch), F32),
        ],
        (pad, left, right, conv_kernel, gain, w_expand, w_contract, coarse, weighted)
        + (expand, contract, gain_sum, mixed_in),
        [taps_s, ((6 * M * z.pad_col, ch), F32), ((2, ch, wide), F32), split] + section_scratch(outer),
        flops=8_000_000_000,
    )
    before, after = lat_margins(last, first)
    got = swap(other, "dp", 1)
    (section_all,) = kernel_call(
        part(section_kernel, z),
        [((z.cells, ch), BF16)],
        (section_in, section_out),
        [((z.cells, ch), F32), split],
        flops=2_000_000_000,
    )
    pad_low, left_low, right_low = kernel_call(
        part(pad_kernel, z, lats), [padded, slab, slab], (low, before, after), pad_scratch
    )
    left_low, right_low = lon_margins(left_low, right_low)
    full = (((z.cols + 2 * M) * z.pad_col, ch), F32)
    (aux,) = kernel_call(
        part(terms_kernel, z),
        [((64, ch), F32)],
        (pad, left, right, mixed_in, mixed_out, gain_sum),
        [full, ((z.cells, ch), F32)],
        flops=5_000_000_000,
    )
    wide_sum = reduce_rows((mine.astype(F32) + got.astype(F32)).astype(BF16), True)
    small = ((ch + 32, ch), BF16)
    back_coarse, mine, other = kernel_call(
        part(back_kernel, z),
        [((z.cells, ch), BF16), small, small],
        (pad_low, left_low, right_low, conv_kernel, weighted, patches, aux),
        [taps_s, full, ((ch, 4 * z.narrow), F32)],
        flops=5_000_000_000,
    )
    got = swap(other, "dp", 1)
    (grad_fine,) = kernel_call(
        part(fine_kernel, z),
        [((z.fine, z.narrow), BF16)],
        (back_coarse, w_merge, fine),
        [((z.fine, z.narrow), F32)],
        flops=5_000_000_000,
    )
    small_sum = reduce_rows((mine.astype(F32) + got.astype(F32)).astype(BF16), False)
    all_cells = z.samples * lax.axis_size("dp") * total_rows * z.cols * lax.axis_size("lon")
    factor = 1.0 / math.sqrt(all_cells)
    grad_expand, grad_contract = kernel_call(
        part(final_wide_kernel, z, factor), [((ch // 2, wide), F32), ((wide // 2, ch), F32)], (wide_sum,)
    )
    grad_merge, grad_kernel, grad_gain = kernel_call(
        part(final_small_kernel, z, factor),
        [((2 * z.narrow, ch), F32), ((KS * KS, ch // 2), F32), ((1, ch // 2), F32)],
        (small_sum,),
    )
    return (
        section_all.reshape(z.samples, z.lat_rows, z.cols, ch),
        grad_fine.reshape(fine_field.shape),
        grad_kernel,
        grad_gain.reshape(ch // 2),
        grad_expand,
        grad_contract,
        grad_merge,
    )


def solution(mesh):
    field = P(("groups", "dp"), "lat", "lon", None)
    owned = P(("groups", "dp"), None)
    return jax.shard_map(
        body,
        mesh=mesh,
        in_specs=(field, field, P(), P(), P(), P(), P()),
        out_specs=(field, field, P("groups", "dp"), P(("groups", "dp")), owned, owned, owned),
        check_vma=False,
    )
```

```python
import functools
import math

import jax
import jax.numpy as jnp
from jax import lax
from jax.experimental import pallas as pl
from jax.experimental.pallas import tpu as pltpu
from jax.sharding import PartitionSpec as P

KS = 7
M = KS // 2
SUB = 8
LANE = 128
F32 = jnp.float32
BF16 = jnp.bfloat16


def kernel_call(fn, outs, args, scratch=(), flops=0, after=()):
    outs = [*outs, ((SUB, LANE), F32)]
    whole = pl.BlockSpec(memory_space=pltpu.VMEM)
    count = len(args)
    held = sum(math.prod(s) * jnp.dtype(d).itemsize for s, d in scratch)

    def run(*refs):
        last = count + len(after) + len(outs) - 1
        refs[last][...] = jnp.zeros((SUB, LANE), F32)
        fn(*refs[:count], *refs[count + len(after) : last], *refs[last + 1 :])

    return pl.pallas_call(
        run,
        out_shape=[jax.ShapeDtypeStruct(s, d) for s, d in outs],
        in_specs=[whole] * count + [whole] * len(after),
        out_specs=[whole] * len(outs),
        scratch_shapes=[pltpu.VMEM(s, d) for s, d in scratch],
        compiler_params=pltpu.CompilerParams(vmem_limit_bytes=held + 8 * 2**20),
        cost_estimate=pl.CostEstimate(
            flops=flops, bytes_accessed=sum(a.size * a.dtype.itemsize for a in args), transcendentals=0
        ),
    )(*args, *after)


def rows(start, size):
    return pl.ds(start if isinstance(start, int) else pl.multiple_of(start, SUB), size)


def lanes_at(start, size):
    return pl.ds(pl.multiple_of(start, LANE), size)


def rows16(start, size):
    return pl.ds(start if isinstance(start, int) else pl.multiple_of(start, 2 * SUB), size)


def dot(a, b):
    return jnp.dot(a, b, preferred_element_type=F32)


def dot_nt(a, b):
    return lax.dot_general(a, b, (((1,), (1,)), ((), ())), preferred_element_type=F32)


def dot_tn(a, b):
    return lax.dot_general(a, b, (((0,), (0,)), ((), ())), preferred_element_type=F32)


class Sizes:
    def __init__(self, fine_field, w_merge, w_expand):
        self.samples, fine_rows, fine_cols, self.narrow = fine_field.shape
        self.lat_rows, self.cols = fine_rows // 2, fine_cols // 2
        self.channels, self.wide = w_merge.shape[1], w_expand.shape[1]
        self.blocks = SUB // self.samples
        self.block_rows = self.lat_rows // self.blocks
        self.col = self.block_rows * SUB
        self.pad_rows = self.block_rows + 2 * M
        self.pad_col = self.pad_rows * SUB
        self.cells = self.cols * self.col
        self.fine = 4 * self.cells
        self.fine_block = 2 * self.block_rows * fine_cols
        self.fine_stride = self.fine_block + SUB
        self.fine_cols = fine_cols
        self.halves = self.channels // LANE


def fine_stats(z, x):
    ones = jnp.full((z.narrow, z.narrow), 1.0 / z.narrow, BF16)
    centered = x.astype(F32) - dot(x, ones)
    inverse = lax.rsqrt(dot((centered * centered).astype(BF16), ones) + 1e-06)
    return centered * inverse, inverse


def fine_rows_of(z, j, i, p, q):
    return pl.ds((2 * i + p) * z.fine_cols + 2 * j + q, SUB, stride=z.fine_stride)


def edge_rows(z, scratch, edge_refs):
    sides = []
    for first_row, block in ((z.block_rows - M, z.blocks - 1), (0, 0)):
        parts = []
        for r in range(M):
            for s in range(z.samples):
                start = (first_row + r) * SUB + s * z.blocks + block
                parts.append(
                    jnp.concatenate(
                        [scratch[h, pl.ds(start, z.cols, stride=z.col), :] for h in range(z.halves)], axis=1
                    )
                )
        sides.append(jnp.concatenate(parts, axis=0))
    if len(edge_refs) == 1:
        edge_refs[0][...] = jnp.where(lax.axis_index("lat") == 0, sides[0], sides[1]).astype(BF16)
    else:
        for ref, side in zip(edge_refs, sides):
            ref[...] = side.astype(BF16)


def merge_kernel(z, fine_ref, w_ref, patches_ref, coarse_ref, inv_ref, *rest):
    *edge_refs, unit_s, split_s = rest
    def norm_step(t, _):
        at = rows16(t * z.fine_block, z.fine_block)
        unit, inverse = fine_stats(z, fine_ref[at, :])
        unit_s[rows(t * z.fine_stride, z.fine_block), :] = unit
        inv_ref[at, :] = inverse
        return 0

    lax.fori_loop(0, SUB, norm_step, 0)
    group = 4

    def step(g, _):
        for jj in range(group):
            j = g * group + jj
            quarters = []
            for p in range(2):
                for q in range(2):
                    quarters.append(
                        jnp.concatenate(
                            [unit_s[fine_rows_of(z, j, i, p, q), :] for i in range(z.block_rows)], axis=0
                        ).astype(BF16)
                    )
            patches_ref[rows16(j * z.col, z.col), :] = jnp.concatenate(quarters, axis=1)
        at = rows16(g * group * z.col, group * z.col)
        low = dot(patches_ref[at, :], w_ref[...]).astype(BF16)
        coarse_ref[at, :] = low
        for h in range(z.halves):
            split_s[h, at, :] = low[:, h * LANE : (h + 1) * LANE].astype(F32)
        return 0

    lax.fori_loop(0, z.cols // group, step, 0)
    edge_rows(z, split_s, edge_refs)


def weighted_kernel(z, lats, grad_ref, w_ref, out_ref, centered_ref, split_s):
    for t in range(4):
        at = slice(t * z.narrow, (t + 1) * z.narrow)
        w = w_ref[at, :].astype(F32)
        w = w - jnp.sum(w, axis=0, keepdims=True) * (1.0 / z.narrow)
        high = w.astype(BF16)
        centered_ref[at, 0 : z.channels] = high
        centered_ref[at, z.channels :] = (w - high.astype(F32)).astype(BF16)
    place = lax.broadcasted_iota(jnp.int32, (z.col, LANE), 0)
    row = lax.axis_index("lat") * z.lat_rows + (place % SUB) % z.blocks * z.block_rows + place // SUB
    cosine = jnp.cos(math.pi * ((row.astype(F32) + 0.5) / (z.lat_rows * lats) - 0.5))
    for h in range(z.halves):
        split_s[h, :, :] = grad_ref[:, h * LANE : (h + 1) * LANE].astype(F32)

    def step(j, _):
        for h in range(z.halves):
            col = jnp.concatenate(
                [
                    split_s[h, pl.ds(i * z.cols + j, SUB, stride=z.block_rows * z.cols), :]
                    for i in range(z.block_rows)
                ],
                axis=0,
            )
            out_ref[rows16(j * z.col, z.col), h * LANE : (h + 1) * LANE] = (col * cosine).astype(BF16)
        return 0

    lax.fori_loop(0, z.cols, step, 0)


def pad_kernel(z, lats, own_ref, before_ref, after_ref, pad_ref, left_ref, right_ref, halo_s):
    lat = lax.axis_index("lat")
    near = z.samples * M * z.cols
    halo_s[0:near, :] = jnp.where(lat > 0, before_ref[...].astype(F32), 0.0)
    halo_s[near : 2 * near, :] = jnp.where(lat < lats - 1, after_ref[...].astype(F32), 0.0)
    place = lax.broadcasted_iota(jnp.int32, (SUB, z.channels), 0)

    def halo(base, r, j, block, inner):
        for s in range(z.samples):
            line = halo_s[pl.ds(base + (r * z.samples + s) * z.cols + j, 1), :]
            inner = jnp.where(place == s * z.blocks + block, line, inner)
        return inner

    def step(j, _):
        own = own_ref[rows16(j * z.col, z.col), :].astype(F32)
        pad_ref[rows(j * z.pad_col + M * SUB, SUB * z.block_rows), :] = own
        for r in range(M):
            i = z.block_rows - M + r
            up = pltpu.roll(own[i * SUB : (i + 1) * SUB], 1, 0)
            down = pltpu.roll(own[r * SUB : (r + 1) * SUB], SUB - 1, 0)
            pad_ref[rows(j * z.pad_col + r * SUB, SUB), :] = halo(0, r, j, 0, up)
            pad_ref[rows(j * z.pad_col + (M + z.block_rows + r) * SUB, SUB), :] = halo(
                near, r, j, z.blocks - 1, down
            )
        return 0

    lax.fori_loop(0, z.cols, step, 0)
    edge = M * z.pad_col
    left_ref[...] = pad_ref[0:edge, :].astype(BF16)
    right_ref[...] = pad_ref[z.cols * z.pad_col - edge :, :].astype(BF16)


def taps(z, pad, taps_s, start, h, flipped):
    lanes = slice(h * LANE, (h + 1) * LANE)
    total = jnp.zeros((z.block_rows, SUB, LANE), F32)
    for e in range(KS):
        column = pad[rows((start + e) * z.pad_col, z.pad_col), lanes].reshape(z.pad_rows, SUB, LANE)
        for a in range(KS):
            t = a * KS + e
            t = KS * KS - 1 - t if flipped else t
            total = total + column[a : a + z.block_rows] * taps_s[t * SUB : (t + 1) * SUB, lanes]
    return total.reshape(z.col, LANE)


def spread_taps(z, kern_ref, taps_s):
    for t in range(KS * KS):
        taps_s[t * SUB : (t + 1) * SUB, :] = jnp.broadcast_to(kern_ref[t : t + 1, :], (SUB, z.channels))


def gelu_parts(x):
    t = 1.0 / (1.0 + jnp.abs(x) * (0.3275911 * 0.7071067811865476))
    bell = jnp.exp(-0.5 * x * x)
    poly = 0.5 * 1.061405429
    for c in (-1.453152027, 1.421413741, -0.284496736, 0.254829592):
        poly = poly * t + 0.5 * c
    tail = poly * t * bell
    return jnp.where(x >= 0, 1.0 - tail, tail), x * bell * 0.3989422804014327


def row_mean(z, x):
    return jnp.sum(x, axis=-1, keepdims=True) * (1.0 / z.channels)


def section(z, pad, sources, groups, refs, scratch, chunk, section_ref, mixed_ref, taps_s):
    gain_ref, we_ref, wc_ref, coarse_ref, weighted_ref = refs
    unit_s, inv_s, normed_s, hidden_s, slope_s, weighted_s = scratch
    count = sum(g[2] for g in groups)

    def step(j, _):
        parts = [taps(z, pad, taps_s, sources(j), h, False) for h in range(z.halves)]
        at = rows16(j * z.col, z.col)
        mean = sum(jnp.sum(p, axis=-1, keepdims=True) for p in parts) * (1.0 / z.channels)
        parts = [p - mean for p in parts]
        var = sum(jnp.sum(p * p, axis=-1, keepdims=True) for p in parts) * (1.0 / z.channels)
        inverse = lax.rsqrt(var + 1e-06)
        inv_s[at, :] = jnp.broadcast_to(inverse, (z.col, LANE))
        for h, p in enumerate(parts):
            lanes = slice(h * LANE, (h + 1) * LANE)
            unit = p * inverse
            unit_s[at, lanes] = unit
            normed_s[at, lanes] = (unit * gain_ref[:, lanes]).astype(BF16)
        return 0

    lax.fori_loop(0, count // z.col, step, 0)
    for low, full, size in groups:
        weighted_s[low : low + size, :] = weighted_ref[full : full + size, :]
    gain_sum = jnp.zeros((SUB, z.channels), F32)
    for low, full, size in groups:
        for c in range(size // chunk):
            at = slice(low + c * chunk, low + (c + 1) * chunk)
            place = slice(full + c * chunk, full + (c + 1) * chunk)
            part = 256
            for f in range(z.wide // part):
                cut = slice(f * part, (f + 1) * part)
                pre = dot(normed_s[at, :], we_ref[:, cut])
                back = dot_nt(weighted_s[at, :], wc_ref[cut, :])
                phi, density = gelu_parts(pre)
                hidden_s[at, cut] = (pre * phi).astype(BF16)
                slope_s[at, cut] = (back * (phi + density)).astype(BF16)
            branch = dot(hidden_s[at, :], wc_ref[...])
            section_ref[at, :] = (coarse_ref[place, :].astype(F32) + branch).astype(BF16)
            back = dot_nt(slope_s[at, :], we_ref[...])
            unit = unit_s[at, :]
            gain_sum = gain_sum + jnp.sum((back * unit).reshape(-1, SUB, z.channels), axis=0)
            back = back * gain_ref[...]
            inverse = jnp.concatenate([inv_s[at, :]] * z.halves, axis=1)
            mixed_ref[at, :] = inverse * (back - row_mean(z, back) - unit * row_mean(z, back * unit))
    return gain_sum


def inner_kernel(
    z, pad_ref, kern_ref, gain_ref, we_ref, wc_ref, coarse_ref, weighted_ref,
    section_ref, mixed_ref, expand_ref, contract_ref, gain_sum_ref, taps_s, *scratch,
):
    spread_taps(z, kern_ref, taps_s)
    size = (z.cols - 2 * M) * z.col
    refs = (gain_ref, we_ref, wc_ref, coarse_ref, weighted_ref)
    gain_sum_ref[...] = section(
        z, pad_ref, lambda j: j, [(0, M * z.col, size)], refs, scratch, size // 2, section_ref, mixed_ref, taps_s
    )
    unit_s, inv_s, normed_s, hidden_s, slope_s, weighted_s = scratch
    expand_ref[...] = dot_tn(normed_s[...], slope_s[...])
    contract_ref[...] = dot_tn(weighted_s[...], hidden_s[...])


def outer_kernel(
    z, pad_ref, left_ref, right_ref, kern_ref, gain_ref, we_ref, wc_ref, coarse_ref, weighted_ref,
    expand_ref, contract_ref, gain_sum_ref, inner_mixed_ref,
    section_ref, mixed_ref, mine_ref, other_ref, low_ref, gain_out_ref, *rest,
):
    *edge_refs, taps_s, edge_s, sum_s, split_s = rest[:-6]
    scratch = rest[-6:]
    spread_taps(z, kern_ref, taps_s)
    edge, near = M * z.pad_col, 2 * M * z.pad_col
    edge_s[0:edge, :] = left_ref[...].astype(F32)
    edge_s[edge : edge + near, :] = pad_ref[0:near, :]
    edge_s[edge + near : edge + 2 * near, :] = pad_ref[z.cols * z.pad_col - near :, :]
    edge_s[edge + 2 * near :, :] = right_ref[...].astype(F32)
    size = M * z.col
    refs = (gain_ref, we_ref, wc_ref, coarse_ref, weighted_ref)
    groups = [(0, 0, size), (size, z.cells - size, size)]
    gain_sum = section(
        z, edge_s, lambda j: jnp.where(j < M, j, j + 2 * M), groups, refs, scratch, size, section_ref, mixed_ref, taps_s
    )
    unit_s, inv_s, normed_s, hidden_s, slope_s, weighted_s = scratch
    gain_out_ref[...] = gain_sum + gain_sum_ref[...]
    sum_s[0, :, :] = expand_ref[...] + dot_tn(normed_s[...], slope_s[...])
    sum_s[1, :, :] = contract_ref[...] + dot_tn(weighted_s[...], hidden_s[...])
    own = lax.axis_index("dp")
    half, cut = z.channels // 2, z.wide // 2
    for ref, owner in ((mine_ref, own), (other_ref, 1 - own)):
        ref[0:half, :] = sum_s[0, rows16(owner * half, half), :].astype(BF16)
        for t in range(2):
            ref[half:, t * cut : (t + 1) * cut] = sum_s[1, t * half : (t + 1) * half, lanes_at(owner * cut, cut)].astype(
                BF16
            )
    low_ref[0:size, :] = mixed_ref[0:size, :].astype(BF16)
    low_ref[size : z.cells - size, :] = inner_mixed_ref[...].astype(BF16)
    low_ref[z.cells - size :, :] = mixed_ref[size:, :].astype(BF16)
    for h in range(z.halves):
        split_s[h, :, :] = low_ref[:, h * LANE : (h + 1) * LANE].astype(F32)
    edge_rows(z, split_s, edge_refs)


def terms_kernel(z, pad_ref, left_ref, right_ref, inner_ref, outer_ref, gain_ref, out_ref, full_s, mixed_s):
    edge = M * z.pad_col
    full_s[0:edge, :] = left_ref[...].astype(F32)
    full_s[edge : edge + z.cols * z.pad_col, :] = pad_ref[...]
    full_s[edge + z.cols * z.pad_col :, :] = right_ref[...].astype(F32)
    size = M * z.col
    mixed_s[0:size, :] = outer_ref[0:size, :]
    mixed_s[size : z.cells - size, :] = inner_ref[...]
    mixed_s[z.cells - size :, :] = outer_ref[size:, :]
    out_ref[...] = jnp.zeros_like(out_ref)
    for h in range(z.halves):
        lanes = slice(h * LANE, (h + 1) * LANE)
        for e in range(KS):

            def step(j, sums):
                column = full_s[rows((j + e) * z.pad_col, z.pad_col), lanes].reshape(z.pad_rows, SUB, LANE)
                back = mixed_s[rows(j * z.col, z.col), lanes].reshape(z.block_rows, SUB, LANE)
                return tuple(
                    sums[a] + jnp.sum(column[a : a + z.block_rows] * back, axis=0) for a in range(KS)
                )

            sums = lax.fori_loop(0, z.cols, step, tuple(jnp.zeros((SUB, LANE), F32) for _ in range(KS)))
            for a in range(KS):
                t = a * KS + e
                out_ref[t : t + 1, lanes] = jnp.sum(sums[a], axis=0, keepdims=True)
    out_ref[KS * KS : KS * KS + 1, :] = jnp.sum(gain_ref[...], axis=0, keepdims=True)


def back_kernel(
    z, pad_ref, left_ref, right_ref, kern_ref, weighted_ref, patches_ref, aux_ref,
    coarse_ref, mine_ref, other_ref, taps_s, full_s, sum_s,
):
    spread_taps(z, kern_ref, taps_s)
    edge = M * z.pad_col
    full_s[0:edge, :] = left_ref[...].astype(F32)
    full_s[edge : edge + z.cols * z.pad_col, :] = pad_ref[...]
    full_s[edge + z.cols * z.pad_col :, :] = right_ref[...].astype(F32)

    def step(j, _):
        at = rows16(j * z.col, z.col)
        for h in range(z.halves):
            lanes = slice(h * LANE, (h + 1) * LANE)
            spread = taps(z, full_s, taps_s, j, h, True)
            coarse_ref[at, lanes] = (weighted_ref[at, lanes].astype(F32) + spread).astype(BF16)
        return 0

    lax.fori_loop(0, z.cols, step, 0)
    sum_s[...] = dot_tn(coarse_ref[...], patches_ref[...])
    own = lax.axis_index("dp")
    cut, depth = 2 * z.narrow, aux_ref.shape[0] // 2
    half = z.channels // 2
    for ref, owner in ((mine_ref, own), (other_ref, 1 - own)):
        ref[0 : z.channels, :] = sum_s[:, lanes_at(owner * cut, cut)].astype(BF16)
        for t in range(2):
            ref[z.channels :, t * half : (t + 1) * half] = aux_ref[
                t * depth : (t + 1) * depth, lanes_at(owner * half, half)
            ].astype(BF16)


def unfold_kernel(z, coarse_ref, centered_ref, patches_ref, back_ref):
    group = 4
    ones = jnp.full((z.narrow, z.narrow), 1.0 / z.narrow, BF16)

    def step(g, _):
        at = rows16(g * group * z.col, group * z.col)
        low = coarse_ref[at, :]
        back = dot_nt(jnp.concatenate([low, low], axis=1), centered_ref[...])
        for p in range(2):
            for q in range(2):
                lanes = slice((p * 2 + q) * z.narrow, (p * 2 + q + 1) * z.narrow)
                unit = patches_ref[at, lanes].astype(F32)
                up = back[:, lanes]
                up = up - unit * dot((up * unit).astype(BF16), ones)
                for jj in range(group):
                    for i in range(z.block_rows):
                        first = jj * z.col + i * SUB
                        back_ref[fine_rows_of(z, g * group + jj, i, p, q), :] = up[first : first + SUB]
        return 0

    lax.fori_loop(0, z.cols // group, step, 0)


def fine_kernel(z, back_ref, inv_ref, out_ref):
    def step(t, _):
        at = rows16(t * z.fine_block, z.fine_block)
        out_ref[at, :] = (inv_ref[at, :] * back_ref[rows(t * z.fine_stride, z.fine_block), :]).astype(BF16)
        return 0

    lax.fori_loop(0, SUB, step, 0)


def second(axis, distance):
    return lax.axis_index(axis) // distance % 2


def add_kernel(step, mine_ref, got_ref, *out_refs):
    if step is None:
        out_refs[0][...] = (mine_ref[...].astype(F32) + got_ref[...].astype(F32)).astype(BF16)
        return
    half, side = mine_ref.shape[0] // 2, second(*step)
    for ref, which in zip(out_refs, (side, 1 - side)):
        at = rows16(which * half, half)
        ref[...] = (mine_ref[at, :].astype(F32) + got_ref[at, :].astype(F32)).astype(BF16)


def join_kernel(step, mine_ref, got_ref, out_ref):
    half, side = mine_ref.shape[0], second(*step)
    out_ref[rows16(side * half, half), :] = mine_ref[...]
    out_ref[rows16((1 - side) * half, half), :] = got_ref[...]


def section_kernel(z, inner_ref, outer_ref, out_ref, all_s, split_s):
    size = M * z.col
    all_s[0:size, :] = outer_ref[0:size, :].astype(F32)
    all_s[size : z.cells - size, :] = inner_ref[...].astype(F32)
    all_s[z.cells - size :, :] = outer_ref[size:, :].astype(F32)

    def step(j, _):
        for h in range(z.halves):
            for i in range(z.block_rows):
                split_s[h, pl.ds(i * z.cols + j, SUB, stride=z.block_rows * z.cols), :] = all_s[
                    rows(j * z.col + i * SUB, SUB), h * LANE : (h + 1) * LANE
                ]
        return 0

    lax.fori_loop(0, z.cols, step, 0)
    for h in range(z.halves):
        out_ref[:, h * LANE : (h + 1) * LANE] = split_s[h, :, :].astype(BF16)


def final_wide_kernel(z, factor, step, mine_ref, got_ref, expand_ref, contract_ref, sum_ref):
    join_kernel(step, mine_ref, got_ref, sum_ref)
    half, cut = z.channels // 2, z.wide // 2
    expand_ref[...] = sum_ref[0:half, :].astype(F32) * factor
    for t in range(2):
        part = sum_ref[half:, t * cut : (t + 1) * cut].astype(F32) * factor
        contract_ref[:, t * half : (t + 1) * half] = part.T


def final_small_kernel(z, factor, sum_ref, merge_ref, kernel_ref, gain_ref):
    merge_ref[...] = (sum_ref[0 : z.channels, :].astype(F32) * factor).T
    half = z.channels // 2
    tail = sum_ref[z.channels :, :].astype(F32) * factor
    depth = tail.shape[0]
    kernel_ref[0:depth, :] = tail[:, :half]
    kernel_ref[depth:, :] = tail[: KS * KS - depth, half:]
    gain_ref[...] = tail[KS * KS - depth : KS * KS - depth + 1, half:]


def swap(x, axis, distance):
    size = lax.axis_size(axis)
    return lax.ppermute(x, axis, [(i, i ^ distance) for i in range(size)])


def add(mine, got, after=(), halve=None):
    count, width = mine.shape
    outs = [((count, width), BF16)] if halve is None else [((count // 2, width), BF16)] * 2
    return kernel_call(functools.partial(add_kernel, halve), outs, (mine, got), after=after)


def join(x, step):
    got = swap(x, *step)
    return kernel_call(functools.partial(join_kernel, step), [((2 * x.shape[0], x.shape[1]), BF16)], (x, got))[0]


def sum_steps(count):
    steps = []
    for axis in ("lat", "lon"):
        distance = 1
        while distance < lax.axis_size(axis):
            steps.append((axis, distance))
            distance *= 2
    halvings = 0
    while halvings < len(steps) - 1 and count >> (halvings + 1) >= 2 * SUB:
        halvings += 1
    return steps, halvings


def lat_margins(last, first=None):
    if first is None:
        got = swap(last, "lat", 1)
        return got, got
    up = [(i, i + 1) for i in range(lax.axis_size("lat") - 1)]
    return lax.ppermute(last, "lat", up), lax.ppermute(first, "lat", [(j, i) for i, j in up])


def lon_margins(left, right):
    size = lax.axis_size("lon")
    up = [(i, (i + 1) % size) for i in range(size)]
    return lax.ppermute(right, "lon", up), lax.ppermute(left, "lon", [(j, i) for i, j in up])


def body(fine_field, grad_out, conv_kernel, norm_gain, w_expand, w_contract, w_merge):
    z = Sizes(fine_field, w_merge, w_expand)
    ch, ff, lats = z.channels, z.wide, lax.axis_size("lat")
    fine = fine_field.reshape(z.fine, z.narrow)
    gain = norm_gain.reshape(1, ch)

    part = functools.partial
    split = ((z.halves, z.cells, LANE), F32)
    edges = [((z.samples * M * z.cols, ch), BF16)] * (1 if lats == 2 else 2)
    patches, coarse, fine_inv, *send, _ = kernel_call(
        part(merge_kernel, z),
        [((z.cells, 4 * z.narrow), BF16), ((z.cells, ch), BF16), ((z.fine, z.narrow), F32), *edges],
        (fine, w_merge),
        [((SUB * z.fine_stride, z.narrow), F32), split],
    )
    before, after = lat_margins(*send)
    weighted, w_centered, _ = kernel_call(
        part(weighted_kernel, z, lats),
        [((z.cells, ch), BF16), ((4 * z.narrow, 2 * ch), BF16)],
        (grad_out.reshape(z.cells, ch), w_merge),
        [split],
        flops=2_000_000_000,
    )
    slab = ((M * z.pad_col, ch), BF16)
    padded = ((z.cols * z.pad_col, ch), F32)
    pad_scratch = [((2 * z.samples * M * z.cols, ch), F32)]
    pad, left, right, _ = kernel_call(part(pad_kernel, z, lats), [padded, slab, slab], (coarse, before, after), pad_scratch)
    left, right = lon_margins(left, right)

    taps_s = ((KS * KS * SUB, ch), F32)

    def section_scratch(count):
        return [
            ((count, ch), F32),
            ((count, LANE), F32),
            ((count, ch), BF16),
            ((count, ff), BF16),
            ((count, ff), BF16),
            ((count, ch), BF16),
        ]

    outer = 2 * M * z.col
    inner = z.cells - outer
    section_in, mixed_in, expand, contract, gain_sum, _ = kernel_call(
        part(inner_kernel, z),
        [((inner, ch), BF16), ((inner, ch), F32), ((ch, ff), F32), ((ch, ff), F32), ((SUB, ch), F32)],
        (pad, conv_kernel, gain, w_expand, w_contract, coarse, weighted),
        [taps_s] + section_scratch(inner),
        flops=8_000_000_000,
    )
    section_out, mixed_out, mine, other, low, gain_sum, *send, _ = kernel_call(
        part(outer_kernel, z),
        [
            ((outer, ch), BF16),
            ((outer, ch), F32),
            ((ch, ff), BF16),
            ((ch, ff), BF16),
            ((z.cells, ch), BF16),
            ((SUB, ch), F32),
            *edges,
        ],
        (pad, left, right, conv_kernel, gain, w_expand, w_contract, coarse, weighted)
        + (expand, contract, gain_sum, mixed_in),
        [taps_s, ((6 * M * z.pad_col, ch), F32), ((2, ch, ff), F32), split] + section_scratch(outer),
        flops=8_000_000_000,
    )
    before, after = lat_margins(*send)
    steps, halvings = sum_steps(ch)
    wide, away, token = add(mine, swap(other, "dp", 1), halve=steps[0])
    pad_low, edge_left, edge_right, token = kernel_call(
        part(pad_kernel, z, lats), [padded, slab, slab], (low, before, after), pad_scratch, after=(token,)
    )
    left_low, right_low = lon_margins(edge_left, edge_right)
    full = (((z.cols + 2 * M) * z.pad_col, ch), F32)
    aux, token = kernel_call(
        part(terms_kernel, z),
        [((64, ch), F32)],
        (pad, left, right, mixed_in, mixed_out, gain_sum),
        [full, ((z.cells, ch), F32)],
        flops=5_000_000_000,
        after=(token,),
    )
    wide, away, token = add(wide, swap(away, *steps[0]), after=(token,), halve=steps[1])
    small = ((ch + 32, ch), BF16)
    back_coarse, mine, other, token = kernel_call(
        part(back_kernel, z),
        [((z.cells, ch), BF16), small, small],
        (pad_low, left_low, right_low, conv_kernel, weighted, patches, aux),
        [taps_s, full, ((ch, 4 * z.narrow), F32)],
        flops=5_000_000_000,
        after=(token,),
    )
    for n in range(1, halvings - 1):
        wide, away, token = add(wide, swap(away, *steps[n]), after=(token,), halve=steps[n + 1])
    wide, token = add(wide, swap(away, *steps[halvings - 1]), after=(token,))
    back_fine, token = kernel_call(
        part(unfold_kernel, z),
        [((SUB * z.fine_stride, z.narrow), F32)],
        (back_coarse, w_centered, patches),
        flops=3_000_000_000,
        after=(token,),
    )
    small_sum, token = add(mine, swap(other, "dp", 1), after=(token,))
    grad_fine, token = kernel_call(
        part(fine_kernel, z),
        [((z.fine, z.narrow), BF16)],
        (back_fine, fine_inv),
        flops=2_000_000_000,
        after=(token,),
    )
    section_all, token = kernel_call(
        part(section_kernel, z),
        [((z.cells, ch), BF16)],
        (section_in, section_out),
        [((z.cells, ch), F32), split],
        flops=2_000_000_000,
        after=(token,),
    )
    small_sum, token = add(small_sum, swap(small_sum, *steps[0]), after=(token,))
    for step in steps[halvings:]:
        wide, token = add(wide, swap(wide, *step), after=(token,))
    for step in steps[1:]:
        small_sum, token = add(small_sum, swap(small_sum, *step))
    for step in reversed(steps[1:halvings]):
        wide = join(wide, step)
    all_cells = z.samples * lax.axis_size("dp") * z.lat_rows * lats * z.cols * lax.axis_size("lon")
    factor = 1.0 / math.sqrt(all_cells)
    grad_expand, grad_contract, _ = kernel_call(
        part(final_wide_kernel, z, factor, steps[0]),
        [((ch // 2, ff), F32), ((ff // 2, ch), F32)],
        (wide, swap(wide, *steps[0])),
        [((ch, ff), BF16)],
    )
    grad_merge, grad_kernel, grad_gain, _ = kernel_call(
        part(final_small_kernel, z, factor),
        [((2 * z.narrow, ch), F32), ((KS * KS, ch // 2), F32), ((1, ch // 2), F32)],
        (small_sum,),
    )
    return (
        section_all.reshape(z.samples, z.lat_rows, z.cols, ch),
        grad_fine.reshape(fine_field.shape),
        grad_kernel,
        grad_gain.reshape(ch // 2),
        grad_expand,
        grad_contract,
        grad_merge,
    )


def solution(mesh):
    field = P(("groups", "dp"), "lat", "lon", None)
    owned = P(("groups", "dp"), None)
    return jax.shard_map(
        body,
        mesh=mesh,
        in_specs=(field, field, P(), P(), P(), P(), P()),
        out_specs=(field, field, P("groups", "dp"), P(("groups", "dp")), owned, owned, owned),
        check_vma=False,
    )
```

```python
import functools
import math

import jax
import jax.numpy as jnp
from jax import lax
from jax.experimental import pallas as pl
from jax.experimental.pallas import tpu as pltpu
from jax.sharding import PartitionSpec as P

KS = 7
M = KS // 2
SUB = 8
LANE = 128
F32 = jnp.float32
BF16 = jnp.bfloat16


def kernel_call(fn, outs, args, scratch=(), flops=0, after=()):
    outs = [*outs, ((SUB, LANE), F32)]
    whole = pl.BlockSpec(memory_space=pltpu.VMEM)
    count = len(args)
    held = sum(math.prod(s) * jnp.dtype(d).itemsize for s, d in scratch)

    def run(*refs):
        last = count + len(after) + len(outs) - 1
        refs[last][...] = jnp.zeros((SUB, LANE), F32)
        fn(*refs[:count], *refs[count + len(after) : last], *refs[last + 1 :])

    return pl.pallas_call(
        run,
        out_shape=[jax.ShapeDtypeStruct(s, d) for s, d in outs],
        in_specs=[whole] * (count + len(after)),
        out_specs=[whole] * len(outs),
        scratch_shapes=[pltpu.VMEM(s, d) for s, d in scratch],
        compiler_params=pltpu.CompilerParams(vmem_limit_bytes=held + 8 * 2**20),
        cost_estimate=pl.CostEstimate(
            flops=flops, bytes_accessed=sum(a.size * a.dtype.itemsize for a in args), transcendentals=0
        ),
    )(*args, *after)


def rows(start, size):
    return pl.ds(start if isinstance(start, int) else pl.multiple_of(start, SUB), size)


def lanes_at(start, size):
    return pl.ds(pl.multiple_of(start, LANE), size)


def rows16(start, size):
    return pl.ds(start if isinstance(start, int) else pl.multiple_of(start, 2 * SUB), size)


def dot(a, b):
    return jnp.dot(a, b, preferred_element_type=F32)


def dot_nt(a, b):
    return lax.dot_general(a, b, (((1,), (1,)), ((), ())), preferred_element_type=F32)


def dot_tn(a, b):
    return lax.dot_general(a, b, (((0,), (0,)), ((), ())), preferred_element_type=F32)


class Sizes:
    def __init__(self, fine_field, w_merge, w_expand):
        self.samples, fine_rows, fine_cols, self.narrow = fine_field.shape
        self.lat_rows, self.cols = fine_rows // 2, fine_cols // 2
        self.channels, self.wide = w_merge.shape[1], w_expand.shape[1]
        self.blocks = SUB // self.samples
        self.block_rows = self.lat_rows // self.blocks
        self.col = self.block_rows * SUB
        self.pad_rows = self.block_rows + 2 * M
        self.pad_col = self.pad_rows * SUB
        self.cells = self.cols * self.col
        self.fine = 4 * self.cells
        self.fine_block = 2 * self.block_rows * fine_cols
        self.fine_stride = self.fine_block + SUB
        self.fine_cols = fine_cols
        self.halves = self.channels // LANE


def fine_stats(z, x):
    ones = jnp.full((z.narrow, z.narrow), 1.0 / z.narrow, BF16)
    centered = x.astype(F32) - dot(x, ones)
    inverse = lax.rsqrt(dot((centered * centered).astype(BF16), ones) + 1e-06)
    return centered * inverse, inverse


def fine_rows_of(z, j, i, p, q):
    return pl.ds((2 * i + p) * z.fine_cols + 2 * j + q, SUB, stride=z.fine_stride)


def edge_rows(z, scratch, edge_refs):
    sides = []
    for first_row, block in ((z.block_rows - M, z.blocks - 1), (0, 0)):
        parts = []
        for r in range(M):
            for s in range(z.samples):
                start = (first_row + r) * SUB + s * z.blocks + block
                parts.append(
                    jnp.concatenate(
                        [scratch[h, pl.ds(start, z.cols, stride=z.col), :] for h in range(z.halves)], axis=1
                    )
                )
        sides.append(jnp.concatenate(parts, axis=0))
    if len(edge_refs) == 1:
        edge_refs[0][...] = jnp.where(lax.axis_index("lat") == 0, sides[0], sides[1]).astype(BF16)
    else:
        for ref, side in zip(edge_refs, sides):
            ref[...] = side.astype(BF16)


def merge_kernel(z, fine_ref, w_ref, patches_ref, coarse_ref, inv_ref, *rest):
    *edge_refs, unit_s, split_s = rest
    for t in range(SUB):
        at = slice(t * z.fine_block, (t + 1) * z.fine_block)
        unit, inverse = fine_stats(z, fine_ref[at, :])
        unit_s[t * z.fine_stride : t * z.fine_stride + z.fine_block, :] = unit
        inv_ref[at, :] = inverse
    group = 4

    def step(g, _):
        for jj in range(group):
            j = g * group + jj
            quarters = []
            for p in range(2):
                for q in range(2):
                    quarters.append(
                        jnp.concatenate(
                            [unit_s[fine_rows_of(z, j, i, p, q), :] for i in range(z.block_rows)], axis=0
                        ).astype(BF16)
                    )
            patches_ref[rows16(j * z.col, z.col), :] = jnp.concatenate(quarters, axis=1)
        at = rows16(g * group * z.col, group * z.col)
        low = dot(patches_ref[at, :], w_ref[...]).astype(BF16)
        coarse_ref[at, :] = low
        for h in range(z.halves):
            split_s[h, at, :] = low[:, h * LANE : (h + 1) * LANE].astype(F32)
        return 0

    lax.fori_loop(0, z.cols // group, step, 0, unroll=True)
    edge_rows(z, split_s, edge_refs)


def weighted_kernel(z, lats, grad_ref, w_ref, out_ref, centered_ref, split_s):
    for t in range(4):
        at = slice(t * z.narrow, (t + 1) * z.narrow)
        w = w_ref[at, :].astype(F32)
        w = w - jnp.sum(w, axis=0, keepdims=True) * (1.0 / z.narrow)
        high = w.astype(BF16)
        centered_ref[at, 0 : z.channels] = high
        centered_ref[at, z.channels :] = (w - high.astype(F32)).astype(BF16)
    place = lax.broadcasted_iota(jnp.int32, (z.col, LANE), 0)
    row = lax.axis_index("lat") * z.lat_rows + (place % SUB) % z.blocks * z.block_rows + place // SUB
    cosine = jnp.cos(math.pi * ((row.astype(F32) + 0.5) / (z.lat_rows * lats) - 0.5))
    for h in range(z.halves):
        split_s[h, :, :] = grad_ref[:, h * LANE : (h + 1) * LANE].astype(F32)

    def step(j, _):
        for h in range(z.halves):
            col = jnp.concatenate(
                [
                    split_s[h, pl.ds(i * z.cols + j, SUB, stride=z.block_rows * z.cols), :]
                    for i in range(z.block_rows)
                ],
                axis=0,
            )
            out_ref[rows16(j * z.col, z.col), h * LANE : (h + 1) * LANE] = (col * cosine).astype(BF16)
        return 0

    lax.fori_loop(0, z.cols, step, 0, unroll=8)


def pad_column(z, own, line, ref, start):
    place = lax.broadcasted_iota(jnp.int32, (SUB, z.channels), 0)
    ref[rows(start + M * SUB, z.col), :] = own
    for r in range(M):
        i = z.block_rows - M + r
        top = pltpu.roll(own[i * SUB : (i + 1) * SUB], 1, 0)
        low = pltpu.roll(own[r * SUB : (r + 1) * SUB], SUB - 1, 0)
        for s in range(z.samples):
            top = jnp.where(place == s * z.blocks, line(0, r, s), top)
            low = jnp.where(place == (s + 1) * z.blocks - 1, line(1, r, s), low)
        ref[rows(start + r * SUB, SUB), :] = top
        ref[rows(start + (M + z.block_rows + r) * SUB, SUB), :] = low


def pad_kernel(z, lats, own_ref, before_ref, after_ref, pad_ref, left_ref, right_ref, halo_s, slab_s):
    lat = lax.axis_index("lat")
    near = z.samples * M * z.cols
    halo_s[0:near, :] = jnp.where(lat > 0, before_ref[...].astype(F32), 0.0)
    halo_s[near : 2 * near, :] = jnp.where(lat < lats - 1, after_ref[...].astype(F32), 0.0)

    def step(j, _):
        own = own_ref[rows16(j * z.col, z.col), :].astype(F32)
        line = lambda side, r, s: halo_s[pl.ds(side * near + (r * z.samples + s) * z.cols + j, 1), :]
        pad_column(z, own, line, pad_ref, j * z.pad_col)
        return 0

    lax.fori_loop(0, z.cols, step, 0, unroll=4)
    own = M * z.col
    slab_s[own:, :] = jnp.zeros_like(slab_s[own:, :])
    for ref, first in ((left_ref, 0), (right_ref, z.cols - M)):
        for t in range(2 * M * z.samples):
            slab_s[own + t * M : own + (t + 1) * M, :] = halo_s[t * z.cols + first : t * z.cols + first + M, :]
        ref[0:own, :] = own_ref[first * z.col : (first + M) * z.col, :]
        ref[own:, :] = slab_s[own:, :].astype(BF16)


def unpack_slab(z, slab_ref, slab_s, ref, start):
    slab_s[...] = slab_ref[...].astype(F32)
    for c in range(M):
        line = lambda side, r, s: slab_s[pl.ds(M * z.col + ((side * M + r) * z.samples + s) * M + c, 1), :]
        pad_column(z, slab_s[c * z.col : (c + 1) * z.col, :], line, ref, start + c * z.pad_col)


def taps(z, pad, taps_s, start, h, flipped):
    lanes = slice(h * LANE, (h + 1) * LANE)
    total = jnp.zeros((z.block_rows, SUB, LANE), F32)
    for e in range(KS):
        column = pad[rows((start + e) * z.pad_col, z.pad_col), lanes].reshape(z.pad_rows, SUB, LANE)
        for a in range(KS):
            t = a * KS + e
            t = KS * KS - 1 - t if flipped else t
            total = total + column[a : a + z.block_rows] * taps_s[t * SUB : (t + 1) * SUB, lanes]
    return total.reshape(z.col, LANE)


def spread_taps(z, kern_ref, taps_s):
    for t in range(KS * KS):
        taps_s[t * SUB : (t + 1) * SUB, :] = jnp.broadcast_to(kern_ref[t : t + 1, :], (SUB, z.channels))


def gelu_parts(x):
    t = 1.0 / (1.0 + jnp.abs(x) * (0.3275911 * 0.7071067811865476))
    bell = jnp.exp(-0.5 * x * x)
    poly = 0.5 * 1.061405429
    for c in (-1.453152027, 1.421413741, -0.284496736, 0.254829592):
        poly = poly * t + 0.5 * c
    tail = poly * t * bell
    return jnp.where(x >= 0, 1.0 - tail, tail), x * bell * 0.3989422804014327


def row_mean(z, x):
    return jnp.sum(x, axis=-1, keepdims=True) * (1.0 / z.channels)


def section(z, pad, sources, groups, refs, scratch, chunk, section_ref, mixed_ref, taps_s):
    gain_ref, we_ref, wc_ref, coarse_ref, weighted_ref = refs
    unit_s, inv_s, normed_s, hidden_s, slope_s, weighted_s = scratch
    count = sum(g[2] for g in groups)

    def step(j, _):
        parts = [taps(z, pad, taps_s, sources(j), h, False) for h in range(z.halves)]
        at = rows16(j * z.col, z.col)
        mean = sum(jnp.sum(p, axis=-1, keepdims=True) for p in parts) * (1.0 / z.channels)
        parts = [p - mean for p in parts]
        var = sum(jnp.sum(p * p, axis=-1, keepdims=True) for p in parts) * (1.0 / z.channels)
        inverse = lax.rsqrt(var + 1e-06)
        inv_s[at, :] = jnp.broadcast_to(inverse, (z.col, LANE))
        for h, p in enumerate(parts):
            lanes = slice(h * LANE, (h + 1) * LANE)
            unit = p * inverse
            unit_s[at, lanes] = unit
            normed_s[at, lanes] = (unit * gain_ref[:, lanes]).astype(BF16)
        return 0

    lax.fori_loop(0, count // z.col, step, 0, unroll=2)
    for low, full, size in groups:
        weighted_s[low : low + size, :] = weighted_ref[full : full + size, :]
    gain_sum = jnp.zeros((SUB, z.channels), F32)
    for low, full, size in groups:
        for c in range(size // chunk):
            at = slice(low + c * chunk, low + (c + 1) * chunk)
            place = slice(full + c * chunk, full + (c + 1) * chunk)
            part = 256
            for f in range(z.wide // part):
                cut = slice(f * part, (f + 1) * part)
                pre = dot(normed_s[at, :], we_ref[:, cut])
                back = dot_nt(weighted_s[at, :], wc_ref[cut, :])
                phi, density = gelu_parts(pre)
                hidden_s[at, cut] = (pre * phi).astype(BF16)
                slope_s[at, cut] = (back * (phi + density)).astype(BF16)
            branch = dot(hidden_s[at, :], wc_ref[...])
            section_ref[at, :] = (coarse_ref[place, :].astype(F32) + branch).astype(BF16)
            back = dot_nt(slope_s[at, :], we_ref[...])
            unit = unit_s[at, :]
            gain_sum = gain_sum + jnp.sum((back * unit).reshape(-1, SUB, z.channels), axis=0)
            back = back * gain_ref[...]
            inverse = jnp.concatenate([inv_s[at, :]] * z.halves, axis=1)
            mixed_ref[at, :] = inverse * (back - row_mean(z, back) - unit * row_mean(z, back * unit))
    return gain_sum


def inner_kernel(
    z, pad_ref, kern_ref, gain_ref, we_ref, wc_ref, coarse_ref, weighted_ref,
    section_ref, mixed_ref, expand_ref, contract_ref, gain_sum_ref, taps_s, *scratch,
):
    spread_taps(z, kern_ref, taps_s)
    size = (z.cols - 2 * M) * z.col
    refs = (gain_ref, we_ref, wc_ref, coarse_ref, weighted_ref)
    gain_sum_ref[...] = section(
        z, pad_ref, lambda j: j, [(0, M * z.col, size)], refs, scratch, size // 2, section_ref, mixed_ref, taps_s
    )
    unit_s, inv_s, normed_s, hidden_s, slope_s, weighted_s = scratch
    expand_ref[...] = dot_tn(normed_s[...], slope_s[...])
    contract_ref[...] = dot_tn(weighted_s[...], hidden_s[...])


def outer_kernel(
    z, pad_ref, left_ref, right_ref, kern_ref, gain_ref, we_ref, wc_ref, coarse_ref, weighted_ref,
    expand_ref, contract_ref, gain_sum_ref, inner_mixed_ref,
    section_ref, mixed_ref, mine_ref, other_ref, low_ref, gain_out_ref, left_out_ref, right_out_ref, *rest,
):
    *edge_refs, taps_s, edge_s, sum_s, split_s, slab_s = rest[:-6]
    scratch = rest[-6:]
    spread_taps(z, kern_ref, taps_s)
    edge_columns(z, left_ref, pad_ref, right_ref, edge_s, slab_s)
    left_out_ref[...] = edge_s[0 : M * z.pad_col, :]
    right_out_ref[...] = edge_s[5 * M * z.pad_col :, :]
    size = M * z.col
    refs = (gain_ref, we_ref, wc_ref, coarse_ref, weighted_ref)
    groups = [(0, 0, size), (size, z.cells - size, size)]
    gain_sum = section(
        z, edge_s, lambda j: jnp.where(j < M, j, j + 2 * M), groups, refs, scratch, size, section_ref, mixed_ref, taps_s
    )
    unit_s, inv_s, normed_s, hidden_s, slope_s, weighted_s = scratch
    gain_out_ref[...] = gain_sum + gain_sum_ref[...]
    sum_s[0, :, :] = expand_ref[...] + dot_tn(normed_s[...], slope_s[...])
    sum_s[1, :, :] = contract_ref[...] + dot_tn(weighted_s[...], hidden_s[...])
    own = lax.axis_index("dp")
    half, cut = z.channels // 2, z.wide // 2
    for ref, owner in ((mine_ref, own), (other_ref, 1 - own)):
        ref[0:half, :] = sum_s[0, rows16(owner * half, half), :].astype(BF16)
        for t in range(2):
            ref[half:, t * cut : (t + 1) * cut] = sum_s[1, t * half : (t + 1) * half, lanes_at(owner * cut, cut)].astype(
                BF16
            )
    low_ref[0:size, :] = mixed_ref[0:size, :].astype(BF16)
    low_ref[size : z.cells - size, :] = inner_mixed_ref[...].astype(BF16)
    low_ref[z.cells - size :, :] = mixed_ref[size:, :].astype(BF16)
    for h in range(z.halves):
        split_s[h, :, :] = low_ref[:, h * LANE : (h + 1) * LANE].astype(F32)
    edge_rows(z, split_s, edge_refs)


def terms_kernel(
    z, pad_ref, left_ref, right_ref, inner_ref, outer_ref, gain_ref, aux_s, full_s, mixed_s
):
    edge, size = M * z.pad_col, M * z.col
    aux_s[...] = jnp.zeros_like(aux_s)
    for h in range(z.halves):
        lanes = slice(h * LANE, (h + 1) * LANE)
        full_s[0:edge, :] = left_ref[:, lanes]
        full_s[edge : edge + z.cols * z.pad_col, :] = pad_ref[:, lanes]
        full_s[edge + z.cols * z.pad_col :, :] = right_ref[:, lanes]
        mixed_s[0:size, :] = outer_ref[0:size, lanes]
        mixed_s[size : z.cells - size, :] = inner_ref[:, lanes]
        mixed_s[z.cells - size :, :] = outer_ref[size:, lanes]
        for e in range(KS):

            def step(j, sums):
                column = full_s[rows((j + e) * z.pad_col, z.pad_col), :].reshape(z.pad_rows, SUB, LANE)
                back = mixed_s[rows(j * z.col, z.col), :].reshape(z.block_rows, SUB, LANE)
                return tuple(sums[a] + jnp.sum(column[a : a + z.block_rows] * back, axis=0) for a in range(KS))

            zeros = tuple(jnp.zeros((SUB, LANE), F32) for _ in range(KS))
            sums = lax.fori_loop(0, z.cols, step, zeros, unroll=2)
            for a in range(KS):
                t = a * KS + e
                aux_s[t : t + 1, lanes] = jnp.sum(sums[a], axis=0, keepdims=True)
    aux_s[KS * KS : KS * KS + 1, :] = jnp.sum(gain_ref[...], axis=0, keepdims=True)


def spread(z, pad, taps_s, source, at, low, weighted_ref, out_ref):
    for h in range(z.halves):
        lanes = slice(h * LANE, (h + 1) * LANE)
        total = taps(z, pad, taps_s, source, h, True)
        out_ref[low, lanes] = (weighted_ref[at, lanes].astype(F32) + total).astype(BF16)


def back_inner_kernel(z, pad_ref, kern_ref, weighted_ref, coarse_ref, taps_s):
    spread_taps(z, kern_ref, taps_s)

    def step(j, _):
        spread(
            z, pad_ref, taps_s, j, rows16((j + M) * z.col, z.col), rows16(j * z.col, z.col), weighted_ref, coarse_ref
        )
        return 0

    lax.fori_loop(0, z.cols - 2 * M, step, 0, unroll=2)


def edge_columns(z, left_ref, pad_ref, right_ref, edge_s, slab_s):
    edge, near = M * z.pad_col, 2 * M * z.pad_col
    unpack_slab(z, left_ref, slab_s, edge_s, 0)
    edge_s[edge : edge + near, :] = pad_ref[0:near, :]
    edge_s[edge + near : edge + 2 * near, :] = pad_ref[z.cols * z.pad_col - near :, :]
    unpack_slab(z, right_ref, slab_s, edge_s, edge + 2 * near)


def back_outer_kernel(
    z, pad_ref, left_ref, right_ref, kern_ref, weighted_ref, patches_ref, inner_ref, aux_ref,
    coarse_ref, mine_ref, other_ref, taps_s, edge_s, sum_s, slab_s,
):
    spread_taps(z, kern_ref, taps_s)
    edge_columns(z, left_ref, pad_ref, right_ref, edge_s, slab_s)

    def step(j, _):
        for first, source in ((0, 0), (z.cols - M, 3 * M)):
            at = rows16((first + j) * z.col, z.col)
            spread(z, edge_s, taps_s, source + j, at, at, weighted_ref, coarse_ref)
        return 0

    lax.fori_loop(0, M, step, 0)
    size = M * z.col
    coarse_ref[size : z.cells - size, :] = inner_ref[...]
    sum_s[...] = dot_tn(coarse_ref[...], patches_ref[...])
    own, cut = lax.axis_index("dp"), 2 * z.narrow
    depth, half = aux_ref.shape[0] // 2, z.channels // 2
    for ref, owner in ((mine_ref, own), (other_ref, 1 - own)):
        ref[0 : z.channels, :] = sum_s[:, lanes_at(owner * cut, cut)].astype(BF16)
        for t in range(2):
            ref[z.channels :, t * half : (t + 1) * half] = aux_ref[
                t * depth : (t + 1) * depth, lanes_at(owner * half, half)
            ].astype(BF16)


def unfold_kernel(z, coarse_ref, centered_ref, patches_ref, back_ref):
    group = 4
    ones = jnp.full((z.narrow, z.narrow), 1.0 / z.narrow, BF16)

    def step(g, _):
        at = rows16(g * group * z.col, group * z.col)
        low = coarse_ref[at, :]
        back = dot_nt(jnp.concatenate([low, low], axis=1), centered_ref[...])
        for p in range(2):
            for q in range(2):
                lanes = slice((p * 2 + q) * z.narrow, (p * 2 + q + 1) * z.narrow)
                unit = patches_ref[at, lanes].astype(F32)
                up = back[:, lanes]
                up = up - unit * dot((up * unit).astype(BF16), ones)
                for jj in range(group):
                    for i in range(z.block_rows):
                        first = jj * z.col + i * SUB
                        back_ref[fine_rows_of(z, g * group + jj, i, p, q), :] = up[first : first + SUB]
        return 0

    lax.fori_loop(0, z.cols // group, step, 0, unroll=True)


def fine_kernel(z, back_ref, inv_ref, out_ref):
    def step(t, _):
        at = rows16(t * z.fine_block, z.fine_block)
        out_ref[at, :] = (inv_ref[at, :] * back_ref[rows(t * z.fine_stride, z.fine_block), :]).astype(BF16)
        return 0

    lax.fori_loop(0, SUB, step, 0, unroll=2)


def second(axis, distance):
    return lax.axis_index(axis) // distance % 2


def add_kernel(step, mine_ref, got_ref, *out_refs):
    if step is None:
        out_refs[0][...] = (mine_ref[...].astype(F32) + got_ref[...].astype(F32)).astype(BF16)
        return
    half, side = mine_ref.shape[0] // 2, second(*step)
    for ref, which in zip(out_refs, (side, 1 - side)):
        at = rows16(which * half, half)
        ref[...] = (mine_ref[at, :].astype(F32) + got_ref[at, :].astype(F32)).astype(BF16)


def join_kernel(step, mine_ref, got_ref, out_ref):
    half, side = mine_ref.shape[0], second(*step)
    out_ref[rows16(side * half, half), :] = mine_ref[...]
    out_ref[rows16((1 - side) * half, half), :] = got_ref[...]


def section_kernel(z, inner_ref, outer_ref, out_ref, all_s, split_s):
    size = M * z.col
    all_s[0:size, :] = outer_ref[0:size, :].astype(F32)
    all_s[size : z.cells - size, :] = inner_ref[...].astype(F32)
    all_s[z.cells - size :, :] = outer_ref[size:, :].astype(F32)

    def step(j, _):
        for h in range(z.halves):
            for i in range(z.block_rows):
                split_s[h, pl.ds(i * z.cols + j, SUB, stride=z.block_rows * z.cols), :] = all_s[
                    rows(j * z.col + i * SUB, SUB), h * LANE : (h + 1) * LANE
                ]
        return 0

    lax.fori_loop(0, z.cols, step, 0, unroll=8)
    for h in range(z.halves):
        out_ref[:, h * LANE : (h + 1) * LANE] = split_s[h, :, :].astype(BF16)


def final_wide_kernel(z, factor, step, mine_ref, got_ref, expand_ref, contract_ref, sum_ref):
    join_kernel(step, mine_ref, got_ref, sum_ref)
    half, cut = z.channels // 2, z.wide // 2
    expand_ref[...] = sum_ref[0:half, :].astype(F32) * factor
    for t in range(2):
        part = sum_ref[half:, t * cut : (t + 1) * cut].astype(F32) * factor
        contract_ref[:, t * half : (t + 1) * half] = part.T


def final_small_kernel(z, factor, mine_ref, got_ref, merge_ref, kernel_ref, gain_ref):
    total = (mine_ref[...].astype(F32) + got_ref[...].astype(F32)) * factor
    merge_ref[...] = total[0 : z.channels].T
    half = z.channels // 2
    tail = total[z.channels :]
    depth = tail.shape[0]
    kernel_ref[0:depth, :] = tail[:, :half]
    kernel_ref[depth:, :] = tail[: KS * KS - depth, half:]
    gain_ref[...] = tail[KS * KS - depth : KS * KS - depth + 1, half:]


def swap(x, axis, distance):
    size = lax.axis_size(axis)
    return lax.ppermute(x, axis, [(i, i ^ distance) for i in range(size)])


def add(mine, got, after=(), halve=None):
    count, width = mine.shape
    outs = [((count, width), BF16)] if halve is None else [((count // 2, width), BF16)] * 2
    return kernel_call(functools.partial(add_kernel, halve), outs, (mine, got), after=after)


def join(x, step, after):
    outs = [((2 * x.shape[0], x.shape[1]), BF16)]
    return kernel_call(functools.partial(join_kernel, step), outs, (x, swap(x, *step)), after=after)


def sum_steps(count):
    steps = []
    for axis in ("lat", "lon"):
        distance = 1
        while distance < lax.axis_size(axis):
            steps.append((axis, distance))
            distance *= 2
    halvings = 0
    while halvings < len(steps) - 1 and count >> (halvings + 1) >= 2 * SUB:
        halvings += 1
    return steps, halvings


def lat_margins(last, first=None):
    if first is None:
        got = swap(last, "lat", 1)
        return got, got
    up = [(i, i + 1) for i in range(lax.axis_size("lat") - 1)]
    return lax.ppermute(last, "lat", up), lax.ppermute(first, "lat", [(j, i) for i, j in up])


def lon_margins(left, right):
    size = lax.axis_size("lon")
    up = [(i, (i + 1) % size) for i in range(size)]
    return lax.ppermute(right, "lon", up), lax.ppermute(left, "lon", [(j, i) for i, j in up])


def body(fine_field, grad_out, conv_kernel, norm_gain, w_expand, w_contract, w_merge):
    z = Sizes(fine_field, w_merge, w_expand)
    ch, ff, lats = z.channels, z.wide, lax.axis_size("lat")
    fine = fine_field.reshape(z.fine, z.narrow)
    gain = norm_gain.reshape(1, ch)

    part = functools.partial
    split = ((z.halves, z.cells, LANE), F32)
    edges = [((z.samples * M * z.cols, ch), BF16)] * (1 if lats == 2 else 2)
    patches, coarse, fine_inv, *send, _ = kernel_call(
        part(merge_kernel, z),
        [((z.cells, 4 * z.narrow), BF16), ((z.cells, ch), BF16), ((z.fine, z.narrow), F32), *edges],
        (fine, w_merge),
        [((SUB * z.fine_stride, z.narrow), F32), split],
    )
    before, after = lat_margins(*send)
    weighted, w_centered, _ = kernel_call(
        part(weighted_kernel, z, lats),
        [((z.cells, ch), BF16), ((4 * z.narrow, 2 * ch), BF16)],
        (grad_out.reshape(z.cells, ch), w_merge),
        [split],
        flops=2_000_000_000,
    )
    slab_rows = -(-(M * z.col + 2 * M * z.samples * M) // (2 * SUB)) * 2 * SUB
    slab, slab_s = ((slab_rows, ch), BF16), ((slab_rows, ch), F32)
    padded = ((z.cols * z.pad_col, ch), F32)
    pad_scratch = [((2 * z.samples * M * z.cols, ch), F32), slab_s]
    pad, left, right, _ = kernel_call(part(pad_kernel, z, lats), [padded, slab, slab], (coarse, before, after), pad_scratch)
    left, right = lon_margins(left, right)

    taps_s = ((KS * KS * SUB, ch), F32)

    def section_scratch(count):
        return [
            ((count, ch), F32),
            ((count, LANE), F32),
            ((count, ch), BF16),
            ((count, ff), BF16),
            ((count, ff), BF16),
            ((count, ch), BF16),
        ]

    outer = 2 * M * z.col
    inner = z.cells - outer
    section_in, mixed_in, expand, contract, gain_sum, _ = kernel_call(
        part(inner_kernel, z),
        [((inner, ch), BF16), ((inner, ch), F32), ((ch, ff), F32), ((ch, ff), F32), ((SUB, ch), F32)],
        (pad, conv_kernel, gain, w_expand, w_contract, coarse, weighted),
        [taps_s] + section_scratch(inner),
        flops=8_000_000_000,
    )
    section_out, mixed_out, mine, other, low, gain_sum, left, right, *send, _ = kernel_call(
        part(outer_kernel, z),
        [
            ((outer, ch), BF16),
            ((outer, ch), F32),
            ((ch, ff), BF16),
            ((ch, ff), BF16),
            ((z.cells, ch), BF16),
            ((SUB, ch), F32),
            ((M * z.pad_col, ch), F32),
            ((M * z.pad_col, ch), F32),
            *edges,
        ],
        (pad, left, right, conv_kernel, gain, w_expand, w_contract, coarse, weighted)
        + (expand, contract, gain_sum, mixed_in),
        [taps_s, ((6 * M * z.pad_col, ch), F32), ((2, ch, ff), F32), split, slab_s] + section_scratch(outer),
        flops=8_000_000_000,
    )
    before, after = lat_margins(*send)
    steps, halvings = sum_steps(ch)
    wide, away, token = add(mine, swap(other, "dp", 1), halve=steps[0])
    pad_low, edge_left, edge_right, token = kernel_call(
        part(pad_kernel, z, lats), [padded, slab, slab], (low, before, after), pad_scratch, after=(token,)
    )
    left_low, right_low = lon_margins(edge_left, edge_right)
    bf = lambda count, width: ((count, width), BF16)
    aux, token = kernel_call(
        part(terms_kernel, z),
        [((64, ch), F32)],
        (pad, left, right, mixed_in, mixed_out, gain_sum),
        [(((z.cols + 2 * M) * z.pad_col, LANE), F32), ((z.cells, LANE), F32)],
        5_000_000_000,
        (token,),
    )
    wide, away, token = add(wide, swap(away, *steps[0]), after=(token,), halve=steps[1])
    back_inner, token = kernel_call(
        part(back_inner_kernel, z), [bf(inner, ch)], (pad_low, conv_kernel, weighted), [taps_s], 4_000_000_000, (token,)
    )
    for n in range(1, halvings - 1):
        wide, away, token = add(wide, swap(away, *steps[n]), after=(token,), halve=steps[n + 1])
    back_coarse, mine, other, token = kernel_call(
        part(back_outer_kernel, z),
        [bf(z.cells, ch), bf(ch + 32, 2 * z.narrow), bf(ch + 32, 2 * z.narrow)],
        (pad_low, left_low, right_low, conv_kernel, weighted, patches, back_inner, aux),
        [taps_s, ((6 * M * z.pad_col, ch), F32), ((ch, 4 * z.narrow), F32), slab_s],
        4_000_000_000,
        (token,),
    )
    small, token = add(mine, swap(other, "dp", 1))
    back_fine, token = kernel_call(
        part(unfold_kernel, z),
        [((SUB * z.fine_stride, z.narrow), F32)],
        (back_coarse, w_centered, patches),
        (),
        3_000_000_000,
        (token,),
    )
    wide, token = add(wide, swap(away, *steps[halvings - 1]), after=(token,))
    grad_fine, token = kernel_call(
        part(fine_kernel, z), [bf(z.fine, z.narrow)], (back_fine, fine_inv), (), 2_000_000_000, (token,)
    )
    small, token = add(small, swap(small, *steps[0]), after=(token,))
    section_all, token = kernel_call(
        part(section_kernel, z),
        [bf(z.cells, ch)],
        (section_in, section_out),
        [((z.cells, ch), F32), split],
        2_000_000_000,
        (token,),
    )
    for step in steps[halvings:]:
        wide, token = add(wide, swap(wide, *step), after=(token,))
    for step in steps[1:-1]:
        small, token = add(small, swap(small, *step), after=(token,))
    small_got = swap(small, *steps[-1])
    for step in reversed(steps[1:halvings]):
        wide, token = join(wide, step, (token,))
    all_cells = z.samples * lax.axis_size("dp") * z.lat_rows * lats * z.cols * lax.axis_size("lon")
    factor = 1.0 / math.sqrt(all_cells)
    grad_expand, grad_contract, token = kernel_call(
        part(final_wide_kernel, z, factor, steps[0]),
        [((ch // 2, ff), F32), ((ff // 2, ch), F32)],
        (wide, swap(wide, *steps[0])),
        [((ch, ff), BF16)],
        after=(token,),
    )
    grad_merge, grad_kernel, grad_gain, _ = kernel_call(
        part(final_small_kernel, z, factor),
        [((2 * z.narrow, ch), F32), ((KS * KS, ch // 2), F32), ((1, ch // 2), F32)],
        (small, small_got),
        after=(token,),
    )
    return (
        section_all.reshape(z.samples, z.lat_rows, z.cols, ch),
        grad_fine.reshape(fine_field.shape),
        grad_kernel,
        grad_gain.reshape(ch // 2),
        grad_expand,
        grad_contract,
        grad_merge,
    )


def solution(mesh):
    field = P(("groups", "dp"), "lat", "lon", None)
    owned = P(("groups", "dp"), None)
    return jax.shard_map(
        body,
        mesh=mesh,
        in_specs=(field, field, P(), P(), P(), P(), P()),
        out_specs=(field, field, P("groups", "dp"), P(("groups", "dp")), owned, owned, owned),
        check_vma=False,
    )
```

```python
import functools
import math

import jax
import jax.numpy as jnp
from jax import lax
from jax.experimental import pallas as pl
from jax.experimental.pallas import tpu as pltpu
from jax.sharding import PartitionSpec as P

KS = 7
M = KS // 2
SUB = 8
LANE = 128
F32 = jnp.float32
BF16 = jnp.bfloat16


def kernel_call(fn, outs, args, scratch=(), flops=0, after=()):
    outs = [*outs, ((SUB, LANE), F32)]
    whole = pl.BlockSpec(memory_space=pltpu.VMEM)
    count = len(args)
    held = sum(math.prod(s) * jnp.dtype(d).itemsize for s, d in scratch)

    def run(*refs):
        last = count + len(after) + len(outs) - 1
        refs[last][...] = jnp.zeros((SUB, LANE), F32)
        fn(*refs[:count], *refs[count + len(after) : last], *refs[last + 1 :])

    return pl.pallas_call(
        run,
        out_shape=[jax.ShapeDtypeStruct(s, d) for s, d in outs],
        in_specs=[whole] * (count + len(after)),
        out_specs=[whole] * len(outs),
        scratch_shapes=[pltpu.VMEM(s, d) for s, d in scratch],
        compiler_params=pltpu.CompilerParams(vmem_limit_bytes=held + 8 * 2**20),
        cost_estimate=pl.CostEstimate(
            flops=flops, bytes_accessed=sum(a.size * a.dtype.itemsize for a in args), transcendentals=0
        ),
    )(*args, *after)


def rows(start, size):
    return pl.ds(start if isinstance(start, int) else pl.multiple_of(start, SUB), size)


def lanes_at(start, size):
    return pl.ds(pl.multiple_of(start, LANE), size)


def rows16(start, size):
    return pl.ds(start if isinstance(start, int) else pl.multiple_of(start, 2 * SUB), size)


def dot(a, b):
    return jnp.dot(a, b, preferred_element_type=F32)


def dot_nt(a, b):
    return lax.dot_general(a, b, (((1,), (1,)), ((), ())), preferred_element_type=F32)


def dot_tn(a, b):
    return lax.dot_general(a, b, (((0,), (0,)), ((), ())), preferred_element_type=F32)


class Sizes:
    def __init__(self, fine_field, w_merge, w_expand):
        self.samples, fine_rows, fine_cols, self.narrow = fine_field.shape
        self.lat_rows, self.cols = fine_rows // 2, fine_cols // 2
        self.channels, self.wide = w_merge.shape[1], w_expand.shape[1]
        self.blocks = SUB // self.samples
        self.block_rows = self.lat_rows // self.blocks
        self.col = self.block_rows * SUB
        self.pad_rows = self.block_rows + 2 * M
        self.pad_col = self.pad_rows * SUB
        self.cells = self.cols * self.col
        self.fine = 4 * self.cells
        self.fine_block = 2 * self.block_rows * fine_cols
        self.fine_stride = self.fine_block + SUB
        self.fine_cols = fine_cols
        self.halves = self.channels // LANE


def fine_stats(z, x):
    ones = jnp.full((z.narrow, z.narrow), 1.0 / z.narrow, BF16)
    centered = x.astype(F32) - dot(x, ones)
    inverse = lax.rsqrt(dot((centered * centered).astype(BF16), ones) + 1e-06)
    return centered * inverse, inverse


def fine_rows_of(z, j, i, p, q):
    return pl.ds((2 * i + p) * z.fine_cols + 2 * j + q, SUB, stride=z.fine_stride)


def edge_rows(z, scratch, edge_refs):
    sides = []
    for first_row, block in ((z.block_rows - M, z.blocks - 1), (0, 0)):
        parts = []
        for r in range(M):
            for s in range(z.samples):
                start = (first_row + r) * SUB + s * z.blocks + block
                parts.append(
                    jnp.concatenate(
                        [scratch[h, pl.ds(start, z.cols, stride=z.col), :] for h in range(z.halves)], axis=1
                    )
                )
        sides.append(jnp.concatenate(parts, axis=0))
    if len(edge_refs) == 1:
        edge_refs[0][...] = jnp.where(lax.axis_index("lat") == 0, sides[0], sides[1]).astype(BF16)
    else:
        for ref, side in zip(edge_refs, sides):
            ref[...] = side.astype(BF16)


def merge_kernel(z, fine_ref, w_ref, patches_ref, coarse_ref, inv_ref, *rest):
    *edge_refs, unit_s, split_s = rest
    for t in range(SUB):
        at = slice(t * z.fine_block, (t + 1) * z.fine_block)
        unit, inverse = fine_stats(z, fine_ref[at, :])
        unit_s[t * z.fine_stride : t * z.fine_stride + z.fine_block, :] = unit
        inv_ref[at, :] = inverse
    group = 4

    def step(g, _):
        for jj in range(group):
            j = g * group + jj
            quarters = []
            for p in range(2):
                for q in range(2):
                    quarters.append(
                        jnp.concatenate(
                            [unit_s[fine_rows_of(z, j, i, p, q), :] for i in range(z.block_rows)], axis=0
                        ).astype(BF16)
                    )
            patches_ref[rows16(j * z.col, z.col), :] = jnp.concatenate(quarters, axis=1)
        at = rows16(g * group * z.col, group * z.col)
        low = dot(patches_ref[at, :], w_ref[...]).astype(BF16)
        coarse_ref[at, :] = low
        for h in range(z.halves):
            split_s[h, at, :] = low[:, h * LANE : (h + 1) * LANE].astype(F32)
        return 0

    lax.fori_loop(0, z.cols // group, step, 0, unroll=True)
    edge_rows(z, split_s, edge_refs)


def weighted_kernel(z, lats, grad_ref, w_ref, out_ref, centered_ref, split_s):
    for t in range(4):
        at = slice(t * z.narrow, (t + 1) * z.narrow)
        w = w_ref[at, :].astype(F32)
        w = w - jnp.sum(w, axis=0, keepdims=True) * (1.0 / z.narrow)
        high = w.astype(BF16)
        centered_ref[at, 0 : z.channels] = high
        centered_ref[at, z.channels :] = (w - high.astype(F32)).astype(BF16)
    place = lax.broadcasted_iota(jnp.int32, (z.col, LANE), 0)
    row = lax.axis_index("lat") * z.lat_rows + (place % SUB) % z.blocks * z.block_rows + place // SUB
    cosine = jnp.cos(math.pi * ((row.astype(F32) + 0.5) / (z.lat_rows * lats) - 0.5))
    for h in range(z.halves):
        split_s[h, :, :] = grad_ref[:, h * LANE : (h + 1) * LANE].astype(F32)

    def step(j, _):
        for h in range(z.halves):
            col = jnp.concatenate(
                [
                    split_s[h, pl.ds(i * z.cols + j, SUB, stride=z.block_rows * z.cols), :]
                    for i in range(z.block_rows)
                ],
                axis=0,
            )
            out_ref[rows16(j * z.col, z.col), h * LANE : (h + 1) * LANE] = (col * cosine).astype(BF16)
        return 0

    lax.fori_loop(0, z.cols, step, 0, unroll=8)


def pad_column(z, own, line, ref, start):
    place = lax.broadcasted_iota(jnp.int32, (SUB, z.channels), 0)
    ref[rows(start + M * SUB, z.col), :] = own
    for r in range(M):
        i = z.block_rows - M + r
        top = pltpu.roll(own[i * SUB : (i + 1) * SUB], 1, 0)
        low = pltpu.roll(own[r * SUB : (r + 1) * SUB], SUB - 1, 0)
        for s in range(z.samples):
            top = jnp.where(place == s * z.blocks, line(0, r, s), top)
            low = jnp.where(place == (s + 1) * z.blocks - 1, line(1, r, s), low)
        ref[rows(start + r * SUB, SUB), :] = top
        ref[rows(start + (M + z.block_rows + r) * SUB, SUB), :] = low


def pad_kernel(z, lats, own_ref, before_ref, after_ref, pad_ref, left_ref, right_ref, halo_s, slab_s):
    lat = lax.axis_index("lat")
    near = z.samples * M * z.cols
    halo_s[0:near, :] = jnp.where(lat > 0, before_ref[...].astype(F32), 0.0)
    halo_s[near : 2 * near, :] = jnp.where(lat < lats - 1, after_ref[...].astype(F32), 0.0)

    def step(j, _):
        own = own_ref[rows16(j * z.col, z.col), :].astype(F32)
        line = lambda side, r, s: halo_s[pl.ds(side * near + (r * z.samples + s) * z.cols + j, 1), :]
        pad_column(z, own, line, pad_ref, j * z.pad_col)
        return 0

    lax.fori_loop(0, z.cols, step, 0, unroll=4)
    own = M * z.col
    slab_s[own:, :] = jnp.zeros_like(slab_s[own:, :])
    for ref, first in ((left_ref, 0), (right_ref, z.cols - M)):
        for t in range(2 * M * z.samples):
            slab_s[own + t * M : own + (t + 1) * M, :] = halo_s[t * z.cols + first : t * z.cols + first + M, :]
        ref[0:own, :] = own_ref[first * z.col : (first + M) * z.col, :]
        ref[own:, :] = slab_s[own:, :].astype(BF16)


def unpack_slab(z, slab_ref, slab_s, ref, start):
    slab_s[...] = slab_ref[...].astype(F32)
    for c in range(M):
        line = lambda side, r, s: slab_s[pl.ds(M * z.col + ((side * M + r) * z.samples + s) * M + c, 1), :]
        pad_column(z, slab_s[c * z.col : (c + 1) * z.col, :], line, ref, start + c * z.pad_col)


def taps(z, pad, taps_s, start, h, flipped):
    lanes = slice(h * LANE, (h + 1) * LANE)
    total = jnp.zeros((z.block_rows, SUB, LANE), F32)
    for e in range(KS):
        column = pad[rows((start + e) * z.pad_col, z.pad_col), lanes].reshape(z.pad_rows, SUB, LANE)
        for a in range(KS):
            t = a * KS + e
            t = KS * KS - 1 - t if flipped else t
            total = total + column[a : a + z.block_rows] * taps_s[t * SUB : (t + 1) * SUB, lanes]
    return total.reshape(z.col, LANE)


def spread_taps(z, kern_ref, taps_s):
    for t in range(KS * KS):
        taps_s[t * SUB : (t + 1) * SUB, :] = jnp.broadcast_to(kern_ref[t : t + 1, :], (SUB, z.channels))


def gelu_parts(x):
    t = 1.0 / (1.0 + jnp.abs(x) * (0.3275911 * 0.7071067811865476))
    bell = jnp.exp(-0.5 * x * x)
    poly = 0.5 * 1.061405429
    for c in (-1.453152027, 1.421413741, -0.284496736, 0.254829592):
        poly = poly * t + 0.5 * c
    tail = poly * t * bell
    return jnp.where(x >= 0, 1.0 - tail, tail), x * bell * 0.3989422804014327


def row_mean(z, x):
    return jnp.sum(x, axis=-1, keepdims=True) * (1.0 / z.channels)


def section(z, pad, sources, groups, refs, scratch, chunk, section_ref, mixed_ref, taps_s):
    gain_ref, we_ref, wc_ref, coarse_ref, weighted_ref = refs
    unit_s, inv_s, normed_s, hidden_s, slope_s, weighted_s = scratch
    count = sum(g[2] for g in groups)

    def step(j, _):
        parts = [taps(z, pad, taps_s, sources(j), h, False) for h in range(z.halves)]
        at = rows16(j * z.col, z.col)
        mean = sum(jnp.sum(p, axis=-1, keepdims=True) for p in parts) * (1.0 / z.channels)
        parts = [p - mean for p in parts]
        var = sum(jnp.sum(p * p, axis=-1, keepdims=True) for p in parts) * (1.0 / z.channels)
        inverse = lax.rsqrt(var + 1e-06)
        inv_s[at, :] = jnp.broadcast_to(inverse, (z.col, LANE))
        for h, p in enumerate(parts):
            lanes = slice(h * LANE, (h + 1) * LANE)
            unit = p * inverse
            unit_s[at, lanes] = unit
            normed_s[at, lanes] = (unit * gain_ref[:, lanes]).astype(BF16)
        return 0

    lax.fori_loop(0, count // z.col, step, 0, unroll=2)
    for low, full, size in groups:
        weighted_s[low : low + size, :] = weighted_ref[full : full + size, :]
    gain_sum = jnp.zeros((SUB, z.channels), F32)
    for low, full, size in groups:
        for c in range(size // chunk):
            at = slice(low + c * chunk, low + (c + 1) * chunk)
            place = slice(full + c * chunk, full + (c + 1) * chunk)
            part = 256
            for f in range(z.wide // part):
                cut = slice(f * part, (f + 1) * part)
                pre = dot(normed_s[at, :], we_ref[:, cut])
                back = dot_nt(weighted_s[at, :], wc_ref[cut, :])
                phi, density = gelu_parts(pre)
                hidden_s[at, cut] = (pre * phi).astype(BF16)
                slope_s[at, cut] = (back * (phi + density)).astype(BF16)
            branch = dot(hidden_s[at, :], wc_ref[...])
            section_ref[at, :] = (coarse_ref[place, :].astype(F32) + branch).astype(BF16)
            back = dot_nt(slope_s[at, :], we_ref[...])
            unit = unit_s[at, :]
            gain_sum = gain_sum + jnp.sum((back * unit).reshape(-1, SUB, z.channels), axis=0)
            back = back * gain_ref[...]
            inverse = jnp.concatenate([inv_s[at, :]] * z.halves, axis=1)
            mixed_ref[at, :] = inverse * (back - row_mean(z, back) - unit * row_mean(z, back * unit))
    return gain_sum


def inner_kernel(
    z, pad_ref, kern_ref, gain_ref, we_ref, wc_ref, coarse_ref, weighted_ref,
    section_ref, mixed_ref, expand_ref, contract_ref, gain_sum_ref, taps_s, *scratch,
):
    spread_taps(z, kern_ref, taps_s)
    size = (z.cols - 2 * M) * z.col
    refs = (gain_ref, we_ref, wc_ref, coarse_ref, weighted_ref)
    gain_sum_ref[...] = section(
        z, pad_ref, lambda j: j, [(0, M * z.col, size)], refs, scratch, size // 2, section_ref, mixed_ref, taps_s
    )
    unit_s, inv_s, normed_s, hidden_s, slope_s, weighted_s = scratch
    expand_ref[...] = dot_tn(normed_s[...], slope_s[...])
    contract_ref[...] = dot_tn(weighted_s[...], hidden_s[...])


def outer_kernel(
    z, pad_ref, left_ref, right_ref, kern_ref, gain_ref, we_ref, wc_ref, coarse_ref, weighted_ref,
    expand_ref, contract_ref, gain_sum_ref, inner_mixed_ref,
    section_ref, mixed_ref, mine_ref, other_ref, low_ref, gain_out_ref, left_out_ref, right_out_ref, *rest,
):
    *edge_refs, taps_s, edge_s, sum_s, split_s, slab_s = rest[:-6]
    scratch = rest[-6:]
    spread_taps(z, kern_ref, taps_s)
    edge_columns(z, left_ref, pad_ref, right_ref, edge_s, slab_s)
    left_out_ref[...] = edge_s[0 : M * z.pad_col, :]
    right_out_ref[...] = edge_s[5 * M * z.pad_col :, :]
    size = M * z.col
    refs = (gain_ref, we_ref, wc_ref, coarse_ref, weighted_ref)
    groups = [(0, 0, size), (size, z.cells - size, size)]
    gain_sum = section(
        z, edge_s, lambda j: jnp.where(j < M, j, j + 2 * M), groups, refs, scratch, size, section_ref, mixed_ref, taps_s
    )
    unit_s, inv_s, normed_s, hidden_s, slope_s, weighted_s = scratch
    gain_out_ref[...] = gain_sum + gain_sum_ref[...]
    sum_s[0, :, :] = expand_ref[...] + dot_tn(normed_s[...], slope_s[...])
    sum_s[1, :, :] = contract_ref[...] + dot_tn(weighted_s[...], hidden_s[...])
    own = lax.axis_index("dp")
    half, cut = z.channels // 2, z.wide // 2
    for ref, owner in ((mine_ref, own), (other_ref, 1 - own)):
        ref[0:half, :] = sum_s[0, rows16(owner * half, half), :].astype(BF16)
        for t in range(2):
            ref[half:, t * cut : (t + 1) * cut] = sum_s[1, t * half : (t + 1) * half, lanes_at(owner * cut, cut)].astype(
                BF16
            )
    low_ref[0:size, :] = mixed_ref[0:size, :].astype(BF16)
    low_ref[size : z.cells - size, :] = inner_mixed_ref[...].astype(BF16)
    low_ref[z.cells - size :, :] = mixed_ref[size:, :].astype(BF16)
    for h in range(z.halves):
        split_s[h, :, :] = low_ref[:, h * LANE : (h + 1) * LANE].astype(F32)
    edge_rows(z, split_s, edge_refs)


def terms_kernel(z, h, pad_ref, left_ref, right_ref, inner_ref, outer_ref, gain_ref, out_ref, full_s, mixed_s):
    edge, size = M * z.pad_col, M * z.col
    lanes = slice(h * LANE, (h + 1) * LANE)
    full_s[0:edge, :] = left_ref[:, lanes]
    full_s[edge : edge + z.cols * z.pad_col, :] = pad_ref[:, lanes]
    full_s[edge + z.cols * z.pad_col :, :] = right_ref[:, lanes]
    mixed_s[0:size, :] = outer_ref[0:size, lanes]
    mixed_s[size : z.cells - size, :] = inner_ref[:, lanes]
    mixed_s[z.cells - size :, :] = outer_ref[size:, lanes]
    out_ref[...] = jnp.zeros_like(out_ref)
    for e in range(KS):

        def step(j, sums):
            column = full_s[rows((j + e) * z.pad_col, z.pad_col), :].reshape(z.pad_rows, SUB, LANE)
            back = mixed_s[rows(j * z.col, z.col), :].reshape(z.block_rows, SUB, LANE)
            return tuple(sums[a] + jnp.sum(column[a : a + z.block_rows] * back, axis=0) for a in range(KS))

        zeros = tuple(jnp.zeros((SUB, LANE), F32) for _ in range(KS))
        sums = lax.fori_loop(0, z.cols, step, zeros, unroll=2)
        for a in range(KS):
            t = a * KS + e
            out_ref[t : t + 1, :] = jnp.sum(sums[a], axis=0, keepdims=True)
    out_ref[KS * KS : KS * KS + 1, :] = jnp.sum(gain_ref[:, lanes], axis=0, keepdims=True)


def spread(z, pad, taps_s, source, at, low, weighted_ref, out_ref):
    for h in range(z.halves):
        lanes = slice(h * LANE, (h + 1) * LANE)
        total = taps(z, pad, taps_s, source, h, True)
        out_ref[low, lanes] = (weighted_ref[at, lanes].astype(F32) + total).astype(BF16)


def back_inner_kernel(z, pad_ref, kern_ref, weighted_ref, coarse_ref, taps_s):
    spread_taps(z, kern_ref, taps_s)

    def step(j, _):
        spread(
            z, pad_ref, taps_s, j, rows16((j + M) * z.col, z.col), rows16(j * z.col, z.col), weighted_ref, coarse_ref
        )
        return 0

    lax.fori_loop(0, z.cols - 2 * M, step, 0, unroll=2)


def edge_columns(z, left_ref, pad_ref, right_ref, edge_s, slab_s):
    edge, near = M * z.pad_col, 2 * M * z.pad_col
    unpack_slab(z, left_ref, slab_s, edge_s, 0)
    edge_s[edge : edge + near, :] = pad_ref[0:near, :]
    edge_s[edge + near : edge + 2 * near, :] = pad_ref[z.cols * z.pad_col - near :, :]
    unpack_slab(z, right_ref, slab_s, edge_s, edge + 2 * near)


def back_outer_kernel(
    z, pad_ref, left_ref, right_ref, kern_ref, weighted_ref, patches_ref, inner_ref, low_aux_ref, high_aux_ref,
    coarse_ref, mine_ref, other_ref, taps_s, edge_s, sum_s, slab_s,
):
    spread_taps(z, kern_ref, taps_s)
    edge_columns(z, left_ref, pad_ref, right_ref, edge_s, slab_s)

    def step(j, _):
        for first, source in ((0, 0), (z.cols - M, 3 * M)):
            at = rows16((first + j) * z.col, z.col)
            spread(z, edge_s, taps_s, source + j, at, at, weighted_ref, coarse_ref)
        return 0

    lax.fori_loop(0, M, step, 0)
    size = M * z.col
    coarse_ref[size : z.cells - size, :] = inner_ref[...]
    sum_s[...] = dot_tn(coarse_ref[...], patches_ref[...])
    own, cut = lax.axis_index("dp"), 2 * z.narrow
    depth, half = low_aux_ref.shape[0] // 2, z.channels // 2
    for ref, owner in ((mine_ref, own), (other_ref, 1 - own)):
        ref[0 : z.channels, :] = sum_s[:, lanes_at(owner * cut, cut)].astype(BF16)
        for t in range(2):
            at = slice(t * depth, (t + 1) * depth)
            aux = jnp.where(owner == 0, low_aux_ref[at, :], high_aux_ref[at, :])
            ref[z.channels :, t * half : (t + 1) * half] = aux.astype(BF16)


def unfold_kernel(z, coarse_ref, centered_ref, patches_ref, back_ref):
    group = 4
    ones = jnp.full((z.narrow, z.narrow), 1.0 / z.narrow, BF16)

    def step(g, _):
        at = rows16(g * group * z.col, group * z.col)
        low = coarse_ref[at, :]
        back = dot_nt(jnp.concatenate([low, low], axis=1), centered_ref[...])
        for p in range(2):
            for q in range(2):
                lanes = slice((p * 2 + q) * z.narrow, (p * 2 + q + 1) * z.narrow)
                unit = patches_ref[at, lanes].astype(F32)
                up = back[:, lanes]
                up = up - unit * dot((up * unit).astype(BF16), ones)
                for jj in range(group):
                    for i in range(z.block_rows):
                        first = jj * z.col + i * SUB
                        back_ref[fine_rows_of(z, g * group + jj, i, p, q), :] = up[first : first + SUB]
        return 0

    lax.fori_loop(0, z.cols // group, step, 0, unroll=True)


def fine_kernel(z, back_ref, inv_ref, out_ref):
    def step(t, _):
        at = rows16(t * z.fine_block, z.fine_block)
        out_ref[at, :] = (inv_ref[at, :] * back_ref[rows(t * z.fine_stride, z.fine_block), :]).astype(BF16)
        return 0

    lax.fori_loop(0, SUB, step, 0, unroll=2)


def second(axis, distance):
    return lax.axis_index(axis) // distance % 2


def add_kernel(step, mine_ref, got_ref, *out_refs):
    if step is None:
        out_refs[0][...] = (mine_ref[...].astype(F32) + got_ref[...].astype(F32)).astype(BF16)
        return
    half, side = mine_ref.shape[0] // 2, second(*step)
    for ref, which in zip(out_refs, (side, 1 - side)):
        at = rows16(which * half, half)
        ref[...] = (mine_ref[at, :].astype(F32) + got_ref[at, :].astype(F32)).astype(BF16)


def join_kernel(step, mine_ref, got_ref, out_ref):
    half, side = mine_ref.shape[0], second(*step)
    out_ref[rows16(side * half, half), :] = mine_ref[...]
    out_ref[rows16((1 - side) * half, half), :] = got_ref[...]


def section_kernel(z, inner_ref, outer_ref, out_ref, all_s, split_s):
    size = M * z.col
    all_s[0:size, :] = outer_ref[0:size, :].astype(F32)
    all_s[size : z.cells - size, :] = inner_ref[...].astype(F32)
    all_s[z.cells - size :, :] = outer_ref[size:, :].astype(F32)

    def step(j, _):
        for h in range(z.halves):
            for i in range(z.block_rows):
                split_s[h, pl.ds(i * z.cols + j, SUB, stride=z.block_rows * z.cols), :] = all_s[
                    rows(j * z.col + i * SUB, SUB), h * LANE : (h + 1) * LANE
                ]
        return 0

    lax.fori_loop(0, z.cols, step, 0, unroll=8)
    for h in range(z.halves):
        out_ref[:, h * LANE : (h + 1) * LANE] = split_s[h, :, :].astype(BF16)


def final_wide_kernel(z, factor, step, mine_ref, got_ref, expand_ref, contract_ref, sum_ref):
    join_kernel(step, mine_ref, got_ref, sum_ref)
    half, cut = z.channels // 2, z.wide // 2
    expand_ref[...] = sum_ref[0:half, :].astype(F32) * factor
    for t in range(2):
        part = sum_ref[half:, t * cut : (t + 1) * cut].astype(F32) * factor
        contract_ref[:, t * half : (t + 1) * half] = part.T


def final_small_kernel(z, factor, mine_ref, got_ref, merge_ref, kernel_ref, gain_ref):
    total = (mine_ref[...].astype(F32) + got_ref[...].astype(F32)) * factor
    merge_ref[...] = total[0 : z.channels].T
    half = z.channels // 2
    tail = total[z.channels :]
    depth = tail.shape[0]
    kernel_ref[0:depth, :] = tail[:, :half]
    kernel_ref[depth:, :] = tail[: KS * KS - depth, half:]
    gain_ref[...] = tail[KS * KS - depth : KS * KS - depth + 1, half:]


def swap(x, axis, distance):
    size = lax.axis_size(axis)
    return lax.ppermute(x, axis, [(i, i ^ distance) for i in range(size)])


def add(mine, got, after=(), halve=None):
    count, width = mine.shape
    outs = [((count, width), BF16)] if halve is None else [((count // 2, width), BF16)] * 2
    return kernel_call(functools.partial(add_kernel, halve), outs, (mine, got), after=after)


def join(x, step, after):
    outs = [((2 * x.shape[0], x.shape[1]), BF16)]
    return kernel_call(functools.partial(join_kernel, step), outs, (x, swap(x, *step)), after=after)


def sum_steps(count):
    steps = []
    for axis in ("lat", "lon"):
        distance = 1
        while distance < lax.axis_size(axis):
            steps.append((axis, distance))
            distance *= 2
    halvings = 0
    while halvings < len(steps) - 1 and count >> (halvings + 1) >= 2 * SUB:
        halvings += 1
    return steps, halvings


def lat_margins(last, first=None):
    if first is None:
        got = swap(last, "lat", 1)
        return got, got
    up = [(i, i + 1) for i in range(lax.axis_size("lat") - 1)]
    return lax.ppermute(last, "lat", up), lax.ppermute(first, "lat", [(j, i) for i, j in up])


def lon_margins(left, right):
    size = lax.axis_size("lon")
    up = [(i, (i + 1) % size) for i in range(size)]
    return lax.ppermute(right, "lon", up), lax.ppermute(left, "lon", [(j, i) for i, j in up])


def body(fine_field, grad_out, conv_kernel, norm_gain, w_expand, w_contract, w_merge):
    z = Sizes(fine_field, w_merge, w_expand)
    ch, ff, lats = z.channels, z.wide, lax.axis_size("lat")
    fine = fine_field.reshape(z.fine, z.narrow)
    gain = norm_gain.reshape(1, ch)

    part = functools.partial
    split = ((z.halves, z.cells, LANE), F32)
    edges = [((z.samples * M * z.cols, ch), BF16)] * (1 if lats == 2 else 2)
    patches, coarse, fine_inv, *send, _ = kernel_call(
        part(merge_kernel, z),
        [((z.cells, 4 * z.narrow), BF16), ((z.cells, ch), BF16), ((z.fine, z.narrow), F32), *edges],
        (fine, w_merge),
        [((SUB * z.fine_stride, z.narrow), F32), split],
    )
    before, after = lat_margins(*send)
    weighted, w_centered, _ = kernel_call(
        part(weighted_kernel, z, lats),
        [((z.cells, ch), BF16), ((4 * z.narrow, 2 * ch), BF16)],
        (grad_out.reshape(z.cells, ch), w_merge),
        [split],
        flops=2_000_000_000,
    )
    slab_rows = -(-(M * z.col + 2 * M * z.samples * M) // (2 * SUB)) * 2 * SUB
    slab, slab_s = ((slab_rows, ch), BF16), ((slab_rows, ch), F32)
    padded = ((z.cols * z.pad_col, ch), F32)
    pad_scratch = [((2 * z.samples * M * z.cols, ch), F32), slab_s]
    pad, left, right, _ = kernel_call(part(pad_kernel, z, lats), [padded, slab, slab], (coarse, before, after), pad_scratch)
    left, right = lon_margins(left, right)

    taps_s = ((KS * KS * SUB, ch), F32)

    def section_scratch(count):
        return [
            ((count, ch), F32),
            ((count, LANE), F32),
            ((count, ch), BF16),
            ((count, ff), BF16),
            ((count, ff), BF16),
            ((count, ch), BF16),
        ]

    outer = 2 * M * z.col
    inner = z.cells - outer
    section_in, mixed_in, expand, contract, gain_sum, _ = kernel_call(
        part(inner_kernel, z),
        [((inner, ch), BF16), ((inner, ch), F32), ((ch, ff), F32), ((ch, ff), F32), ((SUB, ch), F32)],
        (pad, conv_kernel, gain, w_expand, w_contract, coarse, weighted),
        [taps_s] + section_scratch(inner),
        flops=8_000_000_000,
    )
    section_out, mixed_out, mine, other, low, gain_sum, left, right, *send, _ = kernel_call(
        part(outer_kernel, z),
        [
            ((outer, ch), BF16),
            ((outer, ch), F32),
            ((ch, ff), BF16),
            ((ch, ff), BF16),
            ((z.cells, ch), BF16),
            ((SUB, ch), F32),
            ((M * z.pad_col, ch), F32),
            ((M * z.pad_col, ch), F32),
            *edges,
        ],
        (pad, left, right, conv_kernel, gain, w_expand, w_contract, coarse, weighted)
        + (expand, contract, gain_sum, mixed_in),
        [taps_s, ((6 * M * z.pad_col, ch), F32), ((2, ch, ff), F32), split, slab_s] + section_scratch(outer),
        flops=8_000_000_000,
    )
    before, after = lat_margins(*send)
    steps, halvings = sum_steps(ch)
    wide, away, token = add(mine, swap(other, "dp", 1), halve=steps[0])
    pad_low, edge_left, edge_right, token = kernel_call(
        part(pad_kernel, z, lats), [padded, slab, slab], (low, before, after), pad_scratch, after=(token,)
    )
    left_low, right_low = lon_margins(edge_left, edge_right)
    bf = lambda count, width: ((count, width), BF16)

    def terms(h, token):
        return kernel_call(
            part(terms_kernel, z, h),
            [((64, LANE), F32)],
            (pad, left, right, mixed_in, mixed_out, gain_sum),
            [(((z.cols + 2 * M) * z.pad_col, LANE), F32), ((z.cells, LANE), F32)],
            3_000_000_000,
            (token,),
        )

    low_aux, token = terms(0, token)
    wide, away, token = add(wide, swap(away, *steps[0]), after=(token,), halve=steps[1])
    high_aux, token = terms(1, token)
    back_inner, token = kernel_call(
        part(back_inner_kernel, z), [bf(inner, ch)], (pad_low, conv_kernel, weighted), [taps_s], 4_000_000_000, (token,)
    )
    for n in range(1, halvings - 1):
        wide, away, token = add(wide, swap(away, *steps[n]), after=(token,), halve=steps[n + 1])
    wide, token = add(wide, swap(away, *steps[halvings - 1]), after=(token,))
    back_coarse, mine, other, token = kernel_call(
        part(back_outer_kernel, z),
        [bf(z.cells, ch), bf(ch + 32, 2 * z.narrow), bf(ch + 32, 2 * z.narrow)],
        (pad_low, left_low, right_low, conv_kernel, weighted, patches, back_inner, low_aux, high_aux),
        [taps_s, ((6 * M * z.pad_col, ch), F32), ((ch, 4 * z.narrow), F32), slab_s],
        4_000_000_000,
        (token,),
    )
    back_fine, token = kernel_call(
        part(unfold_kernel, z),
        [((SUB * z.fine_stride, z.narrow), F32)],
        (back_coarse, w_centered, patches),
        (),
        3_000_000_000,
        (token,),
    )
    small, token = add(mine, swap(other, "dp", 1), after=(token,))
    grad_fine, token = kernel_call(
        part(fine_kernel, z), [bf(z.fine, z.narrow)], (back_fine, fine_inv), (), 2_000_000_000, (token,)
    )
    for step in steps[halvings:]:
        wide, token = add(wide, swap(wide, *step), after=(token,))
    small, token = add(small, swap(small, *steps[0]), after=(token,))
    section_all, token = kernel_call(
        part(section_kernel, z),
        [bf(z.cells, ch)],
        (section_in, section_out),
        [((z.cells, ch), F32), split],
        2_000_000_000,
        (token,),
    )
    for step in reversed(steps[1:halvings]):
        wide, token = join(wide, step, (token,))
    for step in steps[1:-1]:
        small, token = add(small, swap(small, *step), after=(token,))
    small_got = swap(small, *steps[-1])
    all_cells = z.samples * lax.axis_size("dp") * z.lat_rows * lats * z.cols * lax.axis_size("lon")
    factor = 1.0 / math.sqrt(all_cells)
    grad_expand, grad_contract, token = kernel_call(
        part(final_wide_kernel, z, factor, steps[0]),
        [((ch // 2, ff), F32), ((ff // 2, ch), F32)],
        (wide, swap(wide, *steps[0])),
        [((ch, ff), BF16)],
        after=(token,),
    )
    grad_merge, grad_kernel, grad_gain, _ = kernel_call(
        part(final_small_kernel, z, factor),
        [((2 * z.narrow, ch), F32), ((KS * KS, ch // 2), F32), ((1, ch // 2), F32)],
        (small, small_got),
        after=(token,),
    )
    return (
        section_all.reshape(z.samples, z.lat_rows, z.cols, ch),
        grad_fine.reshape(fine_field.shape),
        grad_kernel,
        grad_gain.reshape(ch // 2),
        grad_expand,
        grad_contract,
        grad_merge,
    )


def solution(mesh):
    field = P(("groups", "dp"), "lat", "lon", None)
    owned = P(("groups", "dp"), None)
    return jax.shard_map(
        body,
        mesh=mesh,
        in_specs=(field, field, P(), P(), P(), P(), P()),
        out_specs=(field, field, P("groups", "dp"), P(("groups", "dp")), owned, owned, owned),
        check_vma=False,
    )
```

```python
import functools
import math

import jax
import jax.numpy as jnp
from jax import lax
from jax.experimental import pallas as pl
from jax.experimental.pallas import tpu as pltpu
from jax.sharding import PartitionSpec as P

KS = 7
M = KS // 2
SUB = 8
LANE = 128
F32 = jnp.float32
BF16 = jnp.bfloat16


def kernel_call(fn, outs, args, scratch=(), flops=0, after=()):
    outs = [*outs, ((SUB, LANE), F32)]
    whole = pl.BlockSpec(memory_space=pltpu.VMEM)
    count = len(args)
    held = sum(math.prod(s) * jnp.dtype(d).itemsize for s, d in scratch)

    def run(*refs):
        last = count + len(after) + len(outs) - 1
        refs[last][...] = jnp.zeros((SUB, LANE), F32)
        fn(*refs[:count], *refs[count + len(after) : last], *refs[last + 1 :])

    return pl.pallas_call(
        run,
        out_shape=[jax.ShapeDtypeStruct(s, d) for s, d in outs],
        in_specs=[whole] * (count + len(after)),
        out_specs=[whole] * len(outs),
        scratch_shapes=[pltpu.VMEM(s, d) for s, d in scratch],
        compiler_params=pltpu.CompilerParams(vmem_limit_bytes=held + 8 * 2**20),
        cost_estimate=pl.CostEstimate(
            flops=flops, bytes_accessed=sum(a.size * a.dtype.itemsize for a in args), transcendentals=0
        ),
    )(*args, *after)


def rows(start, size):
    return pl.ds(start if isinstance(start, int) else pl.multiple_of(start, SUB), size)


def lanes_at(start, size):
    return pl.ds(pl.multiple_of(start, LANE), size)


def rows16(start, size):
    return pl.ds(start if isinstance(start, int) else pl.multiple_of(start, 2 * SUB), size)


def dot(a, b):
    return jnp.dot(a, b, preferred_element_type=F32)


def dot_nt(a, b):
    return lax.dot_general(a, b, (((1,), (1,)), ((), ())), preferred_element_type=F32)


def dot_tn(a, b):
    return lax.dot_general(a, b, (((0,), (0,)), ((), ())), preferred_element_type=F32)


class Sizes:
    def __init__(self, fine_field, w_merge, w_expand):
        self.samples, fine_rows, fine_cols, self.narrow = fine_field.shape
        self.lat_rows, self.cols = fine_rows // 2, fine_cols // 2
        self.channels, self.wide = w_merge.shape[1], w_expand.shape[1]
        self.blocks = SUB // self.samples
        self.block_rows = self.lat_rows // self.blocks
        self.col = self.block_rows * SUB
        self.pad_rows = self.block_rows + 2 * M
        self.pad_col = self.pad_rows * SUB
        self.cells = self.cols * self.col
        self.fine = 4 * self.cells
        self.fine_block = 2 * self.block_rows * fine_cols
        self.fine_stride = self.fine_block + SUB
        self.fine_cols = fine_cols
        self.halves = self.channels // LANE


def fine_stats(z, x):
    ones = jnp.full((z.narrow, z.narrow), 1.0 / z.narrow, BF16)
    centered = x.astype(F32) - dot(x, ones)
    inverse = lax.rsqrt(dot((centered * centered).astype(BF16), ones) + 1e-06)
    return centered * inverse, inverse


def fine_rows_of(z, j, i, p, q):
    return pl.ds((2 * i + p) * z.fine_cols + 2 * j + q, SUB, stride=z.fine_stride)


def edge_rows(z, scratch, edge_refs):
    sides = []
    for first_row, block in ((z.block_rows - M, z.blocks - 1), (0, 0)):
        parts = []
        for r in range(M):
            for s in range(z.samples):
                start = (first_row + r) * SUB + s * z.blocks + block
                parts.append(
                    jnp.concatenate(
                        [scratch[h, pl.ds(start, z.cols, stride=z.col), :] for h in range(z.halves)], axis=1
                    )
                )
        sides.append(jnp.concatenate(parts, axis=0))
    if len(edge_refs) == 1:
        edge_refs[0][...] = jnp.where(lax.axis_index("lat") == 0, sides[0], sides[1]).astype(BF16)
    else:
        for ref, side in zip(edge_refs, sides):
            ref[...] = side.astype(BF16)


def merge_kernel(z, fine_ref, w_ref, patches_ref, coarse_ref, inv_ref, *rest):
    *edge_refs, unit_s, split_s = rest
    for t in range(SUB):
        at = slice(t * z.fine_block, (t + 1) * z.fine_block)
        unit, inverse = fine_stats(z, fine_ref[at, :])
        unit_s[t * z.fine_stride : t * z.fine_stride + z.fine_block, :] = unit
        inv_ref[at, :] = inverse
    group = 4

    def step(g, _):
        for jj in range(group):
            j = g * group + jj
            quarters = []
            for p in range(2):
                for q in range(2):
                    quarters.append(
                        jnp.concatenate(
                            [unit_s[fine_rows_of(z, j, i, p, q), :] for i in range(z.block_rows)], axis=0
                        ).astype(BF16)
                    )
            patches_ref[rows16(j * z.col, z.col), :] = jnp.concatenate(quarters, axis=1)
        at = rows16(g * group * z.col, group * z.col)
        low = dot(patches_ref[at, :], w_ref[...]).astype(BF16)
        coarse_ref[at, :] = low
        for h in range(z.halves):
            split_s[h, at, :] = low[:, h * LANE : (h + 1) * LANE].astype(F32)
        return 0

    lax.fori_loop(0, z.cols // group, step, 0, unroll=True)
    edge_rows(z, split_s, edge_refs)


def weighted_kernel(z, lats, grad_ref, w_ref, out_ref, centered_ref, split_s):
    for t in range(4):
        at = slice(t * z.narrow, (t + 1) * z.narrow)
        w = w_ref[at, :].astype(F32)
        w = w - jnp.sum(w, axis=0, keepdims=True) * (1.0 / z.narrow)
        high = w.astype(BF16)
        centered_ref[at, 0 : z.channels] = high
        centered_ref[at, z.channels :] = (w - high.astype(F32)).astype(BF16)
    place = lax.broadcasted_iota(jnp.int32, (z.col, LANE), 0)
    row = lax.axis_index("lat") * z.lat_rows + (place % SUB) % z.blocks * z.block_rows + place // SUB
    cosine = jnp.cos(math.pi * ((row.astype(F32) + 0.5) / (z.lat_rows * lats) - 0.5))
    for h in range(z.halves):
        split_s[h, :, :] = grad_ref[:, h * LANE : (h + 1) * LANE].astype(F32)

    def step(j, _):
        for h in range(z.halves):
            col = jnp.concatenate(
                [
                    split_s[h, pl.ds(i * z.cols + j, SUB, stride=z.block_rows * z.cols), :]
                    for i in range(z.block_rows)
                ],
                axis=0,
            )
            out_ref[rows16(j * z.col, z.col), h * LANE : (h + 1) * LANE] = (col * cosine).astype(BF16)
        return 0

    lax.fori_loop(0, z.cols, step, 0, unroll=8)


def pad_column(z, own, line, ref, start):
    place = lax.broadcasted_iota(jnp.int32, (SUB, z.channels), 0)
    ref[rows(start + M * SUB, z.col), :] = own
    for r in range(M):
        i = z.block_rows - M + r
        top = pltpu.roll(own[i * SUB : (i + 1) * SUB], 1, 0)
        low = pltpu.roll(own[r * SUB : (r + 1) * SUB], SUB - 1, 0)
        for s in range(z.samples):
            top = jnp.where(place == s * z.blocks, line(0, r, s), top)
            low = jnp.where(place == (s + 1) * z.blocks - 1, line(1, r, s), low)
        ref[rows(start + r * SUB, SUB), :] = top
        ref[rows(start + (M + z.block_rows + r) * SUB, SUB), :] = low


def pad_kernel(z, lats, own_ref, before_ref, after_ref, pad_ref, left_ref, right_ref, halo_s, slab_s):
    lat = lax.axis_index("lat")
    near = z.samples * M * z.cols
    halo_s[0:near, :] = jnp.where(lat > 0, before_ref[...].astype(F32), 0.0)
    halo_s[near : 2 * near, :] = jnp.where(lat < lats - 1, after_ref[...].astype(F32), 0.0)

    def step(j, _):
        own = own_ref[rows16(j * z.col, z.col), :].astype(F32)
        line = lambda side, r, s: halo_s[pl.ds(side * near + (r * z.samples + s) * z.cols + j, 1), :]
        pad_column(z, own, line, pad_ref, j * z.pad_col)
        return 0

    lax.fori_loop(0, z.cols, step, 0, unroll=4)
    own = M * z.col
    slab_s[own:, :] = jnp.zeros_like(slab_s[own:, :])
    for ref, first in ((left_ref, 0), (right_ref, z.cols - M)):
        for t in range(2 * M * z.samples):
            slab_s[own + t * M : own + (t + 1) * M, :] = halo_s[t * z.cols + first : t * z.cols + first + M, :]
        ref[0:own, :] = own_ref[first * z.col : (first + M) * z.col, :]
        ref[own:, :] = slab_s[own:, :].astype(BF16)


def unpack_slab(z, slab_ref, slab_s, ref, start):
    slab_s[...] = slab_ref[...].astype(F32)
    for c in range(M):
        line = lambda side, r, s: slab_s[pl.ds(M * z.col + ((side * M + r) * z.samples + s) * M + c, 1), :]
        pad_column(z, slab_s[c * z.col : (c + 1) * z.col, :], line, ref, start + c * z.pad_col)


def taps(z, pad, taps_s, start, h, flipped):
    lanes = slice(h * LANE, (h + 1) * LANE)
    total = jnp.zeros((z.block_rows, SUB, LANE), F32)
    for e in range(KS):
        column = pad[rows((start + e) * z.pad_col, z.pad_col), lanes].reshape(z.pad_rows, SUB, LANE)
        for a in range(KS):
            t = a * KS + e
            t = KS * KS - 1 - t if flipped else t
            total = total + column[a : a + z.block_rows] * taps_s[t * SUB : (t + 1) * SUB, lanes]
    return total.reshape(z.col, LANE)


def spread_taps(z, kern_ref, taps_s):
    for t in range(KS * KS):
        taps_s[t * SUB : (t + 1) * SUB, :] = jnp.broadcast_to(kern_ref[t : t + 1, :], (SUB, z.channels))


def gelu_parts(x):
    return 0.5 + 0.5 * lax.erf(x * 0.7071067811865476), x * jnp.exp(-0.5 * x * x) * 0.3989422804014327


def row_mean(z, x):
    return jnp.sum(x, axis=-1, keepdims=True) * (1.0 / z.channels)


def section(z, pad, sources, groups, refs, scratch, chunk, section_ref, mixed_ref, taps_s):
    gain_ref, we_ref, wc_ref, coarse_ref, weighted_ref = refs
    unit_s, inv_s, normed_s, hidden_s, slope_s, weighted_s = scratch
    count = sum(g[2] for g in groups)

    def step(j, _):
        parts = [taps(z, pad, taps_s, sources(j), h, False) for h in range(z.halves)]
        at = rows16(j * z.col, z.col)
        mean = sum(jnp.sum(p, axis=-1, keepdims=True) for p in parts) * (1.0 / z.channels)
        parts = [p - mean for p in parts]
        var = sum(jnp.sum(p * p, axis=-1, keepdims=True) for p in parts) * (1.0 / z.channels)
        inverse = lax.rsqrt(var + 1e-06)
        inv_s[at, :] = jnp.broadcast_to(inverse, (z.col, LANE))
        for h, p in enumerate(parts):
            lanes = slice(h * LANE, (h + 1) * LANE)
            unit = p * inverse
            unit_s[at, lanes] = unit
            normed_s[at, lanes] = (unit * gain_ref[:, lanes]).astype(BF16)
        return 0

    lax.fori_loop(0, count // z.col, step, 0, unroll=count // z.col // 2)
    for low, full, size in groups:
        weighted_s[low : low + size, :] = weighted_ref[full : full + size, :]
    gain_sum = jnp.zeros((SUB, z.channels), F32)
    for low, full, size in groups:
        for c in range(size // chunk):
            at = slice(low + c * chunk, low + (c + 1) * chunk)
            place = slice(full + c * chunk, full + (c + 1) * chunk)
            part = 256
            for f in range(z.wide // part):
                cut = slice(f * part, (f + 1) * part)
                pre = dot(normed_s[at, :], we_ref[:, cut])
                back = dot_nt(weighted_s[at, :], wc_ref[cut, :])
                phi, density = gelu_parts(pre)
                hidden_s[at, cut] = (pre * phi).astype(BF16)
                slope_s[at, cut] = (back * (phi + density)).astype(BF16)
            branch = dot(hidden_s[at, :], wc_ref[...])
            section_ref[at, :] = (coarse_ref[place, :].astype(F32) + branch).astype(BF16)
            back = dot_nt(slope_s[at, :], we_ref[...])
            unit = unit_s[at, :]
            gain_sum = gain_sum + jnp.sum((back * unit).reshape(-1, SUB, z.channels), axis=0)
            back = back * gain_ref[...]
            inverse = jnp.concatenate([inv_s[at, :]] * z.halves, axis=1)
            mixed_ref[at, :] = inverse * (back - row_mean(z, back) - unit * row_mean(z, back * unit))
    return gain_sum


def inner_kernel(
    z, pad_ref, kern_ref, gain_ref, we_ref, wc_ref, coarse_ref, weighted_ref,
    section_ref, mixed_ref, expand_ref, contract_ref, gain_sum_ref, taps_s, *scratch,
):
    spread_taps(z, kern_ref, taps_s)
    size = (z.cols - 2 * M) * z.col
    refs = (gain_ref, we_ref, wc_ref, coarse_ref, weighted_ref)
    gain_sum_ref[...] = section(
        z, pad_ref, lambda j: j, [(0, M * z.col, size)], refs, scratch, size, section_ref, mixed_ref, taps_s
    )
    unit_s, inv_s, normed_s, hidden_s, slope_s, weighted_s = scratch
    expand_ref[...] = dot_tn(normed_s[...], slope_s[...])
    contract_ref[...] = dot_tn(weighted_s[...], hidden_s[...])


def outer_kernel(
    z, pad_ref, left_ref, right_ref, kern_ref, gain_ref, we_ref, wc_ref, coarse_ref, weighted_ref,
    expand_ref, contract_ref, gain_sum_ref, inner_mixed_ref,
    section_ref, mixed_ref, mine_ref, other_ref, low_ref, gain_out_ref, left_out_ref, right_out_ref, *rest,
):
    *edge_refs, taps_s, edge_s, split_s, slab_s = rest[:-6]
    scratch = rest[-6:]
    spread_taps(z, kern_ref, taps_s)
    edge_columns(z, left_ref, pad_ref, right_ref, edge_s, slab_s)
    left_out_ref[...] = edge_s[0 : M * z.pad_col, :]
    right_out_ref[...] = edge_s[5 * M * z.pad_col :, :]
    size = M * z.col
    refs = (gain_ref, we_ref, wc_ref, coarse_ref, weighted_ref)
    groups = [(0, 0, size), (size, z.cells - size, size)]
    gain_sum = section(
        z, edge_s, lambda j: jnp.where(j < M, j, j + 2 * M), groups, refs, scratch, size, section_ref, mixed_ref, taps_s
    )
    unit_s, inv_s, normed_s, hidden_s, slope_s, weighted_s = scratch
    gain_out_ref[...] = gain_sum + gain_sum_ref[...]
    half, cut = z.channels // 2, z.wide // 2
    first = lax.axis_index("dp") == 0
    total = (expand_ref[...] + dot_tn(normed_s[...], slope_s[...])).astype(BF16)
    mine_ref[0:half, :] = jnp.where(first, total[:half], total[half:])
    other_ref[0:half, :] = jnp.where(first, total[half:], total[:half])
    total = (contract_ref[...] + dot_tn(weighted_s[...], hidden_s[...])).astype(BF16)
    for t in range(2):
        low, high = total[t * half : (t + 1) * half, :cut], total[t * half : (t + 1) * half, cut:]
        mine_ref[half:, t * cut : (t + 1) * cut] = jnp.where(first, low, high)
        other_ref[half:, t * cut : (t + 1) * cut] = jnp.where(first, high, low)
    low_ref[0:size, :] = mixed_ref[0:size, :].astype(BF16)
    low_ref[size : z.cells - size, :] = inner_mixed_ref[...].astype(BF16)
    low_ref[z.cells - size :, :] = mixed_ref[size:, :].astype(BF16)
    for h in range(z.halves):
        split_s[h, :, :] = low_ref[:, h * LANE : (h + 1) * LANE].astype(F32)
    edge_rows(z, split_s, edge_refs)


def terms_kernel(z, h, pad_ref, left_ref, right_ref, inner_ref, outer_ref, gain_ref, out_ref, full_s, mixed_s):
    edge, size = M * z.pad_col, M * z.col
    lanes = slice(h * LANE, (h + 1) * LANE)
    full_s[0:edge, :] = left_ref[:, lanes]
    full_s[edge : edge + z.cols * z.pad_col, :] = pad_ref[:, lanes]
    full_s[edge + z.cols * z.pad_col :, :] = right_ref[:, lanes]
    mixed_s[0:size, :] = outer_ref[0:size, lanes]
    mixed_s[size : z.cells - size, :] = inner_ref[:, lanes]
    mixed_s[z.cells - size :, :] = outer_ref[size:, lanes]
    out_ref[...] = jnp.zeros_like(out_ref)
    for e in range(KS):

        def step(j, sums):
            column = full_s[rows((j + e) * z.pad_col, z.pad_col), :].reshape(z.pad_rows, SUB, LANE)
            back = mixed_s[rows(j * z.col, z.col), :].reshape(z.block_rows, SUB, LANE)
            return tuple(sums[a] + jnp.sum(column[a : a + z.block_rows] * back, axis=0) for a in range(KS))

        zeros = tuple(jnp.zeros((SUB, LANE), F32) for _ in range(KS))
        sums = lax.fori_loop(0, z.cols, step, zeros, unroll=4)
        for a in range(KS):
            t = a * KS + e
            out_ref[t : t + 1, :] = jnp.sum(sums[a], axis=0, keepdims=True)
    out_ref[KS * KS : KS * KS + 1, :] = jnp.sum(gain_ref[:, lanes], axis=0, keepdims=True)


def spread(z, pad, taps_s, source, at, low, weighted_ref, out_ref):
    for h in range(z.halves):
        lanes = slice(h * LANE, (h + 1) * LANE)
        total = taps(z, pad, taps_s, source, h, True)
        out_ref[low, lanes] = (weighted_ref[at, lanes].astype(F32) + total).astype(BF16)


def back_inner_kernel(z, pad_ref, kern_ref, weighted_ref, coarse_ref, taps_s):
    spread_taps(z, kern_ref, taps_s)

    def step(j, _):
        spread(
            z, pad_ref, taps_s, j, rows16((j + M) * z.col, z.col), rows16(j * z.col, z.col), weighted_ref, coarse_ref
        )
        return 0

    lax.fori_loop(0, z.cols - 2 * M, step, 0, unroll=5)


def edge_columns(z, left_ref, pad_ref, right_ref, edge_s, slab_s):
    edge, near = M * z.pad_col, 2 * M * z.pad_col
    unpack_slab(z, left_ref, slab_s, edge_s, 0)
    edge_s[edge : edge + near, :] = pad_ref[0:near, :]
    edge_s[edge + near : edge + 2 * near, :] = pad_ref[z.cols * z.pad_col - near :, :]
    unpack_slab(z, right_ref, slab_s, edge_s, edge + 2 * near)


def back_outer_kernel(
    z, pad_ref, left_ref, right_ref, kern_ref, weighted_ref, patches_ref, inner_ref, low_aux_ref, high_aux_ref,
    coarse_ref, mine_ref, other_ref, taps_s, edge_s, sum_s, slab_s,
):
    spread_taps(z, kern_ref, taps_s)
    edge_columns(z, left_ref, pad_ref, right_ref, edge_s, slab_s)

    def step(j, _):
        for first, source in ((0, 0), (z.cols - M, 3 * M)):
            at = rows16((first + j) * z.col, z.col)
            spread(z, edge_s, taps_s, source + j, at, at, weighted_ref, coarse_ref)
        return 0

    lax.fori_loop(0, M, step, 0, unroll=True)
    size = M * z.col
    coarse_ref[size : z.cells - size, :] = inner_ref[...]
    sum_s[...] = dot_tn(coarse_ref[...], patches_ref[...])
    own, cut = lax.axis_index("dp"), 2 * z.narrow
    depth, half = low_aux_ref.shape[0] // 2, z.channels // 2
    for ref, owner in ((mine_ref, own), (other_ref, 1 - own)):
        ref[0 : z.channels, :] = sum_s[:, lanes_at(owner * cut, cut)].astype(BF16)
        for t in range(2):
            at = slice(t * depth, (t + 1) * depth)
            aux = jnp.where(owner == 0, low_aux_ref[at, :], high_aux_ref[at, :])
            ref[z.channels :, t * half : (t + 1) * half] = aux.astype(BF16)


def unfold_kernel(z, coarse_ref, centered_ref, patches_ref, back_ref):
    group = 4
    ones = jnp.full((z.narrow, z.narrow), 1.0 / z.narrow, BF16)

    def step(g, _):
        at = rows16(g * group * z.col, group * z.col)
        low = coarse_ref[at, :]
        back = dot_nt(jnp.concatenate([low, low], axis=1), centered_ref[...])
        for p in range(2):
            for q in range(2):
                lanes = slice((p * 2 + q) * z.narrow, (p * 2 + q + 1) * z.narrow)
                unit = patches_ref[at, lanes].astype(F32)
                up = back[:, lanes]
                up = up - unit * dot((up * unit).astype(BF16), ones)
                for jj in range(group):
                    for i in range(z.block_rows):
                        first = jj * z.col + i * SUB
                        back_ref[fine_rows_of(z, g * group + jj, i, p, q), :] = up[first : first + SUB]
        return 0

    lax.fori_loop(0, z.cols // group, step, 0, unroll=True)


def fine_kernel(z, back_ref, inv_ref, out_ref):
    def step(t, _):
        at = rows16(t * z.fine_block, z.fine_block)
        out_ref[at, :] = (inv_ref[at, :] * back_ref[rows(t * z.fine_stride, z.fine_block), :]).astype(BF16)
        return 0

    lax.fori_loop(0, SUB, step, 0, unroll=2)


def second(axis, distance):
    return lax.axis_index(axis) // distance % 2


def add_kernel(step, mine_ref, got_ref, *out_refs):
    if step is None:
        out_refs[0][...] = (mine_ref[...].astype(F32) + got_ref[...].astype(F32)).astype(BF16)
        return
    half, side = mine_ref.shape[0] // 2, second(*step)
    for ref, which in zip(out_refs, (side, 1 - side)):
        at = rows16(which * half, half)
        ref[...] = (mine_ref[at, :].astype(F32) + got_ref[at, :].astype(F32)).astype(BF16)


def join_kernel(step, mine_ref, got_ref, out_ref):
    half, side = mine_ref.shape[0], second(*step)
    out_ref[rows16(side * half, half), :] = mine_ref[...]
    out_ref[rows16((1 - side) * half, half), :] = got_ref[...]


def section_kernel(z, inner_ref, outer_ref, out_ref, all_s, split_s):
    size = M * z.col
    all_s[0:size, :] = outer_ref[0:size, :].astype(F32)
    all_s[size : z.cells - size, :] = inner_ref[...].astype(F32)
    all_s[z.cells - size :, :] = outer_ref[size:, :].astype(F32)

    def step(j, _):
        for h in range(z.halves):
            for i in range(z.block_rows):
                split_s[h, pl.ds(i * z.cols + j, SUB, stride=z.block_rows * z.cols), :] = all_s[
                    rows(j * z.col + i * SUB, SUB), h * LANE : (h + 1) * LANE
                ]
        return 0

    lax.fori_loop(0, z.cols, step, 0, unroll=8)
    for h in range(z.halves):
        out_ref[:, h * LANE : (h + 1) * LANE] = split_s[h, :, :].astype(BF16)


def final_wide_kernel(z, factor, step, mine_ref, got_ref, expand_ref, contract_ref, sum_ref):
    join_kernel(step, mine_ref, got_ref, sum_ref)
    half, cut = z.channels // 2, z.wide // 2
    expand_ref[...] = sum_ref[0:half, :].astype(F32) * factor
    for t in range(2):
        part = sum_ref[half:, t * cut : (t + 1) * cut].astype(F32) * factor
        contract_ref[:, t * half : (t + 1) * half] = part.T


def final_small_kernel(z, factor, mine_ref, got_ref, merge_ref, kernel_ref, gain_ref):
    total = (mine_ref[...].astype(F32) + got_ref[...].astype(F32)) * factor
    merge_ref[...] = total[0 : z.channels].T
    half = z.channels // 2
    tail = total[z.channels :]
    depth = tail.shape[0]
    kernel_ref[0:depth, :] = tail[:, :half]
    kernel_ref[depth:, :] = tail[: KS * KS - depth, half:]
    gain_ref[...] = tail[KS * KS - depth : KS * KS - depth + 1, half:]


def swap(x, axis, distance):
    size = lax.axis_size(axis)
    return lax.ppermute(x, axis, [(i, i ^ distance) for i in range(size)])


def add(mine, got, after=(), halve=None):
    count, width = mine.shape
    outs = [((count, width), BF16)] if halve is None else [((count // 2, width), BF16)] * 2
    return kernel_call(functools.partial(add_kernel, halve), outs, (mine, got), after=after)


def join(x, step, after):
    outs = [((2 * x.shape[0], x.shape[1]), BF16)]
    return kernel_call(functools.partial(join_kernel, step), outs, (x, swap(x, *step)), after=after)


def sum_steps(count):
    steps = []
    for axis in ("lat", "lon"):
        distance = 1
        while distance < lax.axis_size(axis):
            steps.append((axis, distance))
            distance *= 2
    halvings = 0
    while halvings < len(steps) - 1 and count >> (halvings + 1) >= 2 * SUB:
        halvings += 1
    return steps, halvings


def lat_margins(last, first=None):
    if first is None:
        got = swap(last, "lat", 1)
        return got, got
    up = [(i, i + 1) for i in range(lax.axis_size("lat") - 1)]
    return lax.ppermute(last, "lat", up), lax.ppermute(first, "lat", [(j, i) for i, j in up])


def lon_margins(left, right):
    size = lax.axis_size("lon")
    up = [(i, (i + 1) % size) for i in range(size)]
    return lax.ppermute(right, "lon", up), lax.ppermute(left, "lon", [(j, i) for i, j in up])


def body(fine_field, grad_out, conv_kernel, norm_gain, w_expand, w_contract, w_merge):
    z = Sizes(fine_field, w_merge, w_expand)
    ch, ff, lats = z.channels, z.wide, lax.axis_size("lat")
    fine = fine_field.reshape(z.fine, z.narrow)
    gain = norm_gain.reshape(1, ch)

    part = functools.partial
    split = ((z.halves, z.cells, LANE), F32)
    edges = [((z.samples * M * z.cols, ch), BF16)] * (1 if lats == 2 else 2)
    patches, coarse, fine_inv, *send, _ = kernel_call(
        part(merge_kernel, z),
        [((z.cells, 4 * z.narrow), BF16), ((z.cells, ch), BF16), ((z.fine, z.narrow), F32), *edges],
        (fine, w_merge),
        [((SUB * z.fine_stride, z.narrow), F32), split],
    )
    before, after = lat_margins(*send)
    weighted, w_centered, _ = kernel_call(
        part(weighted_kernel, z, lats),
        [((z.cells, ch), BF16), ((4 * z.narrow, 2 * ch), BF16)],
        (grad_out.reshape(z.cells, ch), w_merge),
        [split],
        flops=2_000_000_000,
    )
    slab_rows = -(-(M * z.col + 2 * M * z.samples * M) // (2 * SUB)) * 2 * SUB
    slab, slab_s = ((slab_rows, ch), BF16), ((slab_rows, ch), F32)
    padded = ((z.cols * z.pad_col, ch), F32)
    pad_scratch = [((2 * z.samples * M * z.cols, ch), F32), slab_s]
    pad, left, right, _ = kernel_call(part(pad_kernel, z, lats), [padded, slab, slab], (coarse, before, after), pad_scratch)
    left, right = lon_margins(left, right)

    taps_s = ((KS * KS * SUB, ch), F32)

    def section_scratch(count):
        return [
            ((count, ch), F32),
            ((count, LANE), F32),
            ((count, ch), BF16),
            ((count, ff), BF16),
            ((count, ff), BF16),
            ((count, ch), BF16),
        ]

    outer = 2 * M * z.col
    inner = z.cells - outer
    section_in, mixed_in, expand, contract, gain_sum, _ = kernel_call(
        part(inner_kernel, z),
        [((inner, ch), BF16), ((inner, ch), F32), ((ch, ff), F32), ((ch, ff), F32), ((SUB, ch), F32)],
        (pad, conv_kernel, gain, w_expand, w_contract, coarse, weighted),
        [taps_s] + section_scratch(inner),
        flops=8_000_000_000,
    )
    section_out, mixed_out, mine, other, low, gain_sum, left, right, *send, _ = kernel_call(
        part(outer_kernel, z),
        [
            ((outer, ch), BF16),
            ((outer, ch), F32),
            ((ch, ff), BF16),
            ((ch, ff), BF16),
            ((z.cells, ch), BF16),
            ((SUB, ch), F32),
            ((M * z.pad_col, ch), F32),
            ((M * z.pad_col, ch), F32),
            *edges,
        ],
        (pad, left, right, conv_kernel, gain, w_expand, w_contract, coarse, weighted)
        + (expand, contract, gain_sum, mixed_in),
        [taps_s, ((6 * M * z.pad_col, ch), F32), split, slab_s] + section_scratch(outer),
        flops=8_000_000_000,
    )
    before, after = lat_margins(*send)
    steps, halvings = sum_steps(ch)
    wide, away, token = add(mine, swap(other, "dp", 1), halve=steps[0])
    pad_low, edge_left, edge_right, token = kernel_call(
        part(pad_kernel, z, lats), [padded, slab, slab], (low, before, after), pad_scratch, after=(token,)
    )
    left_low, right_low = lon_margins(edge_left, edge_right)
    bf = lambda count, width: ((count, width), BF16)

    def terms(h, token):
        return kernel_call(
            part(terms_kernel, z, h),
            [((64, LANE), F32)],
            (pad, left, right, mixed_in, mixed_out, gain_sum),
            [(((z.cols + 2 * M) * z.pad_col, LANE), F32), ((z.cells, LANE), F32)],
            3_000_000_000,
            (token,),
        )

    low_aux, token = terms(0, token)
    wide, away, token = add(wide, swap(away, *steps[0]), after=(token,), halve=steps[1])
    high_aux, token = terms(1, token)
    back_inner, token = kernel_call(
        part(back_inner_kernel, z), [bf(inner, ch)], (pad_low, conv_kernel, weighted), [taps_s], 500_000_000, (token,)
    )
    for n in range(1, halvings - 1):
        wide, away, token = add(wide, swap(away, *steps[n]), after=(token,), halve=steps[n + 1])
    wide, token = add(wide, swap(away, *steps[halvings - 1]), after=(token,))
    back_coarse, mine, other, token = kernel_call(
        part(back_outer_kernel, z),
        [bf(z.cells, ch), bf(ch + 32, 2 * z.narrow), bf(ch + 32, 2 * z.narrow)],
        (pad_low, left_low, right_low, conv_kernel, weighted, patches, back_inner, low_aux, high_aux),
        [taps_s, ((6 * M * z.pad_col, ch), F32), ((ch, 4 * z.narrow), F32), slab_s],
        4_000_000_000,
        (token,),
    )
    back_fine, token = kernel_call(
        part(unfold_kernel, z),
        [((SUB * z.fine_stride, z.narrow), F32)],
        (back_coarse, w_centered, patches),
        (),
        3_000_000_000,
        (token,),
    )
    small, token = add(mine, swap(other, "dp", 1), after=(token,))
    grad_fine, token = kernel_call(
        part(fine_kernel, z), [bf(z.fine, z.narrow)], (back_fine, fine_inv), (), 2_000_000_000, (token,)
    )
    for step in steps[halvings:]:
        wide, token = add(wide, swap(wide, *step), after=(token,))
    small, token = add(small, swap(small, *steps[0]), after=(token,))
    section_all, token = kernel_call(
        part(section_kernel, z),
        [bf(z.cells, ch)],
        (section_in, section_out),
        [((z.cells, ch), F32), split],
        2_000_000_000,
        (token,),
    )
    for step in reversed(steps[1:halvings]):
        wide, token = join(wide, step, (token,))
    for step in steps[1:-1]:
        small, token = add(small, swap(small, *step), after=(token,))
    small_got = swap(small, *steps[-1])
    all_cells = z.samples * lax.axis_size("dp") * z.lat_rows * lats * z.cols * lax.axis_size("lon")
    factor = 1.0 / math.sqrt(all_cells)
    grad_expand, grad_contract, token = kernel_call(
        part(final_wide_kernel, z, factor, steps[0]),
        [((ch // 2, ff), F32), ((ff // 2, ch), F32)],
        (wide, swap(wide, *steps[0])),
        [((ch, ff), BF16)],
        after=(token,),
    )
    grad_merge, grad_kernel, grad_gain, _ = kernel_call(
        part(final_small_kernel, z, factor),
        [((2 * z.narrow, ch), F32), ((KS * KS, ch // 2), F32), ((1, ch // 2), F32)],
        (small, small_got),
        after=(token,),
    )
    return (
        section_all.reshape(z.samples, z.lat_rows, z.cols, ch),
        grad_fine.reshape(fine_field.shape),
        grad_kernel,
        grad_gain.reshape(ch // 2),
        grad_expand,
        grad_contract,
        grad_merge,
    )


def solution(mesh):
    field = P(("groups", "dp"), "lat", "lon", None)
    owned = P(("groups", "dp"), None)
    return jax.shard_map(
        body,
        mesh=mesh,
        in_specs=(field, field, P(), P(), P(), P(), P()),
        out_specs=(field, field, P("groups", "dp"), P(("groups", "dp")), owned, owned, owned),
        check_vma=False,
    )
```

```python
import functools
import math

import jax
import jax.numpy as jnp
from jax import lax
from jax.experimental import pallas as pl
from jax.experimental.pallas import tpu as pltpu
from jax.sharding import PartitionSpec as P

KS = 7
M = KS // 2
SUB = 8
LANE = 128
F32 = jnp.float32
BF16 = jnp.bfloat16


def kernel_call(fn, outs, args, scratch=(), flops=0, after=()):
    outs = [*outs, ((SUB, LANE), F32)]
    whole = pl.BlockSpec(memory_space=pltpu.VMEM)
    count = len(args)
    held = sum(math.prod(s) * jnp.dtype(d).itemsize for s, d in scratch)

    def run(*refs):
        last = count + len(after) + len(outs) - 1
        refs[last][...] = jnp.zeros((SUB, LANE), F32)
        fn(*refs[:count], *refs[count + len(after) : last], *refs[last + 1 :])

    return pl.pallas_call(
        run,
        out_shape=[jax.ShapeDtypeStruct(s, d) for s, d in outs],
        in_specs=[whole] * (count + len(after)),
        out_specs=[whole] * len(outs),
        scratch_shapes=[pltpu.VMEM(s, d) for s, d in scratch],
        compiler_params=pltpu.CompilerParams(vmem_limit_bytes=held + 8 * 2**20),
        cost_estimate=pl.CostEstimate(
            flops=flops, bytes_accessed=sum(a.size * a.dtype.itemsize for a in args), transcendentals=0
        ),
    )(*args, *after)


def rows(start, size):
    return pl.ds(start if isinstance(start, int) else pl.multiple_of(start, SUB), size)


def lanes_at(start, size):
    return pl.ds(pl.multiple_of(start, LANE), size)


def rows16(start, size):
    return pl.ds(start if isinstance(start, int) else pl.multiple_of(start, 2 * SUB), size)


def dot(a, b):
    return jnp.dot(a, b, preferred_element_type=F32)


def dot_nt(a, b):
    return lax.dot_general(a, b, (((1,), (1,)), ((), ())), preferred_element_type=F32)


def dot_tn(a, b):
    return lax.dot_general(a, b, (((0,), (0,)), ((), ())), preferred_element_type=F32)


class Sizes:
    def __init__(self, fine_field, w_merge, w_expand):
        self.samples, fine_rows, fine_cols, self.narrow = fine_field.shape
        self.lat_rows, self.cols = fine_rows // 2, fine_cols // 2
        self.channels, self.wide = w_merge.shape[1], w_expand.shape[1]
        self.blocks = SUB // self.samples
        self.block_rows = self.lat_rows // self.blocks
        self.col = self.block_rows * SUB
        self.pad_rows = self.block_rows + 2 * M
        self.pad_col = self.pad_rows * SUB
        self.cells = self.cols * self.col
        self.fine = 4 * self.cells
        self.fine_block = 2 * self.block_rows * fine_cols
        self.fine_stride = self.fine_block + SUB
        self.fine_cols = fine_cols
        self.halves = self.channels // LANE


def fine_stats(z, x):
    ones = jnp.full((z.narrow, z.narrow), 1.0 / z.narrow, BF16)
    centered = x.astype(F32) - dot(x, ones)
    inverse = lax.rsqrt(dot((centered * centered).astype(BF16), ones) + 1e-06)
    return centered * inverse, inverse


def fine_rows_of(z, j, i, p, q):
    return pl.ds((2 * i + p) * z.fine_cols + 2 * j + q, SUB, stride=z.fine_stride)


def edge_rows(z, scratch, edge_refs):
    sides = []
    for first_row, block in ((z.block_rows - M, z.blocks - 1), (0, 0)):
        parts = []
        for r in range(M):
            for s in range(z.samples):
                start = (first_row + r) * SUB + s * z.blocks + block
                parts.append(
                    jnp.concatenate(
                        [scratch[h, pl.ds(start, z.cols, stride=z.col), :] for h in range(z.halves)], axis=1
                    )
                )
        sides.append(jnp.concatenate(parts, axis=0))
    if len(edge_refs) == 1:
        edge_refs[0][...] = jnp.where(lax.axis_index("lat") == 0, sides[0], sides[1]).astype(BF16)
    else:
        for ref, side in zip(edge_refs, sides):
            ref[...] = side.astype(BF16)


def merge_kernel(z, fine_ref, w_ref, patches_ref, coarse_ref, inv_ref, *rest):
    *edge_refs, unit_s, split_s = rest
    for t in range(SUB):
        at = slice(t * z.fine_block, (t + 1) * z.fine_block)
        unit, inverse = fine_stats(z, fine_ref[at, :])
        unit_s[t * z.fine_stride : t * z.fine_stride + z.fine_block, :] = unit
        inv_ref[at, :] = inverse
    group = 4

    def step(g, _):
        for jj in range(group):
            j = g * group + jj
            quarters = []
            for p in range(2):
                for q in range(2):
                    quarters.append(
                        jnp.concatenate(
                            [unit_s[fine_rows_of(z, j, i, p, q), :] for i in range(z.block_rows)], axis=0
                        ).astype(BF16)
                    )
            patches_ref[rows16(j * z.col, z.col), :] = jnp.concatenate(quarters, axis=1)
        at = rows16(g * group * z.col, group * z.col)
        low = dot(patches_ref[at, :], w_ref[...]).astype(BF16)
        coarse_ref[at, :] = low
        for h in range(z.halves):
            split_s[h, at, :] = low[:, h * LANE : (h + 1) * LANE].astype(F32)
        return 0

    lax.fori_loop(0, z.cols // group, step, 0, unroll=True)
    edge_rows(z, split_s, edge_refs)


def weighted_kernel(z, lats, grad_ref, w_ref, out_ref, centered_ref, split_s):
    for t in range(4):
        at = slice(t * z.narrow, (t + 1) * z.narrow)
        w = w_ref[at, :].astype(F32)
        w = w - jnp.sum(w, axis=0, keepdims=True) * (1.0 / z.narrow)
        high = w.astype(BF16)
        centered_ref[at, 0 : z.channels] = high
        centered_ref[at, z.channels :] = (w - high.astype(F32)).astype(BF16)
    place = lax.broadcasted_iota(jnp.int32, (z.col, LANE), 0)
    row = lax.axis_index("lat") * z.lat_rows + (place % SUB) % z.blocks * z.block_rows + place // SUB
    cosine = jnp.cos(math.pi * ((row.astype(F32) + 0.5) / (z.lat_rows * lats) - 0.5))
    for h in range(z.halves):
        split_s[h, :, :] = grad_ref[:, h * LANE : (h + 1) * LANE].astype(F32)

    def step(j, _):
        for h in range(z.halves):
            col = jnp.concatenate(
                [
                    split_s[h, pl.ds(i * z.cols + j, SUB, stride=z.block_rows * z.cols), :]
                    for i in range(z.block_rows)
                ],
                axis=0,
            )
            out_ref[rows16(j * z.col, z.col), h * LANE : (h + 1) * LANE] = (col * cosine).astype(BF16)
        return 0

    lax.fori_loop(0, z.cols, step, 0, unroll=8)


def pad_column(z, own, line, ref, start):
    place = lax.broadcasted_iota(jnp.int32, (SUB, z.channels), 0)
    ref[rows(start + M * SUB, z.col), :] = own
    for r in range(M):
        i = z.block_rows - M + r
        top = pltpu.roll(own[i * SUB : (i + 1) * SUB], 1, 0)
        low = pltpu.roll(own[r * SUB : (r + 1) * SUB], SUB - 1, 0)
        for s in range(z.samples):
            top = jnp.where(place == s * z.blocks, line(0, r, s), top)
            low = jnp.where(place == (s + 1) * z.blocks - 1, line(1, r, s), low)
        ref[rows(start + r * SUB, SUB), :] = top
        ref[rows(start + (M + z.block_rows + r) * SUB, SUB), :] = low


def pad_kernel(z, lats, own_ref, before_ref, after_ref, pad_ref, left_ref, right_ref, halo_s, slab_s):
    lat = lax.axis_index("lat")
    near = z.samples * M * z.cols
    halo_s[0:near, :] = jnp.where(lat > 0, before_ref[...].astype(F32), 0.0)
    halo_s[near : 2 * near, :] = jnp.where(lat < lats - 1, after_ref[...].astype(F32), 0.0)

    def step(j, _):
        own = own_ref[rows16(j * z.col, z.col), :].astype(F32)
        line = lambda side, r, s: halo_s[pl.ds(side * near + (r * z.samples + s) * z.cols + j, 1), :]
        pad_column(z, own, line, pad_ref, j * z.pad_col)
        return 0

    lax.fori_loop(0, z.cols, step, 0, unroll=4)
    own = M * z.col
    slab_s[own:, :] = jnp.zeros_like(slab_s[own:, :])
    sides = []
    for first in (0, z.cols - M):
        for t in range(2 * M * z.samples):
            slab_s[own + t * M : own + (t + 1) * M, :] = halo_s[t * z.cols + first : t * z.cols + first + M, :]
        lines = slab_s[own:, :].astype(BF16)
        sides.append(jnp.concatenate([own_ref[first * z.col : (first + M) * z.col, :], lines], axis=0))
    even = lax.axis_index("lon") % 2 == 0
    left_ref[...] = jnp.where(even, sides[1], sides[0])
    right_ref[...] = jnp.where(even, sides[0], sides[1])


def unpack_slab(z, slab, slab_s, ref, start):
    slab_s[...] = slab.astype(F32)
    for c in range(M):
        line = lambda side, r, s: slab_s[pl.ds(M * z.col + ((side * M + r) * z.samples + s) * M + c, 1), :]
        pad_column(z, slab_s[c * z.col : (c + 1) * z.col, :], line, ref, start + c * z.pad_col)


def taps(z, pad, taps_s, start, h, flipped):
    lanes = slice(h * LANE, (h + 1) * LANE)
    total = jnp.zeros((z.block_rows, SUB, LANE), F32)
    for e in range(KS):
        column = pad[rows((start + e) * z.pad_col, z.pad_col), lanes].reshape(z.pad_rows, SUB, LANE)
        for a in range(KS):
            t = a * KS + e
            t = KS * KS - 1 - t if flipped else t
            total = total + column[a : a + z.block_rows] * taps_s[t * SUB : (t + 1) * SUB, lanes]
    return total.reshape(z.col, LANE)


def spread_taps(z, kern_ref, taps_s):
    for t in range(KS * KS):
        taps_s[t * SUB : (t + 1) * SUB, :] = jnp.broadcast_to(kern_ref[t : t + 1, :], (SUB, z.channels))


def gelu_parts(x):
    return 0.5 + 0.5 * lax.erf(x * 0.7071067811865476), x * jnp.exp(-0.5 * x * x) * 0.3989422804014327


def row_mean(z, x):
    return jnp.sum(x, axis=-1, keepdims=True) * (1.0 / z.channels)


def section(z, pad, sources, groups, refs, scratch, chunk, section_ref, mixed_ref, taps_s):
    gain_ref, we_ref, wc_ref, coarse_ref, weighted_ref = refs
    unit_s, inv_s, normed_s, hidden_s, slope_s, weighted_s = scratch
    count = sum(g[2] for g in groups)

    def step(j, _):
        parts = [taps(z, pad, taps_s, sources(j), h, False) for h in range(z.halves)]
        at = rows16(j * z.col, z.col)
        mean = sum(jnp.sum(p, axis=-1, keepdims=True) for p in parts) * (1.0 / z.channels)
        parts = [p - mean for p in parts]
        var = sum(jnp.sum(p * p, axis=-1, keepdims=True) for p in parts) * (1.0 / z.channels)
        inverse = lax.rsqrt(var + 1e-06)
        inv_s[at, :] = jnp.broadcast_to(inverse, (z.col, LANE))
        for h, p in enumerate(parts):
            lanes = slice(h * LANE, (h + 1) * LANE)
            unit = p * inverse
            unit_s[at, lanes] = unit
            normed_s[at, lanes] = (unit * gain_ref[:, lanes]).astype(BF16)
        return 0

    lax.fori_loop(0, count // z.col, step, 0, unroll=count // z.col // 2)
    for low, full, size in groups:
        weighted_s[low : low + size, :] = weighted_ref[full : full + size, :]
    gain_sum = jnp.zeros((SUB, z.channels), F32)
    for low, full, size in groups:
        for c in range(size // chunk):
            at = slice(low + c * chunk, low + (c + 1) * chunk)
            place = slice(full + c * chunk, full + (c + 1) * chunk)
            part = 256
            for f in range(z.wide // part):
                cut = slice(f * part, (f + 1) * part)
                pre = dot(normed_s[at, :], we_ref[:, cut])
                back = dot_nt(weighted_s[at, :], wc_ref[cut, :])
                phi, density = gelu_parts(pre)
                hidden_s[at, cut] = (pre * phi).astype(BF16)
                slope_s[at, cut] = (back * (phi + density)).astype(BF16)
            branch = dot(hidden_s[at, :], wc_ref[...])
            section_ref[at, :] = (coarse_ref[place, :].astype(F32) + branch).astype(BF16)
            back = dot_nt(slope_s[at, :], we_ref[...])
            unit = unit_s[at, :]
            gain_sum = gain_sum + jnp.sum((back * unit).reshape(-1, SUB, z.channels), axis=0)
            back = back * gain_ref[...]
            inverse = jnp.concatenate([inv_s[at, :]] * z.halves, axis=1)
            mixed_ref[at, :] = inverse * (back - row_mean(z, back) - unit * row_mean(z, back * unit))
    return gain_sum


def inner_kernel(
    z, pad_ref, kern_ref, gain_ref, we_ref, wc_ref, coarse_ref, weighted_ref,
    section_ref, mixed_ref, expand_ref, contract_ref, gain_sum_ref, taps_s, *scratch,
):
    spread_taps(z, kern_ref, taps_s)
    size = (z.cols - 2 * M) * z.col
    refs = (gain_ref, we_ref, wc_ref, coarse_ref, weighted_ref)
    gain_sum_ref[...] = section(
        z, pad_ref, lambda j: j, [(0, M * z.col, size)], refs, scratch, size, section_ref, mixed_ref, taps_s
    )
    unit_s, inv_s, normed_s, hidden_s, slope_s, weighted_s = scratch
    expand_ref[...] = dot_tn(normed_s[...], slope_s[...])
    contract_ref[...] = dot_tn(weighted_s[...], hidden_s[...])


def outer_kernel(
    z, pad_ref, left_ref, right_ref, kern_ref, gain_ref, we_ref, wc_ref, coarse_ref, weighted_ref,
    expand_ref, contract_ref, gain_sum_ref, inner_mixed_ref,
    section_ref, mixed_ref, mine_ref, other_ref, low_ref, gain_out_ref, left_out_ref, right_out_ref, *rest,
):
    *edge_refs, taps_s, edge_s, split_s, slab_s = rest[:-6]
    scratch = rest[-6:]
    spread_taps(z, kern_ref, taps_s)
    edge_columns(z, left_ref, pad_ref, right_ref, edge_s, slab_s)
    left_out_ref[...] = edge_s[0 : M * z.pad_col, :]
    right_out_ref[...] = edge_s[5 * M * z.pad_col :, :]
    size = M * z.col
    refs = (gain_ref, we_ref, wc_ref, coarse_ref, weighted_ref)
    groups = [(0, 0, size), (size, z.cells - size, size)]
    gain_sum = section(
        z, edge_s, lambda j: jnp.where(j < M, j, j + 2 * M), groups, refs, scratch, size, section_ref, mixed_ref, taps_s
    )
    unit_s, inv_s, normed_s, hidden_s, slope_s, weighted_s = scratch
    gain_out_ref[...] = gain_sum + gain_sum_ref[...]
    half, cut = z.channels // 2, z.wide // 2
    first = lax.axis_index("dp") == 0
    total = (expand_ref[...] + dot_tn(normed_s[...], slope_s[...])).astype(BF16)
    mine_ref[0:half, :] = jnp.where(first, total[:half], total[half:])
    other_ref[0:half, :] = jnp.where(first, total[half:], total[:half])
    total = (contract_ref[...] + dot_tn(weighted_s[...], hidden_s[...])).astype(BF16)
    for t in range(2):
        low, high = total[t * half : (t + 1) * half, :cut], total[t * half : (t + 1) * half, cut:]
        mine_ref[half:, t * cut : (t + 1) * cut] = jnp.where(first, low, high)
        other_ref[half:, t * cut : (t + 1) * cut] = jnp.where(first, high, low)
    low_ref[0:size, :] = mixed_ref[0:size, :].astype(BF16)
    low_ref[size : z.cells - size, :] = inner_mixed_ref[...].astype(BF16)
    low_ref[z.cells - size :, :] = mixed_ref[size:, :].astype(BF16)
    for h in range(z.halves):
        split_s[h, :, :] = low_ref[:, h * LANE : (h + 1) * LANE].astype(F32)
    edge_rows(z, split_s, edge_refs)


def terms_kernel(z, h, pad_ref, left_ref, right_ref, inner_ref, outer_ref, gain_ref, out_ref, full_s, mixed_s):
    edge, size = M * z.pad_col, M * z.col
    lanes = slice(h * LANE, (h + 1) * LANE)
    full_s[0:edge, :] = left_ref[:, lanes]
    full_s[edge : edge + z.cols * z.pad_col, :] = pad_ref[:, lanes]
    full_s[edge + z.cols * z.pad_col :, :] = right_ref[:, lanes]
    mixed_s[0:size, :] = outer_ref[0:size, lanes]
    mixed_s[size : z.cells - size, :] = inner_ref[:, lanes]
    mixed_s[z.cells - size :, :] = outer_ref[size:, lanes]
    out_ref[...] = jnp.zeros_like(out_ref)
    for e in range(KS):

        def step(j, sums):
            column = full_s[rows((j + e) * z.pad_col, z.pad_col), :].reshape(z.pad_rows, SUB, LANE)
            back = mixed_s[rows(j * z.col, z.col), :].reshape(z.block_rows, SUB, LANE)
            return tuple(sums[a] + jnp.sum(column[a : a + z.block_rows] * back, axis=0) for a in range(KS))

        zeros = tuple(jnp.zeros((SUB, LANE), F32) for _ in range(KS))
        sums = lax.fori_loop(0, z.cols, step, zeros, unroll=4)
        for a in range(KS):
            t = a * KS + e
            out_ref[t : t + 1, :] = jnp.sum(sums[a], axis=0, keepdims=True)
    out_ref[KS * KS : KS * KS + 1, :] = jnp.sum(gain_ref[:, lanes], axis=0, keepdims=True)


def spread(z, pad, taps_s, source, at, low, weighted_ref, out_ref):
    for h in range(z.halves):
        lanes = slice(h * LANE, (h + 1) * LANE)
        total = taps(z, pad, taps_s, source, h, True)
        out_ref[low, lanes] = (weighted_ref[at, lanes].astype(F32) + total).astype(BF16)


def back_inner_kernel(z, pad_ref, kern_ref, weighted_ref, coarse_ref, taps_s):
    spread_taps(z, kern_ref, taps_s)

    def step(j, _):
        spread(
            z, pad_ref, taps_s, j, rows16((j + M) * z.col, z.col), rows16(j * z.col, z.col), weighted_ref, coarse_ref
        )
        return 0

    lax.fori_loop(0, z.cols - 2 * M, step, 0, unroll=5)


def edge_columns(z, left_ref, pad_ref, right_ref, edge_s, slab_s):
    edge, near = M * z.pad_col, 2 * M * z.pad_col
    even = lax.axis_index("lon") % 2 == 0
    one, two = left_ref[...], right_ref[...]
    unpack_slab(z, jnp.where(even, two, one), slab_s, edge_s, 0)
    edge_s[edge : edge + near, :] = pad_ref[0:near, :]
    edge_s[edge + near : edge + 2 * near, :] = pad_ref[z.cols * z.pad_col - near :, :]
    unpack_slab(z, jnp.where(even, one, two), slab_s, edge_s, edge + 2 * near)


def back_outer_kernel(
    z, pad_ref, left_ref, right_ref, kern_ref, weighted_ref, patches_ref, inner_ref, low_aux_ref, high_aux_ref,
    coarse_ref, mine_ref, other_ref, taps_s, edge_s, sum_s, slab_s,
):
    spread_taps(z, kern_ref, taps_s)
    edge_columns(z, left_ref, pad_ref, right_ref, edge_s, slab_s)

    def step(j, _):
        for first, source in ((0, 0), (z.cols - M, 3 * M)):
            at = rows16((first + j) * z.col, z.col)
            spread(z, edge_s, taps_s, source + j, at, at, weighted_ref, coarse_ref)
        return 0

    lax.fori_loop(0, M, step, 0, unroll=True)
    size = M * z.col
    coarse_ref[size : z.cells - size, :] = inner_ref[...]
    sum_s[...] = dot_tn(coarse_ref[...], patches_ref[...])
    own, cut = lax.axis_index("dp"), 2 * z.narrow
    depth, half = low_aux_ref.shape[0] // 2, z.channels // 2
    for ref, owner in ((mine_ref, own), (other_ref, 1 - own)):
        ref[0 : z.channels, :] = sum_s[:, lanes_at(owner * cut, cut)].astype(BF16)
        for t in range(2):
            at = slice(t * depth, (t + 1) * depth)
            aux = jnp.where(owner == 0, low_aux_ref[at, :], high_aux_ref[at, :])
            ref[z.channels :, t * half : (t + 1) * half] = aux.astype(BF16)


def unfold_kernel(z, coarse_ref, centered_ref, patches_ref, back_ref):
    group = 4
    ones = jnp.full((z.narrow, z.narrow), 1.0 / z.narrow, BF16)

    def step(g, _):
        at = rows16(g * group * z.col, group * z.col)
        low = coarse_ref[at, :]
        back = dot_nt(jnp.concatenate([low, low], axis=1), centered_ref[...])
        for p in range(2):
            for q in range(2):
                lanes = slice((p * 2 + q) * z.narrow, (p * 2 + q + 1) * z.narrow)
                unit = patches_ref[at, lanes].astype(F32)
                up = back[:, lanes]
                up = up - unit * dot((up * unit).astype(BF16), ones)
                for jj in range(group):
                    for i in range(z.block_rows):
                        first = jj * z.col + i * SUB
                        back_ref[fine_rows_of(z, g * group + jj, i, p, q), :] = up[first : first + SUB]
        return 0

    lax.fori_loop(0, z.cols // group, step, 0, unroll=True)


def fine_kernel(z, back_ref, inv_ref, out_ref):
    def step(t, _):
        at = rows16(t * z.fine_block, z.fine_block)
        out_ref[at, :] = (inv_ref[at, :] * back_ref[rows(t * z.fine_stride, z.fine_block), :]).astype(BF16)
        return 0

    lax.fori_loop(0, SUB, step, 0, unroll=2)


def second(axis, distance):
    return lax.axis_index(axis) // distance % 2


def add_kernel(step, mine_ref, got_ref, *out_refs):
    if step is None:
        out_refs[0][...] = (mine_ref[...].astype(F32) + got_ref[...].astype(F32)).astype(BF16)
        return
    half, side = mine_ref.shape[0] // 2, second(*step)
    for ref, which in zip(out_refs, (side, 1 - side)):
        at = rows16(which * half, half)
        ref[...] = (mine_ref[at, :].astype(F32) + got_ref[at, :].astype(F32)).astype(BF16)


def join_kernel(step, mine_ref, got_ref, out_ref):
    half, side = mine_ref.shape[0], second(*step)
    out_ref[rows16(side * half, half), :] = mine_ref[...]
    out_ref[rows16((1 - side) * half, half), :] = got_ref[...]


def section_kernel(z, inner_ref, outer_ref, out_ref, all_s, split_s):
    size = M * z.col
    all_s[0:size, :] = outer_ref[0:size, :].astype(F32)
    all_s[size : z.cells - size, :] = inner_ref[...].astype(F32)
    all_s[z.cells - size :, :] = outer_ref[size:, :].astype(F32)

    def step(j, _):
        for h in range(z.halves):
            for i in range(z.block_rows):
                split_s[h, pl.ds(i * z.cols + j, SUB, stride=z.block_rows * z.cols), :] = all_s[
                    rows(j * z.col + i * SUB, SUB), h * LANE : (h + 1) * LANE
                ]
        return 0

    lax.fori_loop(0, z.cols, step, 0, unroll=8)
    for h in range(z.halves):
        out_ref[:, h * LANE : (h + 1) * LANE] = split_s[h, :, :].astype(BF16)


def final_wide_kernel(z, factor, step, mine_ref, got_ref, expand_ref, contract_ref, sum_ref):
    join_kernel(step, mine_ref, got_ref, sum_ref)
    half, cut = z.channels // 2, z.wide // 2
    expand_ref[...] = sum_ref[0:half, :].astype(F32) * factor
    for t in range(2):
        part = sum_ref[half:, t * cut : (t + 1) * cut].astype(F32) * factor
        contract_ref[:, t * half : (t + 1) * half] = part.T


def final_small_kernel(z, factor, mine_ref, got_ref, merge_ref, kernel_ref, gain_ref):
    total = (mine_ref[...].astype(F32) + got_ref[...].astype(F32)) * factor
    merge_ref[...] = total[0 : z.channels].T
    half = z.channels // 2
    tail = total[z.channels :]
    depth = tail.shape[0]
    kernel_ref[0:depth, :] = tail[:, :half]
    kernel_ref[depth:, :] = tail[: KS * KS - depth, half:]
    gain_ref[...] = tail[KS * KS - depth : KS * KS - depth + 1, half:]


def swap(x, axis, distance):
    size = lax.axis_size(axis)
    return lax.ppermute(x, axis, [(i, i ^ distance) for i in range(size)])


def add(mine, got, after=(), halve=None):
    count, width = mine.shape
    outs = [((count, width), BF16)] if halve is None else [((count // 2, width), BF16)] * 2
    return kernel_call(functools.partial(add_kernel, halve), outs, (mine, got), after=after)


def join(x, step, after):
    outs = [((2 * x.shape[0], x.shape[1]), BF16)]
    return kernel_call(functools.partial(join_kernel, step), outs, (x, swap(x, *step)), after=after)


def sum_steps(count):
    steps = []
    for axis in ("lat", "lon"):
        distance = 1
        while distance < lax.axis_size(axis):
            steps.append((axis, distance))
            distance *= 2
    halvings = 0
    while halvings < len(steps) - 1 and count >> (halvings + 1) >= 2 * SUB:
        halvings += 1
    return steps, halvings


def lat_margins(last, first=None):
    if first is None:
        got = swap(last, "lat", 1)
        return got, got
    up = [(i, i + 1) for i in range(lax.axis_size("lat") - 1)]
    return lax.ppermute(last, "lat", up), lax.ppermute(first, "lat", [(j, i) for i, j in up])


def lon_margins(one, two):
    size = lax.axis_size("lon")
    pairs = [(i, i ^ 1) for i in range(size)]
    return lax.ppermute(one, "lon", pairs), lax.ppermute(two, "lon", [((i + 1) % size, (j + 1) % size) for i, j in pairs])


def body(fine_field, grad_out, conv_kernel, norm_gain, w_expand, w_contract, w_merge):
    z = Sizes(fine_field, w_merge, w_expand)
    ch, ff, lats = z.channels, z.wide, lax.axis_size("lat")
    fine = fine_field.reshape(z.fine, z.narrow)
    gain = norm_gain.reshape(1, ch)

    part = functools.partial
    split = ((z.halves, z.cells, LANE), F32)
    edges = [((z.samples * M * z.cols, ch), BF16)] * (1 if lats == 2 else 2)
    patches, coarse, fine_inv, *send, _ = kernel_call(
        part(merge_kernel, z),
        [((z.cells, 4 * z.narrow), BF16), ((z.cells, ch), BF16), ((z.fine, z.narrow), F32), *edges],
        (fine, w_merge),
        [((SUB * z.fine_stride, z.narrow), F32), split],
    )
    before, after = lat_margins(*send)
    weighted, w_centered, _ = kernel_call(
        part(weighted_kernel, z, lats),
        [((z.cells, ch), BF16), ((4 * z.narrow, 2 * ch), BF16)],
        (grad_out.reshape(z.cells, ch), w_merge),
        [split],
        flops=2_000_000_000,
    )
    slab_rows = -(-(M * z.col + 2 * M * z.samples * M) // (2 * SUB)) * 2 * SUB
    slab, slab_s = ((slab_rows, ch), BF16), ((slab_rows, ch), F32)
    padded = ((z.cols * z.pad_col, ch), F32)
    pad_scratch = [((2 * z.samples * M * z.cols, ch), F32), slab_s]
    pad, left, right, _ = kernel_call(part(pad_kernel, z, lats), [padded, slab, slab], (coarse, before, after), pad_scratch)
    left, right = lon_margins(left, right)

    taps_s = ((KS * KS * SUB, ch), F32)

    def section_scratch(count):
        return [
            ((count, ch), F32),
            ((count, LANE), F32),
            ((count, ch), BF16),
            ((count, ff), BF16),
            ((count, ff), BF16),
            ((count, ch), BF16),
        ]

    outer = 2 * M * z.col
    inner = z.cells - outer
    section_in, mixed_in, expand, contract, gain_sum, _ = kernel_call(
        part(inner_kernel, z),
        [((inner, ch), BF16), ((inner, ch), F32), ((ch, ff), F32), ((ch, ff), F32), ((SUB, ch), F32)],
        (pad, conv_kernel, gain, w_expand, w_contract, coarse, weighted),
        [taps_s] + section_scratch(inner),
        flops=8_000_000_000,
    )
    section_out, mixed_out, mine, other, low, gain_sum, left, right, *send, _ = kernel_call(
        part(outer_kernel, z),
        [
            ((outer, ch), BF16),
            ((outer, ch), F32),
            ((ch, ff), BF16),
            ((ch, ff), BF16),
            ((z.cells, ch), BF16),
            ((SUB, ch), F32),
            ((M * z.pad_col, ch), F32),
            ((M * z.pad_col, ch), F32),
            *edges,
        ],
        (pad, left, right, conv_kernel, gain, w_expand, w_contract, coarse, weighted)
        + (expand, contract, gain_sum, mixed_in),
        [taps_s, ((6 * M * z.pad_col, ch), F32), split, slab_s] + section_scratch(outer),
        flops=8_000_000_000,
    )
    before, after = lat_margins(*send)
    steps, halvings = sum_steps(ch)
    wide, away, token = add(mine, swap(other, "dp", 1), halve=steps[0])
    pad_low, edge_left, edge_right, token = kernel_call(
        part(pad_kernel, z, lats), [padded, slab, slab], (low, before, after), pad_scratch, after=(token,)
    )
    left_low, right_low = lon_margins(edge_left, edge_right)
    bf = lambda count, width: ((count, width), BF16)

    def terms(h, token):
        return kernel_call(
            part(terms_kernel, z, h),
            [((64, LANE), F32)],
            (pad, left, right, mixed_in, mixed_out, gain_sum),
            [(((z.cols + 2 * M) * z.pad_col, LANE), F32), ((z.cells, LANE), F32)],
            3_000_000_000,
            (token,),
        )

    low_aux, token = terms(0, token)
    wide, away, token = add(wide, swap(away, *steps[0]), after=(token,), halve=steps[1])
    high_aux, token = terms(1, token)
    back_inner, token = kernel_call(
        part(back_inner_kernel, z), [bf(inner, ch)], (pad_low, conv_kernel, weighted), [taps_s], 500_000_000, (token,)
    )
    for n in range(1, halvings - 1):
        wide, away, token = add(wide, swap(away, *steps[n]), after=(token,), halve=steps[n + 1])
    wide, token = add(wide, swap(away, *steps[halvings - 1]), after=(token,))
    back_coarse, mine, other, token = kernel_call(
        part(back_outer_kernel, z),
        [bf(z.cells, ch), bf(ch + 32, 2 * z.narrow), bf(ch + 32, 2 * z.narrow)],
        (pad_low, left_low, right_low, conv_kernel, weighted, patches, back_inner, low_aux, high_aux),
        [taps_s, ((6 * M * z.pad_col, ch), F32), ((ch, 4 * z.narrow), F32), slab_s],
        4_000_000_000,
        (token,),
    )
    back_fine, token = kernel_call(
        part(unfold_kernel, z),
        [((SUB * z.fine_stride, z.narrow), F32)],
        (back_coarse, w_centered, patches),
        (),
        3_000_000_000,
        (token,),
    )
    small, token = add(mine, swap(other, "dp", 1), after=(token,))
    grad_fine, token = kernel_call(
        part(fine_kernel, z), [bf(z.fine, z.narrow)], (back_fine, fine_inv), (), 2_000_000_000, (token,)
    )
    for step in steps[halvings:]:
        wide, token = add(wide, swap(wide, *step), after=(token,))
    small, token = add(small, swap(small, *steps[0]), after=(token,))
    section_all, token = kernel_call(
        part(section_kernel, z),
        [bf(z.cells, ch)],
        (section_in, section_out),
        [((z.cells, ch), F32), split],
        2_000_000_000,
        (token,),
    )
    for step in reversed(steps[1:halvings]):
        wide, token = join(wide, step, (token,))
    for step in steps[1:-1]:
        small, token = add(small, swap(small, *step), after=(token,))
    small_got = swap(small, *steps[-1])
    all_cells = z.samples * lax.axis_size("dp") * z.lat_rows * lats * z.cols * lax.axis_size("lon")
    factor = 1.0 / math.sqrt(all_cells)
    grad_expand, grad_contract, token = kernel_call(
        part(final_wide_kernel, z, factor, steps[0]),
        [((ch // 2, ff), F32), ((ff // 2, ch), F32)],
        (wide, swap(wide, *steps[0])),
        [((ch, ff), BF16)],
        after=(token,),
    )
    grad_merge, grad_kernel, grad_gain, _ = kernel_call(
        part(final_small_kernel, z, factor),
        [((2 * z.narrow, ch), F32), ((KS * KS, ch // 2), F32), ((1, ch // 2), F32)],
        (small, small_got),
        after=(token,),
    )
    return (
        section_all.reshape(z.samples, z.lat_rows, z.cols, ch),
        grad_fine.reshape(fine_field.shape),
        grad_kernel,
        grad_gain.reshape(ch // 2),
        grad_expand,
        grad_contract,
        grad_merge,
    )


def solution(mesh):
    field = P(("groups", "dp"), "lat", "lon", None)
    owned = P(("groups", "dp"), None)
    return jax.shard_map(
        body,
        mesh=mesh,
        in_specs=(field, field, P(), P(), P(), P(), P()),
        out_specs=(field, field, P("groups", "dp"), P(("groups", "dp")), owned, owned, owned),
        check_vma=False,
    )
```
